32 devices in a mesh: pipe: 2 (over x), dp: 4 (over y, core), inner: 4 (over z).
Axes of the slice: x: 2, y: 2, z: 4, core: 2. Of those that a mesh axis runs over, the one named last changes fastest.
Arguments:
- pixels: bfloat16 [16, 48, 16, 256], P('dp', 'inner'), may hold values from -6 to 6
- date_days: int32 [16, 16], P('dp'), may hold values from 0 to 364
- clear_count: int32 [16], P('dp'), may hold values from 3 to 16, as said below
- batch_slot: int32 [16], P('dp'), may hold values from 0 to 3, as said below
- labels: int32 [16, 48], P('dp'), may hold values from 0 to 15
- class_tokens: bfloat16 [16, 256], replicated, may hold values from -6 to 6
- section_gain: float32 [2, 256], P('pipe'), may hold values from 0.5 to 2
- segment_probe_lookup_content: bfloat16 [2, 256, 768], P('pipe'), may hold values from -0.375 to 0.375
- section_out: bfloat16 [2, 256, 256], P('pipe'), may hold values from -0.375 to 0.375
- head_vec: float32 [256], replicated, may hold values from -1 to 1
Outputs:
- batch_loss: float32 [4], replicated
- class_grad: float32 [16, 256], replicated
- section_gain_grad: float32 [2, 256], P('pipe')
- section_qkv_grad: float32 [2, 256, 768], P('pipe')
- section_out_grad: float32 [2, 256, 256], P('pipe')
- readout_derivative: float32 [256], replicated
The draws below stay inside these ranges and needn't reach their ends.
Inputs may be any that keep to these rules, and one draw needn't show every extreme that they name: The clear dates of tile b are its dates 0 to clear_count[b] - 1. Some tile has all 16 dates clear and some tile has the fewest. `batch_slot`: within each aligned block of 4 tiles (the tiles of one index of dp) every micro-batch number appears exactly once.
All inputs are finite; a program needn't handle non-finite values.
Results may differ from the reference program's by a relative error of at most 0.0015.
The reference program's roundings to bfloat16 on the way count: a program that leaves them out, or rounds other values in their place, can miss the bound.
Values may be sent and summed in bfloat16 or wider, within the bound.
A program may use at most 64 MiB of HBM per device.

```python
import math
import jax
import jax.numpy as jnp
from jax import lax

D = 256
HEADS = 8
CLASSES = 16
PATCHES = 48
DATES = 16
MICRO = 4
TILE_DEV = 4
TILES = 16


def draw_clear_count(key, part):
    lowest = DATES // 6 + 1
    counts = jax.random.randint(jax.random.fold_in(key, 11), (TILES,), lowest, DATES + 1)
    places = jax.random.permutation(jax.random.fold_in(key, 12), TILES)
    counts = counts.at[places[0]].set(DATES)
    counts = counts.at[places[1]].set(lowest)
    return counts.astype(jnp.int32)


def draw_batch_slot(key, part):
    blocks = TILES // TILE_DEV
    pattern = jnp.arange(TILE_DEV, dtype=jnp.int32) % MICRO
    block_keys = jax.random.split(jax.random.fold_in(key, 21), blocks)
    shuffled = jax.vmap(lambda block_key: jax.random.permutation(block_key, pattern))(block_keys)
    return shuffled.reshape(TILES).astype(jnp.int32)


def with_ends(array, key, smallest, largest):
    longest = array.shape.index(max(array.shape))
    spots = []
    for shift in (0, 1):
        where = [jax.random.randint(jax.random.fold_in(key, axis), (), 0, length) for axis, length in enumerate(array.shape)]
        where[longest] = (where[longest] + shift) % array.shape[longest]
        spots.append(tuple(where))
    return array.at[spots[0]].set(smallest).at[spots[1]].set(largest)


def block_levels(stream_key, extent, pieces, smallest, top_value):
    gain = 1.0
    for axis_at, parts in pieces:
        heights = jax.random.uniform(jax.random.fold_in(jax.random.fold_in(stream_key, 6), axis_at), (parts,), jnp.float32, smallest / len(pieces), top_value / len(pieces))
        gain = gain * jnp.repeat(jnp.exp(heights), extent[axis_at] // parts).reshape((-1,) + (1,) * (len(extent) - 1 - axis_at))
    return gain


def noise(own_key, dims, width, most, cuts=(), kind=jnp.bfloat16):
    values = width * jax.random.normal(own_key, dims, jnp.float32)
    if cuts:
        values = values * block_levels(own_key, dims, cuts, -0.22, 0.18)
    return jnp.clip(values, -most, most).astype(kind)


def setup_inputs(seed: int = 0) -> dict:
    streams_of = jax.random.split(jax.random.key(seed), 11)
    return {
        "pixels": noise(streams_of[0], (TILES, PATCHES, DATES, D), 1.0, 6.0, ((0, 4), (1, 4))),
        "date_days": with_ends(jax.random.randint(streams_of[1], (TILES, DATES), 0, 365), jax.random.fold_in(streams_of[1], 1), 0, 364).astype(jnp.int32),
        "clear_count": draw_clear_count(jax.random.fold_in(streams_of[10], 71), 0),
        "batch_slot": draw_batch_slot(jax.random.fold_in(streams_of[10], 71), 0),
        "labels": with_ends(jax.random.randint(streams_of[4], (TILES, PATCHES), 0, CLASSES), jax.random.fold_in(streams_of[4], 1), 0, CLASSES - 1).astype(jnp.int32),
        "class_tokens": noise(streams_of[5], (CLASSES, D), 1.0, 6.0),
        "section_gain": jnp.clip(jnp.exp(math.log(2.0) - 1.3862944 * jax.random.uniform(streams_of[6], (2, D), jnp.float32) ** block_levels(streams_of[6], (2, D), ((0, 2),), -0.2, 0.2)), 0.5, 2.0),
        "segment_probe_lookup_content": noise(streams_of[7], (2, D, 3 * D), D ** -0.5, 0.375, ((0, 2),)),
        "section_out": noise(streams_of[8], (2, D, D), D ** -0.5, 0.375, ((0, 2),)),
        "head_vec": noise(streams_of[9], (D,), (D // 9) ** -0.5, 1.0, (), jnp.float32),
    }


normalizer_sharpness = 10.0
logit_cap = 15.0
norm_eps = 1e-05
head_eps = 1e-06

def matmul_f32(left_side, right_side):
    return jnp.einsum('...d,de->...e', left_side.astype(jnp.float32), right_side.astype(jnp.float32), precision=lax.Precision.HIGHEST)

def rms_norm(inputs, gain_vec):
    inverse_rms = lax.rsqrt(lax.optimization_barrier(jnp.mean(inputs * inputs, axis=-1, keepdims=True)) + norm_eps)
    return inputs * inverse_rms * gain_vec

def unit_heads(values):
    shaped = values.reshape(values.shape[:-1] + (HEADS, values.shape[-1] // HEADS))
    return shaped * lax.rsqrt(lax.optimization_barrier(jnp.sum(shaped * shaped, axis=-1, keepdims=True)) + head_eps)

def temporal(pixel_rows, date_days, counts, params):
    class_init, gain_vec, w_qkv, w_out = params
    batch_count, patches, dates_max, model_width = pixel_rows.shape
    classes = class_init.shape[0]
    band_channel = jnp.arange(model_width)
    frequency = jnp.exp((band_channel // 2 * 2).astype(jnp.float32) * (-math.log(10000.0) / model_width))
    phases = date_days.astype(jnp.float32)[:, :, None] * frequency
    encoding = jnp.where(band_channel % 2 == 0, jnp.sin(phases), jnp.cos(phases))
    date_rows = pixel_rows.astype(jnp.float32) + encoding[:, None]
    class_rows = jnp.broadcast_to(class_init, (batch_count, patches, classes, model_width))
    sequence = jnp.concatenate([class_rows, date_rows], axis=2)
    normed = rms_norm(sequence, gain_vec).astype(jnp.bfloat16)
    probe_entry_lines = unit_heads(matmul_f32(normed[:, :, :classes], w_qkv[:, :model_width]))
    lookup_entry_lines = unit_heads(matmul_f32(normed, w_qkv[:, model_width:2 * model_width]))
    value_rows = matmul_f32(normed, w_qkv[:, 2 * model_width:]).astype(jnp.bfloat16)
    value_heads = value_rows.reshape(batch_count, patches, classes + dates_max, HEADS, model_width // HEADS)
    affinity_logit_grid = normalizer_sharpness * jnp.einsum('ohbyv,ohsyv->ohybs', probe_entry_lines, lookup_entry_lines, precision=lax.Precision.HIGHEST)
    position = jnp.arange(classes + dates_max)
    key_mask = ((position[None, :] < classes) | (position[None, :] - classes < counts[:, None])).astype(jnp.float32)
    raised = jnp.exp(affinity_logit_grid) * key_mask[:, None, None, None, :]
    weights = (raised / lax.optimization_barrier(jnp.sum(raised, axis=-1, keepdims=True))).astype(jnp.bfloat16)
    attended = jnp.einsum('bphqk,bpkhe->bpqhe', weights.astype(jnp.float32), value_heads.astype(jnp.float32), precision=lax.Precision.HIGHEST)
    attended = attended.reshape(batch_count, patches, classes, model_width).astype(jnp.bfloat16)
    updated = sequence[:, :, :classes] + matmul_f32(attended, w_out)
    return jnp.swapaxes(updated, 1, 2).astype(jnp.bfloat16)

def spatial(inputs, params):
    gain_vec, w_qkv, w_out, head_vec = params
    batch_count, groups, classes, patches, model_width = inputs.shape
    class_seq = jnp.swapaxes(inputs, 1, 2).reshape(batch_count, classes, groups * patches, model_width).astype(jnp.float32)
    normed = rms_norm(class_seq, gain_vec).astype(jnp.bfloat16)
    probe_entry_lines = unit_heads(matmul_f32(normed, w_qkv[:, :model_width]))
    lookup_entry_lines = unit_heads(matmul_f32(normed, w_qkv[:, model_width:2 * model_width]))
    value_rows = matmul_f32(normed, w_qkv[:, 2 * model_width:]).astype(jnp.bfloat16)
    value_heads = value_rows.reshape(batch_count, classes, groups * patches, HEADS, model_width // HEADS)
    affinity_logit_grid = normalizer_sharpness * jnp.einsum('wisbx,wiqbx->wibsq', probe_entry_lines, lookup_entry_lines, precision=lax.Precision.HIGHEST)
    raised = jnp.exp(affinity_logit_grid)
    weights = (raised / lax.optimization_barrier(jnp.sum(raised, axis=-1, keepdims=True))).astype(jnp.bfloat16)
    attended = jnp.einsum('bchqk,bckhe->bcqhe', weights.astype(jnp.float32), value_heads.astype(jnp.float32), precision=lax.Precision.HIGHEST)
    attended = attended.reshape(batch_count, classes, groups * patches, model_width).astype(jnp.bfloat16)
    hidden = class_seq + matmul_f32(attended, w_out)
    raw_logits = jnp.einsum('bcpd,d->bcp', hidden, head_vec, precision=lax.Precision.HIGHEST)
    logits = logit_cap * jnp.tanh(raw_logits / logit_cap)
    return logits.reshape(batch_count, classes, groups, patches)

def reference(pixels, date_days, clear_count, batch_slot, labels, class_tokens, section_gain, segment_probe_lookup_content, section_out, head_vec):
    first_params = (class_tokens.astype(jnp.float32), section_gain[0], segment_probe_lookup_content[0].astype(jnp.float32), section_out[0].astype(jnp.float32))
    second_params = (section_gain[1], segment_probe_lookup_content[1].astype(jnp.float32), section_out[1].astype(jnp.float32), head_vec)
    tile_count = pixels.shape[0]
    model_width = pixels.shape[3]
    class_ids = jnp.arange(CLASSES)

    def one_tile(totals, tile_args):
        pixel_rows, day_rows, count_one, label_row = tile_args
        encoded, pull_first = jax.vjp(lambda params: temporal(pixel_rows[None], day_rows[None], count_one[None], params), first_params)
        inputs = encoded.reshape(1, 1, CLASSES, PATCHES, model_width)
        logits, pull_second = jax.vjp(spatial, inputs, second_params)
        exp_logits = jnp.exp(logits)
        class_total = lax.optimization_barrier(jnp.sum(exp_logits, axis=1))
        indicator_rows = (label_row.reshape(1, 1, 1, PATCHES) == class_ids[None, :, None, None]).astype(jnp.float32)
        dlogit = (exp_logits / class_total[:, None] - indicator_rows) / tile_count
        grad_in, grads_second = pull_second(dlogit)
        first_gradients, = pull_first(grad_in.reshape(encoded.shape))
        tile_loss = jnp.sum(indicator_rows * (jnp.log(class_total)[:, None] - logits))
        new_totals = (totals[0] + first_gradients[0], totals[1] + first_gradients[1], totals[2] + first_gradients[2], totals[3] + first_gradients[3], totals[4] + grads_second[0], totals[5] + grads_second[1], totals[6] + grads_second[2], totals[7] + grads_second[3])
        return (new_totals, tile_loss)
    initial = (jnp.zeros((CLASSES, model_width), jnp.float32), jnp.zeros((model_width,), jnp.float32), jnp.zeros((model_width, 3 * model_width), jnp.float32), jnp.zeros((model_width, model_width), jnp.float32), jnp.zeros((model_width,), jnp.float32), jnp.zeros((model_width, 3 * model_width), jnp.float32), jnp.zeros((model_width, model_width), jnp.float32), jnp.zeros((model_width,), jnp.float32))
    totals, tile_losses = lax.scan(one_tile, initial, (pixels, date_days, clear_count, labels))
    slot_onehot = (batch_slot[None, :] == jnp.arange(MICRO)[:, None]).astype(jnp.float32)
    batch_loss = lax.optimization_barrier(jnp.sum(slot_onehot * tile_losses[None, :], axis=1)) / (tile_count // MICRO * PATCHES)
    section_gain_grad = jnp.stack([totals[1], totals[4]])
    section_qkv_grad = jnp.stack([totals[2], totals[5]])
    section_out_grad = jnp.stack([totals[3], totals[6]])
    return (batch_loss, totals[0], section_gain_grad, section_qkv_grad, section_out_grad, totals[7])
```

```python
import functools
import math

import jax
import jax.numpy as jnp
from jax import lax
from jax.experimental import pallas as pl
from jax.experimental.pallas import tpu as pltpu
from jax.sharding import PartitionSpec as P

HEADS = 8
CLASSES = 16
PATCHES = 48
MICRO = 4


normalizer_sharpness = 10.0
logit_cap = 15.0
norm_eps = 1e-05
head_eps = 1e-06


def matmul_f32(left_side, right_side):
    return jnp.einsum(
        "...d,de->...e",
        left_side,
        right_side.astype(jnp.bfloat16),
        preferred_element_type=jnp.float32,
    )


def rms_norm(inputs, gain_vec):
    inverse_rms = lax.rsqrt(jnp.mean(inputs * inputs, axis=-1, keepdims=True) + norm_eps)
    return inputs * inverse_rms * gain_vec


def unit_heads(values):
    shaped = values.reshape(values.shape[:-1] + (HEADS, values.shape[-1] // HEADS))
    return shaped * lax.rsqrt(jnp.sum(shaped * shaped, axis=-1, keepdims=True) + head_eps)


def temporal(pixel_rows, date_days, counts, params):
    class_init, gain_vec, w_qkv, w_out = params
    batch_count, patches, dates_max, model_width = pixel_rows.shape
    classes = class_init.shape[0]
    band_channel = jnp.arange(model_width)
    frequency = jnp.exp(
        (band_channel // 2 * 2).astype(jnp.float32) * (-math.log(10000.0) / model_width)
    )
    phases = date_days.astype(jnp.float32)[:, :, None] * frequency
    encoding = jnp.where(band_channel % 2 == 0, jnp.sin(phases), jnp.cos(phases))
    date_rows = pixel_rows.astype(jnp.float32) + encoding[:, None]
    class_rows = jnp.broadcast_to(class_init, (batch_count, patches, classes, model_width))
    sequence = jnp.concatenate([class_rows, date_rows], axis=2)
    normed = rms_norm(sequence, gain_vec).astype(jnp.bfloat16)
    probe_entry_lines = unit_heads(matmul_f32(normed[:, :, :classes], w_qkv[:, :model_width]))
    lookup_entry_lines = unit_heads(matmul_f32(normed, w_qkv[:, model_width : 2 * model_width]))
    value_rows = matmul_f32(normed, w_qkv[:, 2 * model_width :]).astype(jnp.bfloat16)
    value_heads = value_rows.reshape(
        batch_count, patches, classes + dates_max, HEADS, model_width // HEADS
    )
    affinity_logit_grid = normalizer_sharpness * jnp.einsum(
        "ohbyv,ohsyv->ohybs", probe_entry_lines, lookup_entry_lines, precision=lax.Precision.HIGHEST
    )
    position = jnp.arange(classes + dates_max)
    key_mask = (
        (position[None, :] < classes) | (position[None, :] - classes < counts[:, None])
    ).astype(jnp.float32)
    raised = jnp.exp(affinity_logit_grid) * key_mask[:, None, None, None, :]
    weights = (raised / jnp.sum(raised, axis=-1, keepdims=True)).astype(jnp.bfloat16)
    attended = jnp.einsum(
        "bphqk,bpkhe->bpqhe", weights, value_heads, preferred_element_type=jnp.float32
    )
    attended = attended.reshape(batch_count, patches, classes, model_width).astype(jnp.bfloat16)
    updated = sequence[:, :, :classes] + matmul_f32(attended, w_out)
    return jnp.swapaxes(updated, 1, 2).astype(jnp.bfloat16)


def spatial(inputs, params):
    gain_vec, w_qkv, w_out, head_vec = params
    batch_count, groups, classes, patches, model_width = inputs.shape
    class_seq = (
        jnp.swapaxes(inputs, 1, 2)
        .reshape(batch_count, classes, groups * patches, model_width)
        .astype(jnp.float32)
    )
    normed = rms_norm(class_seq, gain_vec).astype(jnp.bfloat16)
    probe_entry_lines = unit_heads(matmul_f32(normed, w_qkv[:, :model_width]))
    lookup_entry_lines = unit_heads(matmul_f32(normed, w_qkv[:, model_width : 2 * model_width]))
    value_rows = matmul_f32(normed, w_qkv[:, 2 * model_width :]).astype(jnp.bfloat16)
    value_heads = value_rows.reshape(
        batch_count, classes, groups * patches, HEADS, model_width // HEADS
    )
    affinity_logit_grid = normalizer_sharpness * jnp.einsum(
        "wisbx,wiqbx->wibsq", probe_entry_lines, lookup_entry_lines, precision=lax.Precision.HIGHEST
    )
    raised = jnp.exp(affinity_logit_grid)
    weights = (raised / jnp.sum(raised, axis=-1, keepdims=True)).astype(jnp.bfloat16)
    attended = jnp.einsum(
        "bchqk,bckhe->bcqhe", weights, value_heads, preferred_element_type=jnp.float32
    )
    attended = attended.reshape(batch_count, classes, groups * patches, model_width).astype(
        jnp.bfloat16
    )
    hidden = class_seq + matmul_f32(attended, w_out)
    raw_logits = jnp.einsum("bcpd,d->bcp", hidden, head_vec, precision=lax.Precision.HIGHEST)
    logits = logit_cap * jnp.tanh(raw_logits / logit_cap)
    return logits.reshape(batch_count, classes, groups, patches)


def shards_general(
    pixels,
    date_days,
    clear_count,
    batch_slot,
    labels,
    class_tokens,
    section_gain,
    segment_probe_lookup_content,
    section_out,
    head_vec,
):
    tiles_dev = pixels.shape[0]
    patches_dev = pixels.shape[1]
    model_width = pixels.shape[3]
    inner_count = lax.axis_size("inner")
    classes_dev = CLASSES // inner_count
    total_tiles = tiles_dev * lax.axis_size("dp")
    my_group = lax.axis_index("inner")
    class_ids = my_group * classes_dev + jnp.arange(classes_dev, dtype=jnp.int32)
    batch_norm = 1.0 / (total_tiles // MICRO * PATCHES)
    gains, qkv_all, out_all = (
        lax.all_gather(section_gain, "pipe", axis=0, tiled=True),
        lax.all_gather(
            segment_probe_lookup_content.astype(jnp.float32), "pipe", axis=0, tiled=True
        ),
        lax.all_gather(section_out.astype(jnp.float32), "pipe", axis=0, tiled=True),
    )
    pipe_pos = lax.axis_index("pipe")
    half_tiles = tiles_dev // 2
    first_params = (class_tokens.astype(jnp.float32), gains[0], qkv_all[0], out_all[0])
    second_params = (gains[1], qkv_all[1], out_all[1], head_vec)
    fold_shape = (1, inner_count, classes_dev, patches_dev, model_width)
    first_gradients = jax.tree.map(jnp.zeros_like, first_params)
    grads_second = jax.tree.map(jnp.zeros_like, second_params)
    loss_vec = jnp.zeros((MICRO,), jnp.float32)
    for tile_step in range(half_tiles):
        start = pipe_pos * half_tiles + tile_step
        single_pixel = lax.dynamic_slice_in_dim(pixels, start, 1, 0)
        days_one = lax.dynamic_slice_in_dim(date_days, start, 1, 0)
        count_one = lax.dynamic_slice_in_dim(clear_count, start, 1, 0)
        label_one = lax.dynamic_slice_in_dim(labels, start, 1, 0)
        slot_one = lax.dynamic_slice_in_dim(batch_slot, start, 1, 0)
        encoded, pull_first = jax.vjp(
            lambda params: temporal(single_pixel, days_one, count_one, params), first_params
        )
        arrived = lax.all_to_all(
            encoded.reshape(fold_shape), "inner", split_axis=1, concat_axis=1, tiled=True
        )
        logits, pull_second = jax.vjp(spatial, arrived, second_params)
        exp_logits = jnp.exp(logits)
        class_total = lax.psum(jnp.sum(exp_logits, axis=1), "inner")
        label_rows = label_one.reshape(1, 1, inner_count, patches_dev)
        indicator_rows = (label_rows == class_ids[None, :, None, None]).astype(jnp.float32)
        dlogit = (exp_logits / class_total[:, None] - indicator_rows) / total_tiles
        grad_in, grad_two = pull_second(dlogit)
        returned = lax.all_to_all(grad_in, "inner", split_axis=1, concat_axis=1, tiled=True)
        (derivative_lone,) = pull_first(returned.reshape(encoded.shape))
        first_gradients = jax.tree.map(
            lambda total, extra: total + extra, first_gradients, derivative_lone
        )
        grads_second = jax.tree.map(lambda total, extra: total + extra, grads_second, grad_two)
        loss_term = jnp.sum(indicator_rows * (jnp.log(class_total)[:, None] - logits)) * batch_norm
        loss_vec = loss_vec + loss_term * (jnp.arange(MICRO) == slot_one[0]).astype(jnp.float32)
    stacked = (
        jnp.stack([first_gradients[1], grads_second[0]]),
        jnp.stack([first_gradients[2], grads_second[1]]),
        jnp.stack([first_gradients[3], grads_second[2]]),
        first_gradients[0],
        grads_second[3],
        loss_vec,
    )
    summed = lax.psum(
        (stacked[0], stacked[1], stacked[2], stacked[3], stacked[4], stacked[5]),
        ("pipe", "dp", "inner"),
    )
    gain_grad = lax.dynamic_slice_in_dim(summed[0], pipe_pos, 1, 0)
    qkv_grad = lax.dynamic_slice_in_dim(summed[1], pipe_pos, 1, 0)
    out_grad = lax.dynamic_slice_in_dim(summed[2], pipe_pos, 1, 0)
    return (summed[5], summed[3], gain_grad, qkv_grad, out_grad, summed[4])


F32 = jnp.float32
BF16 = jnp.bfloat16
VMEM_LIMIT = 56 * 2**20


def params(**kw):
    return pltpu.CompilerParams(vmem_limit_bytes=VMEM_LIMIT, **kw)


def vmem(count):
    return [pl.BlockSpec(memory_space=pltpu.VMEM)] * count


def mm(a, b, ca=1, cb=0):
    return lax.dot_general(a, b, (((ca,), (cb,)), ((), ())), preferred_element_type=F32)


def split(a):
    hi = a.astype(BF16)
    return hi, (a - hi.astype(F32)).astype(BF16)


def mm2(a, b, ca=1, cb=0):
    hi, lo = split(a)
    return mm(hi, b, ca, cb) + mm(lo, b, ca, cb)


def mm2r(a, b, ca=1, cb=0):
    hi, lo = split(b)
    return mm(a, hi, ca, cb) + mm(a, lo, ca, cb)


def mm3(a, b, ca=1, cb=0):
    ah, al = split(a)
    bh, bl = split(b)
    return mm(ah, bh, ca, cb) + (mm(ah, bl, ca, cb) + mm(al, bh, ca, cb))


def same_block(rows, cols, size):
    r = lax.broadcasted_iota(jnp.int32, (rows, cols), 0) // size
    c = lax.broadcasted_iota(jnp.int32, (rows, cols), 1) // size
    return (r == c).astype(F32)


def head_ones(width):
    return same_block(width, width, width // HEADS).astype(BF16)


def head_mask(width):
    h = lax.broadcasted_iota(jnp.int32, (HEADS, 1, width), 0)
    c = lax.broadcasted_iota(jnp.int32, (HEADS, 1, width), 2) // (width // HEADS)
    return (h == c).astype(F32)


def unit(x, ones):
    r = lax.rsqrt(mm2(x * x, ones) + head_eps)
    return x * r, r


def unit_back(dxn, xn, r, ones):
    return r * (dxn - xn * mm2(dxn * xn, ones))


def norm_scale(x):
    return lax.rsqrt(jnp.mean(x * x, axis=-1, keepdims=True) + norm_eps)


def rounded(x):
    return x.astype(BF16).astype(F32)


def expand_heads(x, hm):
    n, d = x.shape
    return (x[None] * hm).reshape(HEADS * n, d)


def fold_heads(x, hm):
    n = x.shape[0] // HEADS
    return jnp.sum(x.reshape(HEADS, n, x.shape[1]) * hm, axis=0)


def permutation(n, outer):
    inner = n // outer
    r = lax.broadcasted_iota(jnp.int32, (n, n), 0)
    c = lax.broadcasted_iota(jnp.int32, (n, n), 1)
    return (c == (r % inner) * outer + r // inner).astype(F32).astype(BF16)


def date_sequence(pix, enc):
    return (pix.astype(F32) + enc[:, None]).reshape(-1, pix.shape[-1])


def temporal_fwd(pix_ref, enc_ref, mask_ref, cls_ref, gain_ref, w_ref, wo_ref,
                 send_ref, nd_ref, kn_ref, rk_ref, v_ref, ad_ref, ac_ref, att_ref, cq_ref):
    d = pix_ref.shape[-1]
    dates = pix_ref.shape[2]
    classes = cls_ref.shape[0]
    gain = gain_ref[...]
    x = date_sequence(pix_ref[...], enc_ref[...])
    rows = x.shape[0]
    bps = rows // dates
    nd = (x * norm_scale(x) * gain).astype(BF16)
    nd_ref[...] = nd
    cls = cls_ref[...].astype(F32)
    nc = (cls * norm_scale(cls) * gain).astype(BF16)
    ones = head_ones(d)
    hm = head_mask(d)
    kv = mm(nd, w_ref[:, d:])
    qkvc = mm(nc, w_ref[...])
    kn, rk = unit(kv[:, :d], ones)
    kn_ref[...] = kn
    rk_ref[...] = rk
    v = kv[:, d:].astype(BF16)
    v_ref[...] = v
    qn, rq = unit(qkvc[:, :d], ones)
    kcn, rkc = unit(qkvc[:, d : 2 * d], ones)
    vc = qkvc[:, 2 * d :].astype(BF16)
    cq_ref[0] = qn
    cq_ref[1] = rq
    cq_ref[2] = kcn
    cq_ref[3] = rkc
    cq_ref[4] = vc.astype(F32)
    group = 128 // dates
    qe = expand_heads(qn, hm)
    kct = jnp.concatenate([kcn] * group, axis=0)
    ed = jnp.exp(normalizer_sharpness * mm3(qe, kn, 1, 1)) * mask_ref[...]
    ec = jnp.exp(normalizer_sharpness * mm3(qe, kct, 1, 1))
    seg = same_block(128, 128, dates).astype(BF16)
    sum_c = mm2(ec, seg)
    vct = jnp.concatenate([vc] * group, axis=0)
    bm = group_mask(group, dates)
    atts = []
    for g in range(bps // group):
        lanes = slice(g * 128, (g + 1) * 128)
        e = ed[:, lanes]
        den = mm2(e, seg) + sum_c
        ad = e / den
        ac = ec / den
        ad_ref[:, lanes] = ad
        ac_ref[:, lanes] = ac
        aexp = (jnp.concatenate([ad, ac], axis=1)[None] * bm).reshape(-1, 256).astype(BF16)
        vst = jnp.concatenate([v[lanes], vct], axis=0)
        o = mm(aexp, vst).reshape(group, HEADS, classes, d)
        atts.append(jnp.sum(o * hm[None], axis=1).reshape(group * classes, d))
    att = jnp.concatenate(atts, axis=0).astype(BF16)
    att_ref[...] = att
    upd = jnp.concatenate([cls] * bps, axis=0) + mm(att, wo_ref[...])
    send_ref[...] = mm(permutation(rows, classes), upd.astype(BF16)).astype(BF16)


def group_mask(group, dates):
    g = lax.broadcasted_iota(jnp.int32, (group, 1, 256), 0)
    c = (lax.broadcasted_iota(jnp.int32, (group, 1, 256), 2) % 128) // dates
    return (g == c).astype(F32)


def temporal_bwd(back_ref, pix_ref, enc_ref, cls_ref, gain_ref, w_ref, wo_ref,
                 nd_ref, kn_ref, rk_ref, v_ref, ad_ref, ac_ref, att_ref, cq_ref,
                 dw_ref, dgain_ref, dcls_ref):
    d = pix_ref.shape[-1]
    dates = pix_ref.shape[2]
    classes = cls_ref.shape[0]
    gain = gain_ref[...]
    x = date_sequence(pix_ref[...], enc_ref[...])
    rows = x.shape[0]
    bps = rows // dates
    cls = cls_ref[...].astype(F32)
    inv_c = norm_scale(cls)
    nc = (cls * inv_c * gain).astype(BF16)
    nd = nd_ref[...]
    ones = head_ones(d)
    hm = head_mask(d)
    group = 128 // dates
    du = mm(permutation(rows, rows // classes), back_ref[...]).astype(BF16)
    dw_ref[:, 3 * d :] = mm(att_ref[...], du, 0, 0)
    do = rounded(mm(du, wo_ref[...], 1, 1))
    qn = cq_ref[0]
    rq = cq_ref[1]
    kcn = cq_ref[2]
    rkc = cq_ref[3]
    vct = jnp.concatenate([cq_ref[4].astype(BF16)] * group, axis=0)
    kct = jnp.concatenate([kcn] * group, axis=0)
    qe = expand_heads(qn, hm)
    seg = same_block(128, 128, dates).astype(BF16)
    bm = group_mask(group, dates)
    qnt = jnp.concatenate([qn] * group, axis=0)
    rqt = jnp.concatenate([rq] * group, axis=0)
    rkct = jnp.concatenate([rkc] * group, axis=0)
    w = w_ref[...]
    wq, wk, wv = w[:, :d], w[:, d : 2 * d], w[:, 2 * d :]
    nct = jnp.concatenate([nc] * group, axis=0)
    dwq = jnp.zeros((d, d), F32)
    dwk = jnp.zeros((d, d), F32)
    dwv = jnp.zeros((d, d), F32)
    dnc = jnp.zeros((classes, d), F32)
    dgain = jnp.zeros((1, d), F32)
    xhat = x * norm_scale(x)
    for g in range(bps // group):
        lanes = slice(g * 128, (g + 1) * 128)
        ad = ad_ref[:, lanes]
        ac = ac_ref[:, lanes]
        a2 = jnp.concatenate([ad, ac], axis=1)
        aexp = (a2[None] * bm).reshape(-1, 256).astype(BF16)
        vst = jnp.concatenate([v_ref[lanes, :], vct], axis=0)
        doe = (do[lanes].reshape(group, 1, classes, d) * hm[None]).reshape(-1, d).astype(BF16)
        da = jnp.sum(mm(doe, vst, 1, 1).reshape(group, -1, 256) * bm, axis=0)
        da = rounded(da)
        dvst = mm(aexp, doe, 0, 0).astype(BF16)
        prod = da * a2
        dot = mm2(prod[:, :128] + prod[:, 128:], seg)
        ds = normalizer_sharpness * a2 * (da - jnp.concatenate([dot, dot], axis=1))
        kn = kn_ref[lanes, :]
        kst = jnp.concatenate([kn, kct], axis=0)
        dse = (ds[None] * bm).reshape(-1, 256)
        dqn = jnp.sum(mm3(dse, kst).reshape(group, HEADS, classes, d) * hm[None], axis=1)
        dqn = dqn.reshape(group * classes, d)
        dkst = mm3(ds, qe, 0, 0)
        dq = unit_back(dqn, qnt, rqt, ones)
        dk = unit_back(dkst[:128], kn, rk_ref[lanes, :], ones)
        dkc = unit_back(dkst[128:], kct, rkct, ones)
        ndg = nd[lanes]
        dwq += mm2r(nct, dq, 0, 0)
        dwk += mm2r(ndg, dk, 0, 0) + mm2r(nct, dkc, 0, 0)
        dwv += mm(ndg, dvst[:128], 0, 0) + mm(nct, dvst[128:], 0, 0)
        dn_k = rounded(mm2(jnp.concatenate([dk, dkc], axis=0), wk, 1, 1))
        dn = rounded(rounded(mm(dvst, wv, 1, 1)) + dn_k)
        dn_c = rounded(dn[128:] + rounded(mm2(dq, wq, 1, 1)))
        dgain += jnp.sum(dn[:128] * xhat[lanes], axis=0, keepdims=True)
        dnc += jnp.sum(dn_c.reshape(group, classes, d), axis=0)
    dw_ref[:, :d] = dwq
    dw_ref[:, d : 2 * d] = dwk
    dw_ref[:, 2 * d : 3 * d] = dwv
    dgain_ref[...] = dgain + jnp.sum(dnc * cls * inv_c, axis=0, keepdims=True)
    t = dnc * gain
    dcls = inv_c * (t - cls * (inv_c * inv_c * jnp.mean(t * cls, axis=-1, keepdims=True)))
    dcls_ref[...] = dcls + jnp.sum(du.astype(F32).reshape(bps, classes, d), axis=0)


def spatial_rows(recv_ref, kinds):
    sources, rows, d = recv_ref.shape
    n = rows // kinds
    blocks = [recv_ref[s].astype(F32) for s in range(sources)]
    return jnp.concatenate(
        [blocks[s][k * n : (k + 1) * n] for k in range(kinds) for s in range(sources)], axis=0
    )


def spatial_fwd(kinds, tiles, recv_ref, gain_ref, w_ref, wo_ref, head_ref,
                u_ref, n_ref, qk_ref, r_ref, v_ref, a_ref, o_ref, hid_ref, raw_ref, sum_ref):
    d = recv_ref.shape[-1]
    u = spatial_rows(recv_ref, kinds)
    u_ref[...] = u
    rows = u.shape[0]
    n = (u * norm_scale(u) * gain_ref[...]).astype(BF16)
    n_ref[...] = n
    ones = head_ones(d)
    hm = head_mask(d)
    qkv = mm(n, w_ref[...])
    qn, rq = unit(qkv[:, :d], ones)
    kn, rk = unit(qkv[:, d : 2 * d], ones)
    v = qkv[:, 2 * d :].astype(BF16)
    qk_ref[0] = qn
    qk_ref[1] = kn
    r_ref[0] = rq
    r_ref[1] = rk
    v_ref[...] = v
    per = rows // kinds
    patches = per // (recv_ref.shape[0] * tiles)
    ri = (lax.broadcasted_iota(jnp.int32, (per, per), 0) // patches) % tiles
    ci = (lax.broadcasted_iota(jnp.int32, (per, per), 1) // patches) % tiles
    tm = jnp.concatenate([(ri == ci).astype(F32)] * HEADS, axis=0)
    outs = []
    for k in range(kinds):
        rs = slice(k * per, (k + 1) * per)
        e = jnp.exp(normalizer_sharpness * mm3(expand_heads(qn[rs], hm), kn[rs], 1, 1)) * tm
        a = e / jnp.sum(e, axis=-1, keepdims=True)
        a_ref[k] = a
        outs.append(fold_heads(mm(a.astype(BF16), v[rs]), hm))
    o = jnp.concatenate(outs, axis=0).astype(BF16)
    o_ref[...] = o
    hid = u + mm(o, wo_ref[...])
    hid_ref[...] = hid
    raw = jnp.sum(hid * head_ref[...], axis=-1, keepdims=True)
    raw = jnp.broadcast_to(raw, (rows, 128))
    raw_ref[...] = raw
    ex = jnp.exp(logit_cap * jnp.tanh(raw / logit_cap))
    sum_ref[...] = jnp.sum(ex.reshape(kinds, per, 128), axis=0)


def spatial_bwd(kinds, tiles, total_tiles, tot_ref, label_ref, slot_ref, gain_ref, w_ref, wo_ref, head_ref,
                u_ref, n_ref, qk_ref, r_ref, v_ref, a_ref, o_ref, hid_ref, raw_ref,
                send_ref, dw_ref, dgain_ref, dhead_ref, loss_ref):
    d = u_ref.shape[-1]
    rows = u_ref.shape[0]
    per = rows // kinds
    sources = tot_ref.shape[0]
    total = jnp.sum(tot_ref[...], axis=0)
    total = jnp.concatenate([total] * kinds, axis=0)
    th = jnp.tanh(raw_ref[...] / logit_cap)
    logits = logit_cap * th
    kind = lax.broadcasted_iota(jnp.int32, (rows, 128), 0) // per
    ind = (jnp.concatenate([label_ref[...]] * kinds, axis=0) == kind).astype(F32)
    slot = jnp.concatenate([slot_ref[...]] * kinds, axis=0)
    loss_ref[...] = jnp.sum(ind * (jnp.log(total) - logits) * slot, axis=0, keepdims=True)
    draw = (jnp.exp(logits) / total - ind) / total_tiles * (1.0 - th * th)
    dr = jnp.concatenate([draw] * (d // 128), axis=1)
    head = head_ref[...]
    dhead_ref[...] = jnp.sum(dr * hid_ref[...], axis=0, keepdims=True)
    col = mm2r(o_ref[...], draw, 0, 0)
    dw_ref[:, 3 * d :] = jnp.concatenate([col] * (d // 128), axis=1) * head
    head_back = mm2(jnp.broadcast_to(head, (8, d)), wo_ref[...], 1, 1)[:1]
    do = rounded(dr * head_back)
    ones = head_ones(d)
    hm = head_mask(d)
    dqs, dks, dvs = [], [], []
    for k in range(kinds):
        rs = slice(k * per, (k + 1) * per)
        a = a_ref[k]
        doe = expand_heads(do[rs], hm).astype(BF16)
        da = rounded(mm(doe, v_ref[rs, :], 1, 1))
        dvs.append(mm(a.astype(BF16), doe, 0, 0))
        ds = normalizer_sharpness * a * (da - jnp.sum(da * a, axis=-1, keepdims=True))
        qn = qk_ref[0, rs, :]
        kn = qk_ref[1, rs, :]
        dqs.append(unit_back(fold_heads(mm3(ds, kn), hm), qn, r_ref[0, rs, :], ones))
        dks.append(unit_back(mm3(ds, expand_heads(qn, hm), 0, 0), kn, r_ref[1, rs, :], ones))
    dq = jnp.concatenate(dqs, axis=0)
    dk = jnp.concatenate(dks, axis=0)
    dv = jnp.concatenate(dvs, axis=0).astype(BF16)
    n = n_ref[...]
    dw_ref[:, :d] = mm2r(n, dq, 0, 0)
    dw_ref[:, d : 2 * d] = mm2r(n, dk, 0, 0)
    dw_ref[:, 2 * d : 3 * d] = mm(n, dv, 0, 0)
    w = w_ref[...]
    dn = rounded(rounded(mm(dv, w[:, 2 * d :], 1, 1)) + rounded(mm2(dk, w[:, d : 2 * d], 1, 1)))
    dn = rounded(dn + rounded(mm2(dq, w[:, :d], 1, 1)))
    u = u_ref[...]
    inv = norm_scale(u)
    dgain_ref[...] = jnp.sum(dn * u * inv, axis=0, keepdims=True)
    t = dn * gain_ref[...]
    du = dr * head + inv * (t - u * (inv * inv * jnp.mean(t * u, axis=-1, keepdims=True)))
    m = per // sources
    for s in range(sources):
        parts = [du[k * per + s * m : k * per + (s + 1) * m] for k in range(kinds)]
        send_ref[s] = jnp.concatenate(parts, axis=0).astype(BF16)


MESH = pl.DeviceIdType.MESH


def enter(devices):
    barrier = pltpu.get_barrier_semaphore()
    for dev in devices:
        pl.semaphore_signal(barrier, inc=1, device_id=dev, device_id_type=MESH)
    pl.semaphore_wait(barrier, len(devices))


def swap_kernel(count, whole, x_ref, o_ref, send_sem, recv_sem, own_sem):
    me = lax.axis_index("inner")
    others = [lax.rem(me + k, count) for k in range(1, count)]
    own = pltpu.make_async_copy(x_ref if whole else x_ref.at[me], o_ref.at[me], own_sem)
    own.start()
    enter([{"inner": dev} for dev in others])
    copies = []
    for k, dev in enumerate(others):
        copy = pltpu.make_async_remote_copy(
            src_ref=x_ref if whole else x_ref.at[dev], dst_ref=o_ref.at[me],
            send_sem=send_sem.at[k], recv_sem=recv_sem.at[k],
            device_id={"inner": dev}, device_id_type=MESH,
        )
        copy.start()
        copies.append(copy)
    own.wait()
    for copy in copies:
        copy.wait()


def swap(x, count, whole, cid):
    shape = ((count,) + x.shape) if whole else x.shape
    return pl.pallas_call(
        functools.partial(swap_kernel, count, whole),
        out_shape=jax.ShapeDtypeStruct(shape, x.dtype),
        in_specs=vmem(1),
        out_specs=vmem(1)[0],
        scratch_shapes=[
            pltpu.SemaphoreType.DMA((count - 1,)),
            pltpu.SemaphoreType.DMA((count - 1,)),
            pltpu.SemaphoreType.DMA,
        ],
        compiler_params=params(collective_id=cid, has_side_effects=True),
    )(x)


def weights_kernel(wq_ref, wo_ref, oq_ref, oo_ref, send_sem, recv_sem, own_sem):
    pipe = lax.axis_index("pipe")
    dp = lax.axis_index("dp")
    core = lax.rem(dp, 2)
    far = {"pipe": 1 - pipe}
    near = {"dp": dp + 1 - 2 * core}
    half = wq_ref.shape[1] // 2
    mine = pl.ds(pl.multiple_of(core * half, half), half)
    owns = []
    for k, (src, dst) in enumerate(((wq_ref, oq_ref), (wo_ref, oo_ref))):
        own = pltpu.make_async_copy(src.at[0], dst.at[pipe], own_sem.at[k])
        own.start()
        owns.append(own)
    enter([far, near])
    firsts = []
    for k, (src, dst) in enumerate(((wq_ref, oq_ref), (wo_ref, oo_ref))):
        copy = pltpu.make_async_remote_copy(
            src_ref=src.at[0, mine], dst_ref=dst.at[pipe, mine],
            send_sem=send_sem.at[k], recv_sem=recv_sem.at[k],
            device_id=far, device_id_type=MESH,
        )
        copy.start()
        firsts.append(copy)
    seconds = []
    for k, dst in enumerate((oq_ref, oo_ref)):
        firsts[k].wait_recv()
        copy = pltpu.make_async_remote_copy(
            src_ref=dst.at[1 - pipe, mine], dst_ref=dst.at[1 - pipe, mine],
            send_sem=send_sem.at[2 + k], recv_sem=recv_sem.at[2 + k],
            device_id=near, device_id_type=MESH,
        )
        copy.start()
        seconds.append(copy)
    for copy in firsts:
        copy.wait_send()
    for copy in seconds:
        copy.wait()
    for own in owns:
        own.wait()


def bring_weights(wqkv, wout, cid):
    return pl.pallas_call(
        weights_kernel,
        out_shape=[
            jax.ShapeDtypeStruct((2,) + wqkv.shape[1:], wqkv.dtype),
            jax.ShapeDtypeStruct((2,) + wout.shape[1:], wout.dtype),
        ],
        in_specs=vmem(2),
        out_specs=vmem(2),
        scratch_shapes=[
            pltpu.SemaphoreType.DMA((4,)),
            pltpu.SemaphoreType.DMA((4,)),
            pltpu.SemaphoreType.DMA((2,)),
        ],
        compiler_params=params(collective_id=cid, has_side_effects=True),
    )(wqkv, wout)


def total_kernel(g_ref, x_ref, o_ref, ox_ref, a0, a1, a2, a3, a4, b0, b1, b2, b3, b4, xs, xr, send_sem, recv_sem):
    pipe = lax.axis_index("pipe")
    dp = lax.axis_index("dp")
    inner = lax.axis_index("inner")
    core = lax.rem(dp, 2)
    y = dp // 2
    z_hi = inner // 2
    z_lo = lax.rem(inner, 2)
    rows = g_ref.shape[1]
    partners = [
        {"dp": dp + 1 - 2 * core},
        {"pipe": 1 - pipe},
        {"dp": dp + 2 - 4 * y},
        {"inner": inner + 2 - 4 * z_hi},
        {"inner": inner + 1 - 2 * z_lo},
    ]
    enter(partners)

    def send(k, src, dst, sem):
        copy = pltpu.make_async_remote_copy(
            src_ref=src, dst_ref=dst, send_sem=send_sem.at[sem], recv_sem=recv_sem.at[sem],
            device_id=partners[k], device_id_type=MESH,
        )
        copy.start()
        return copy

    def part(bit, size):
        return pl.ds(pl.multiple_of(bit * size, size), size)

    started = []
    half = rows // 2
    main = send(0, g_ref.at[:, part(1 - core, half)], b0, 0)
    small = send(0, x_ref, xr.at[pl.ds(0, 2)], 5)
    main.wait_recv()
    a0[...] = g_ref[:, part(core, half)] + b0[...]
    small.wait_recv()
    xs[pl.ds(0, 2)] = x_ref[...] + xr[pl.ds(0, 2)]
    started += [main, small]
    main = send(1, a0.at[1 - pipe], b1, 1)
    small = send(1, xs.at[1 - pipe], xr.at[2], 6)
    main.wait_recv()
    a1[...] = a0[pipe] + b1[...]
    small.wait_recv()
    xs[2] = xs[pipe] + xr[2]
    started += [main, small]
    source, size = a1, half
    for k, bit, acc, got in ((2, y, a2, b2), (3, z_hi, a3, b3), (4, z_lo, a4, b4)):
        size //= 2
        main = send(k, source.at[part(1 - bit, size)], got, k)
        small = send(k, xs.at[k], xr.at[k + 1], 5 + k)
        main.wait_recv()
        acc[...] = source[part(bit, size)] + got[...]
        small.wait_recv()
        xs[k + 1] = xs[k] + xr[k + 1]
        started += [main, small]
        source = acc
    ox_ref[...] = xs[5]
    start = core * half + y * (half // 2) + z_hi * (half // 4) + z_lo * size
    o_ref[pl.ds(pl.multiple_of(start, size), size)] = a4[...]
    for n, (k, bit) in enumerate(((4, z_lo), (3, z_hi), (2, y), (0, core))):
        span = pl.ds(pl.multiple_of(start, size), size)
        copy = send(k, o_ref.at[span], o_ref.at[span], 10 + n)
        copy.wait_recv()
        started.append(copy)
        start = start - bit * size
        size *= 2
    for copy in started:
        copy.wait_send()


def total(g, x, cid):
    rows, width = g.shape[1:]
    half = rows // 2
    sizes = [(2, half, width), (half, width), (half // 2, width), (half // 4, width), (half // 8, width)]
    return pl.pallas_call(
        total_kernel,
        out_shape=[
            jax.ShapeDtypeStruct((rows, width), F32),
            jax.ShapeDtypeStruct(x.shape[1:], F32),
        ],
        in_specs=vmem(2),
        out_specs=vmem(2),
        scratch_shapes=[pltpu.VMEM(s, F32) for s in sizes] * 2
        + [pltpu.VMEM((6,) + x.shape[1:], F32)] * 2
        + [pltpu.SemaphoreType.DMA((14,)), pltpu.SemaphoreType.DMA((14,))],
        compiler_params=params(collective_id=cid, has_side_effects=True),
    )(g, x)


def local(fn, outs, *args):
    return pl.pallas_call(
        fn,
        out_shape=[jax.ShapeDtypeStruct(s, t) for s, t in outs],
        in_specs=vmem(len(args)),
        out_specs=vmem(len(outs)),
        compiler_params=params(),
    )(*args)


def shards(pixels, date_days, clear_count, batch_slot, labels, class_tokens, section_gain,
           segment_probe_lookup_content, section_out, head_vec):
    tiles_dev, patches_dev, dates, width = pixels.shape
    inner_count = lax.axis_size("inner")
    kinds = CLASSES // inner_count
    total_tiles = tiles_dev * lax.axis_size("dp")
    group = lax.axis_index("inner")
    pipe_pos = lax.axis_index("pipe")
    tiles = tiles_dev // 2
    rows = tiles * patches_dev * dates
    batch_norm = 1.0 / (total_tiles // MICRO * PATCHES)
    w_all, wo_all = bring_weights(segment_probe_lookup_content, section_out, 0)
    gains = lax.all_gather(section_gain, "pipe", axis=0, tiled=True)

    def own(a):
        return lax.dynamic_slice_in_dim(a, pipe_pos * tiles, tiles, 0)

    pix, days, counts, label, slot = map(own, (pixels, date_days, clear_count, labels, batch_slot))
    channel = jnp.arange(width)
    frequency = jnp.exp((channel // 2 * 2).astype(F32) * (-math.log(10000.0) / width))
    phases = days.astype(F32)[:, :, None] * frequency
    enc = jnp.where(channel % 2 == 0, jnp.sin(phases), jnp.cos(phases))
    mask = (jnp.arange(dates)[None, None] < counts[:, None, None]).astype(F32)
    mask = jnp.broadcast_to(mask, (tiles, patches_dev, dates)).reshape(1, rows)
    label_rows = label.reshape(tiles, inner_count, patches_dev) - group * kinds
    label_rows = jnp.swapaxes(label_rows, 0, 1).reshape(-1, 1)
    per = label_rows.shape[0]
    label_rows = jnp.broadcast_to(label_rows, (per, 128))
    slot_rows = jnp.broadcast_to(slot[None, :, None], (inner_count, tiles, patches_dev)).reshape(per, 1)
    slot_rows = (slot_rows == jnp.arange(128)[None]).astype(F32) * batch_norm
    w0, w1 = w_all[0], w_all[1]
    wo0, wo1 = wo_all[0], wo_all[1]
    g0, g1 = gains[0:1], gains[1:2]
    head = head_vec.reshape(1, width)
    hq = HEADS * CLASSES
    f, b = F32, BF16
    send, *saved = local(
        temporal_fwd,
        [((rows, width), b), ((rows, width), b), ((rows, width), f), ((rows, width), f), ((rows, width), b),
         ((hq, rows), f), ((hq, rows), f), ((rows, width), b), ((5, CLASSES, width), f)],
        pix, enc, mask, class_tokens, g0, w0, wo0,
    )
    recv = swap(send.reshape(inner_count, -1, width), inner_count, False, 1)
    srows = kinds * per
    *kept, sums = local(
        functools.partial(spatial_fwd, kinds, tiles),
        [((srows, width), f), ((srows, width), b), ((2, srows, width), f), ((2, srows, width), f),
         ((srows, width), b), ((kinds, HEADS * per, per), f), ((srows, width), b), ((srows, width), f),
         ((srows, 128), f), ((per, 128), f)],
        recv, g1, w1, wo1, head,
    )
    totals = swap(sums, inner_count, True, 2)
    back, dw1, dg1, dhead, loss = local(
        functools.partial(spatial_bwd, kinds, tiles, total_tiles),
        [((inner_count, srows // inner_count, width), b), ((width, 4 * width), f), ((1, width), f),
         ((1, width), f), ((1, 128), f)],
        totals, label_rows, slot_rows, g1, w1, wo1, head, *kept,
    )
    returned = swap(back, inner_count, False, 3).reshape(rows, width)
    dw0, dg0, dcls = local(
        temporal_bwd,
        [((width, 4 * width), f), ((1, width), f), ((CLASSES, width), f)],
        returned, pix, enc, class_tokens, g0, w0, wo0, *saved,
    )
    common = [dcls.reshape(-1, 128), dhead.reshape(-1, 128), loss]
    pad = -(dcls.size // 128 + dhead.size // 128 + 1 + width // 128) % 8
    fill = [jnp.zeros((pad, 128), F32)]
    extra = jnp.stack(
        [jnp.concatenate(common + [g.reshape(-1, 128)] + fill, axis=0) for g in (dg0, dg1)]
    )
    grad, small = total(jnp.stack([dw0, dw1]), extra, 4)
    nc, nh = dcls.size // 128, width // 128
    return (
        small[nc + nh, :MICRO],
        small[:nc].reshape(CLASSES, width),
        small[nc + nh + 1 : nc + 2 * nh + 1].reshape(1, width),
        grad[None, :, : 3 * width],
        grad[None, :, 3 * width :],
        small[nc : nc + nh].reshape(width),
    )


def solution(mesh):
    placed = (
        P("dp", "inner", None, None),
        P("dp", None),
        P("dp"),
        P("dp"),
        P("dp", None),
        P(),
        P("pipe", None),
        P("pipe", None, None),
        P("pipe", None, None),
        P(),
    )

    def body(*args):
        tiles_dev, patches_dev, dates, width = args[0].shape
        pairs = tiles_dev // 2 * patches_dev
        sizes = tuple(mesh.shape[a] for a in ("pipe", "dp", "inner"))
        fits = sizes == (2, 4, 4) and pairs % 8 == 0 and dates == CLASSES and width == 256
        return (shards if fits else shards_general)(*args)

    return jax.shard_map(
        body,
        mesh=mesh,
        in_specs=placed,
        out_specs=(P(), P(), P("pipe", None), P("pipe", None, None), P("pipe", None, None), P()),
        check_vma=False,
    )
```

```python
import functools
import math

import jax
import jax.numpy as jnp
from jax import lax
from jax.experimental import pallas as pl
from jax.experimental.pallas import tpu as pltpu
from jax.sharding import PartitionSpec as P

HEADS = 8
CLASSES = 16
PATCHES = 48
MICRO = 4


normalizer_sharpness = 10.0
logit_cap = 15.0
norm_eps = 1e-05
head_eps = 1e-06


def matmul_f32(left_side, right_side):
    return jnp.einsum(
        "...d,de->...e",
        left_side,
        right_side.astype(jnp.bfloat16),
        preferred_element_type=jnp.float32,
    )


def rms_norm(inputs, gain_vec):
    inverse_rms = lax.rsqrt(jnp.mean(inputs * inputs, axis=-1, keepdims=True) + norm_eps)
    return inputs * inverse_rms * gain_vec


def unit_heads(values):
    shaped = values.reshape(values.shape[:-1] + (HEADS, values.shape[-1] // HEADS))
    return shaped * lax.rsqrt(jnp.sum(shaped * shaped, axis=-1, keepdims=True) + head_eps)


def temporal(pixel_rows, date_days, counts, params):
    class_init, gain_vec, w_qkv, w_out = params
    batch_count, patches, dates_max, model_width = pixel_rows.shape
    classes = class_init.shape[0]
    band_channel = jnp.arange(model_width)
    frequency = jnp.exp(
        (band_channel // 2 * 2).astype(jnp.float32) * (-math.log(10000.0) / model_width)
    )
    phases = date_days.astype(jnp.float32)[:, :, None] * frequency
    encoding = jnp.where(band_channel % 2 == 0, jnp.sin(phases), jnp.cos(phases))
    date_rows = pixel_rows.astype(jnp.float32) + encoding[:, None]
    class_rows = jnp.broadcast_to(class_init, (batch_count, patches, classes, model_width))
    sequence = jnp.concatenate([class_rows, date_rows], axis=2)
    normed = rms_norm(sequence, gain_vec).astype(jnp.bfloat16)
    probe_entry_lines = unit_heads(matmul_f32(normed[:, :, :classes], w_qkv[:, :model_width]))
    lookup_entry_lines = unit_heads(matmul_f32(normed, w_qkv[:, model_width : 2 * model_width]))
    value_rows = matmul_f32(normed, w_qkv[:, 2 * model_width :]).astype(jnp.bfloat16)
    value_heads = value_rows.reshape(
        batch_count, patches, classes + dates_max, HEADS, model_width // HEADS
    )
    affinity_logit_grid = normalizer_sharpness * jnp.einsum(
        "ohbyv,ohsyv->ohybs", probe_entry_lines, lookup_entry_lines, precision=lax.Precision.HIGHEST
    )
    position = jnp.arange(classes + dates_max)
    key_mask = (
        (position[None, :] < classes) | (position[None, :] - classes < counts[:, None])
    ).astype(jnp.float32)
    raised = jnp.exp(affinity_logit_grid) * key_mask[:, None, None, None, :]
    weights = (raised / jnp.sum(raised, axis=-1, keepdims=True)).astype(jnp.bfloat16)
    attended = jnp.einsum(
        "bphqk,bpkhe->bpqhe", weights, value_heads, preferred_element_type=jnp.float32
    )
    attended = attended.reshape(batch_count, patches, classes, model_width).astype(jnp.bfloat16)
    updated = sequence[:, :, :classes] + matmul_f32(attended, w_out)
    return jnp.swapaxes(updated, 1, 2).astype(jnp.bfloat16)


def spatial(inputs, params):
    gain_vec, w_qkv, w_out, head_vec = params
    batch_count, groups, classes, patches, model_width = inputs.shape
    class_seq = (
        jnp.swapaxes(inputs, 1, 2)
        .reshape(batch_count, classes, groups * patches, model_width)
        .astype(jnp.float32)
    )
    normed = rms_norm(class_seq, gain_vec).astype(jnp.bfloat16)
    probe_entry_lines = unit_heads(matmul_f32(normed, w_qkv[:, :model_width]))
    lookup_entry_lines = unit_heads(matmul_f32(normed, w_qkv[:, model_width : 2 * model_width]))
    value_rows = matmul_f32(normed, w_qkv[:, 2 * model_width :]).astype(jnp.bfloat16)
    value_heads = value_rows.reshape(
        batch_count, classes, groups * patches, HEADS, model_width // HEADS
    )
    affinity_logit_grid = normalizer_sharpness * jnp.einsum(
        "wisbx,wiqbx->wibsq", probe_entry_lines, lookup_entry_lines, precision=lax.Precision.HIGHEST
    )
    raised = jnp.exp(affinity_logit_grid)
    weights = (raised / jnp.sum(raised, axis=-1, keepdims=True)).astype(jnp.bfloat16)
    attended = jnp.einsum(
        "bchqk,bckhe->bcqhe", weights, value_heads, preferred_element_type=jnp.float32
    )
    attended = attended.reshape(batch_count, classes, groups * patches, model_width).astype(
        jnp.bfloat16
    )
    hidden = class_seq + matmul_f32(attended, w_out)
    raw_logits = jnp.einsum("bcpd,d->bcp", hidden, head_vec, precision=lax.Precision.HIGHEST)
    logits = logit_cap * jnp.tanh(raw_logits / logit_cap)
    return logits.reshape(batch_count, classes, groups, patches)


def shards_general(
    pixels,
    date_days,
    clear_count,
    batch_slot,
    labels,
    class_tokens,
    section_gain,
    segment_probe_lookup_content,
    section_out,
    head_vec,
):
    tiles_dev = pixels.shape[0]
    patches_dev = pixels.shape[1]
    model_width = pixels.shape[3]
    inner_count = lax.axis_size("inner")
    classes_dev = CLASSES // inner_count
    total_tiles = tiles_dev * lax.axis_size("dp")
    my_group = lax.axis_index("inner")
    class_ids = my_group * classes_dev + jnp.arange(classes_dev, dtype=jnp.int32)
    batch_norm = 1.0 / (total_tiles // MICRO * PATCHES)
    gains, qkv_all, out_all = (
        lax.all_gather(section_gain, "pipe", axis=0, tiled=True),
        lax.all_gather(
            segment_probe_lookup_content.astype(jnp.float32), "pipe", axis=0, tiled=True
        ),
        lax.all_gather(section_out.astype(jnp.float32), "pipe", axis=0, tiled=True),
    )
    pipe_pos = lax.axis_index("pipe")
    half_tiles = tiles_dev // 2
    first_params = (class_tokens.astype(jnp.float32), gains[0], qkv_all[0], out_all[0])
    second_params = (gains[1], qkv_all[1], out_all[1], head_vec)
    fold_shape = (1, inner_count, classes_dev, patches_dev, model_width)
    first_gradients = jax.tree.map(jnp.zeros_like, first_params)
    grads_second = jax.tree.map(jnp.zeros_like, second_params)
    loss_vec = jnp.zeros((MICRO,), jnp.float32)
    for tile_step in range(half_tiles):
        start = pipe_pos * half_tiles + tile_step
        single_pixel = lax.dynamic_slice_in_dim(pixels, start, 1, 0)
        days_one = lax.dynamic_slice_in_dim(date_days, start, 1, 0)
        count_one = lax.dynamic_slice_in_dim(clear_count, start, 1, 0)
        label_one = lax.dynamic_slice_in_dim(labels, start, 1, 0)
        slot_one = lax.dynamic_slice_in_dim(batch_slot, start, 1, 0)
        encoded, pull_first = jax.vjp(
            lambda params: temporal(single_pixel, days_one, count_one, params), first_params
        )
        arrived = lax.all_to_all(
            encoded.reshape(fold_shape), "inner", split_axis=1, concat_axis=1, tiled=True
        )
        logits, pull_second = jax.vjp(spatial, arrived, second_params)
        exp_logits = jnp.exp(logits)
        class_total = lax.psum(jnp.sum(exp_logits, axis=1), "inner")
        label_rows = label_one.reshape(1, 1, inner_count, patches_dev)
        indicator_rows = (label_rows == class_ids[None, :, None, None]).astype(jnp.float32)
        dlogit = (exp_logits / class_total[:, None] - indicator_rows) / total_tiles
        grad_in, grad_two = pull_second(dlogit)
        returned = lax.all_to_all(grad_in, "inner", split_axis=1, concat_axis=1, tiled=True)
        (derivative_lone,) = pull_first(returned.reshape(encoded.shape))
        first_gradients = jax.tree.map(
            lambda total, extra: total + extra, first_gradients, derivative_lone
        )
        grads_second = jax.tree.map(lambda total, extra: total + extra, grads_second, grad_two)
        loss_term = jnp.sum(indicator_rows * (jnp.log(class_total)[:, None] - logits)) * batch_norm
        loss_vec = loss_vec + loss_term * (jnp.arange(MICRO) == slot_one[0]).astype(jnp.float32)
    stacked = (
        jnp.stack([first_gradients[1], grads_second[0]]),
        jnp.stack([first_gradients[2], grads_second[1]]),
        jnp.stack([first_gradients[3], grads_second[2]]),
        first_gradients[0],
        grads_second[3],
        loss_vec,
    )
    summed = lax.psum(
        (stacked[0], stacked[1], stacked[2], stacked[3], stacked[4], stacked[5]),
        ("pipe", "dp", "inner"),
    )
    gain_grad = lax.dynamic_slice_in_dim(summed[0], pipe_pos, 1, 0)
    qkv_grad = lax.dynamic_slice_in_dim(summed[1], pipe_pos, 1, 0)
    out_grad = lax.dynamic_slice_in_dim(summed[2], pipe_pos, 1, 0)
    return (summed[5], summed[3], gain_grad, qkv_grad, out_grad, summed[4])


F32 = jnp.float32
BF16 = jnp.bfloat16
VMEM_LIMIT = 56 * 2**20


def params(**kw):
    return pltpu.CompilerParams(vmem_limit_bytes=VMEM_LIMIT, **kw)


def vmem(count):
    return [pl.BlockSpec(memory_space=pltpu.VMEM)] * count


def mm(a, b, ca=1, cb=0):
    return lax.dot_general(a, b, (((ca,), (cb,)), ((), ())), preferred_element_type=F32)


def split(a):
    hi = a.astype(BF16)
    return hi, (a - hi.astype(F32)).astype(BF16)


def mm2(a, b, ca=1, cb=0):
    hi, lo = split(a)
    return mm(hi, b, ca, cb) + mm(lo, b, ca, cb)


def mm2r(a, b, ca=1, cb=0):
    hi, lo = split(b)
    return mm(a, hi, ca, cb) + mm(a, lo, ca, cb)


def mm3(a, b, ca=1, cb=0):
    ah, al = split(a)
    bh, bl = split(b)
    return mm(ah, bh, ca, cb) + (mm(ah, bl, ca, cb) + mm(al, bh, ca, cb))


def same_block(rows, cols, size):
    r = lax.broadcasted_iota(jnp.int32, (rows, cols), 0) // size
    c = lax.broadcasted_iota(jnp.int32, (rows, cols), 1) // size
    return (r == c).astype(F32)


def head_ones(width):
    return same_block(width, width, width // HEADS).astype(BF16)


def head_mask(width):
    h = lax.broadcasted_iota(jnp.int32, (HEADS, 1, width), 0)
    c = lax.broadcasted_iota(jnp.int32, (HEADS, 1, width), 2) // (width // HEADS)
    return (h == c).astype(F32)


def unit(x, ones):
    r = lax.rsqrt(mm2(x * x, ones) + head_eps)
    return x * r, r


def unit_back(dxn, xn, r, ones):
    return r * (dxn - xn * mm2(dxn * xn, ones))


def norm_scale(x):
    return lax.rsqrt(jnp.mean(x * x, axis=-1, keepdims=True) + norm_eps)


def rounded(x):
    return x.astype(BF16).astype(F32)


def expand_heads(x, hm):
    n, d = x.shape
    return (x[None] * hm).reshape(HEADS * n, d)


def fold_heads(x, hm):
    n = x.shape[0] // HEADS
    return jnp.sum(x.reshape(HEADS, n, x.shape[1]) * hm, axis=0)


def permutation(n, outer):
    inner = n // outer
    r = lax.broadcasted_iota(jnp.int32, (n, n), 0)
    c = lax.broadcasted_iota(jnp.int32, (n, n), 1)
    return (c == (r % inner) * outer + r // inner).astype(F32).astype(BF16)


def date_sequence(pix, enc):
    return (pix.astype(F32) + enc[:, None]).reshape(-1, pix.shape[-1])


def own_tiles(tiles):
    return pl.ds(lax.axis_index("pipe") * tiles, tiles)


def clear_mask(count_ref, tiles, rows, dates):
    lane = lax.broadcasted_iota(jnp.int32, (1, rows), 1)
    first = lax.axis_index("pipe") * tiles
    mask = jnp.zeros((1, rows), F32)
    for t in range(tiles):
        clear = (lane // (rows // tiles) == t) & (lane % dates < count_ref[first + t])
        mask = mask + clear.astype(F32)
    return mask


def temporal_fwd(tiles, pix_ref, enc_ref, count_ref, cls_ref, gain_ref, w_ref, wo_ref,
                 send_ref, nd_ref, kn_ref, rk_ref, v_ref, ad_ref, ac_ref, att_ref, cq_ref):
    d = pix_ref.shape[-1]
    dates = pix_ref.shape[2]
    classes = cls_ref.shape[0]
    gain = gain_ref[0]
    w_ref = w_ref.at[0]
    wo_ref = wo_ref.at[0]
    x = date_sequence(pix_ref[own_tiles(tiles)], enc_ref[own_tiles(tiles)])
    rows = x.shape[0]
    bps = rows // dates
    mask = clear_mask(count_ref, tiles, rows, dates)
    nd = (x * norm_scale(x) * gain).astype(BF16)
    nd_ref[...] = nd
    cls = cls_ref[...].astype(F32)
    nc = (cls * norm_scale(cls) * gain).astype(BF16)
    ones = head_ones(d)
    hm = head_mask(d)
    kv = mm(nd, w_ref[:, d:])
    qkvc = mm(nc, w_ref[...])
    kn, rk = unit(kv[:, :d], ones)
    kn_ref[...] = kn
    rk_ref[...] = rk
    v = kv[:, d:].astype(BF16)
    v_ref[...] = v
    qn, rq = unit(qkvc[:, :d], ones)
    kcn, rkc = unit(qkvc[:, d : 2 * d], ones)
    vc = qkvc[:, 2 * d :].astype(BF16)
    cq_ref[0] = qn
    cq_ref[1] = rq
    cq_ref[2] = kcn
    cq_ref[3] = rkc
    cq_ref[4] = vc.astype(F32)
    group = 128 // dates
    qe = expand_heads(qn, hm)
    kct = jnp.concatenate([kcn] * group, axis=0)
    ed = jnp.exp(normalizer_sharpness * mm3(qe, kn, 1, 1)) * mask
    ec = jnp.exp(normalizer_sharpness * mm3(qe, kct, 1, 1))
    seg = same_block(128, 128, dates).astype(BF16)
    sum_c = mm2(ec, seg)
    vct = jnp.concatenate([vc] * group, axis=0)
    bm = group_mask(group, dates)
    atts = []
    for g in range(bps // group):
        lanes = slice(g * 128, (g + 1) * 128)
        e = ed[:, lanes]
        den = mm2(e, seg) + sum_c
        ad = e / den
        ac = ec / den
        ad_ref[:, lanes] = ad
        ac_ref[:, lanes] = ac
        aexp = (jnp.concatenate([ad, ac], axis=1)[None] * bm).reshape(-1, 256).astype(BF16)
        vst = jnp.concatenate([v[lanes], vct], axis=0)
        o = mm(aexp, vst).reshape(group, HEADS, classes, d)
        atts.append(jnp.sum(o * hm[None], axis=1).reshape(group * classes, d))
    att = jnp.concatenate(atts, axis=0).astype(BF16)
    att_ref[...] = att
    upd = jnp.concatenate([cls] * bps, axis=0) + mm(att, wo_ref[...])
    send = mm(permutation(rows, classes), upd.astype(BF16)).astype(BF16)
    part = send_ref.shape[1]
    for k in range(send_ref.shape[0]):
        send_ref[k] = send[k * part : (k + 1) * part]


def group_mask(group, dates):
    g = lax.broadcasted_iota(jnp.int32, (group, 1, 256), 0)
    c = (lax.broadcasted_iota(jnp.int32, (group, 1, 256), 2) % 128) // dates
    return (g == c).astype(F32)


def temporal_bwd(tiles, back_ref, pix_ref, enc_ref, cls_ref, gain_ref, w_ref, wo_ref,
                 nd_ref, kn_ref, rk_ref, v_ref, ad_ref, ac_ref, att_ref, cq_ref,
                 dw_ref, dgain_ref, dcls_ref):
    d = pix_ref.shape[-1]
    dates = pix_ref.shape[2]
    classes = cls_ref.shape[0]
    gain = gain_ref[0]
    w_ref = w_ref.at[0]
    wo_ref = wo_ref.at[0]
    x = date_sequence(pix_ref[own_tiles(tiles)], enc_ref[own_tiles(tiles)])
    rows = x.shape[0]
    bps = rows // dates
    cls = cls_ref[...].astype(F32)
    inv_c = norm_scale(cls)
    nc = (cls * inv_c * gain).astype(BF16)
    nd = nd_ref[...]
    ones = head_ones(d)
    hm = head_mask(d)
    group = 128 // dates
    back = jnp.concatenate([back_ref[k] for k in range(back_ref.shape[0])], axis=0)
    du = mm(permutation(rows, rows // classes), back).astype(BF16)
    dw_ref[:, 3 * d :] = mm(att_ref[...], du, 0, 0)
    do = rounded(mm(du, wo_ref[...], 1, 1))
    qn = cq_ref[0]
    rq = cq_ref[1]
    kcn = cq_ref[2]
    rkc = cq_ref[3]
    vct = jnp.concatenate([cq_ref[4].astype(BF16)] * group, axis=0)
    kct = jnp.concatenate([kcn] * group, axis=0)
    qe = expand_heads(qn, hm)
    seg = same_block(128, 128, dates).astype(BF16)
    bm = group_mask(group, dates)
    qnt = jnp.concatenate([qn] * group, axis=0)
    rqt = jnp.concatenate([rq] * group, axis=0)
    rkct = jnp.concatenate([rkc] * group, axis=0)
    w = w_ref[...]
    wq, wk, wv = w[:, :d], w[:, d : 2 * d], w[:, 2 * d :]
    nct = jnp.concatenate([nc] * group, axis=0)
    dwq = jnp.zeros((d, d), F32)
    dwk = jnp.zeros((d, d), F32)
    dwv = jnp.zeros((d, d), F32)
    dnc = jnp.zeros((classes, d), F32)
    dgain = jnp.zeros((1, d), F32)
    xhat = x * norm_scale(x)
    for g in range(bps // group):
        lanes = slice(g * 128, (g + 1) * 128)
        ad = ad_ref[:, lanes]
        ac = ac_ref[:, lanes]
        a2 = jnp.concatenate([ad, ac], axis=1)
        aexp = (a2[None] * bm).reshape(-1, 256).astype(BF16)
        vst = jnp.concatenate([v_ref[lanes, :], vct], axis=0)
        doe = (do[lanes].reshape(group, 1, classes, d) * hm[None]).reshape(-1, d).astype(BF16)
        da = jnp.sum(mm(doe, vst, 1, 1).reshape(group, -1, 256) * bm, axis=0)
        da = rounded(da)
        dvst = mm(aexp, doe, 0, 0).astype(BF16)
        prod = da * a2
        dot = mm2(prod[:, :128] + prod[:, 128:], seg)
        ds = normalizer_sharpness * a2 * (da - jnp.concatenate([dot, dot], axis=1))
        kn = kn_ref[lanes, :]
        kst = jnp.concatenate([kn, kct], axis=0)
        dse = (ds[None] * bm).reshape(-1, 256)
        dqn = jnp.sum(mm3(dse, kst).reshape(group, HEADS, classes, d) * hm[None], axis=1)
        dqn = dqn.reshape(group * classes, d)
        dkst = mm3(ds, qe, 0, 0)
        dq = unit_back(dqn, qnt, rqt, ones)
        dk = unit_back(dkst[:128], kn, rk_ref[lanes, :], ones)
        dkc = unit_back(dkst[128:], kct, rkct, ones)
        ndg = nd[lanes]
        dwq += mm2r(nct, dq, 0, 0)
        dwk += mm2r(ndg, dk, 0, 0) + mm2r(nct, dkc, 0, 0)
        dwv += mm(ndg, dvst[:128], 0, 0) + mm(nct, dvst[128:], 0, 0)
        dn_k = rounded(mm2(jnp.concatenate([dk, dkc], axis=0), wk, 1, 1))
        dn = rounded(rounded(mm(dvst, wv, 1, 1)) + dn_k)
        dn_c = rounded(dn[128:] + rounded(mm2(dq, wq, 1, 1)))
        dgain += jnp.sum(dn[:128] * xhat[lanes], axis=0, keepdims=True)
        dnc += jnp.sum(dn_c.reshape(group, classes, d), axis=0)
    dw_ref[:, :d] = dwq
    dw_ref[:, d : 2 * d] = dwk
    dw_ref[:, 2 * d : 3 * d] = dwv
    dgain_ref[...] = dgain + jnp.sum(dnc * cls * inv_c, axis=0, keepdims=True)
    t = dnc * gain
    dcls = inv_c * (t - cls * (inv_c * inv_c * jnp.mean(t * cls, axis=-1, keepdims=True)))
    dcls_ref[...] = dcls + jnp.sum(du.astype(F32).reshape(bps, classes, d), axis=0)


def spatial_rows(recv_ref, kinds):
    sources, rows, d = recv_ref.shape
    n = rows // kinds
    blocks = [recv_ref[s].astype(F32) for s in range(sources)]
    return jnp.concatenate(
        [blocks[s][k * n : (k + 1) * n] for k in range(kinds) for s in range(sources)], axis=0
    )


def spatial_fwd(kinds, tiles, recv_ref, gain_ref, w_ref, wo_ref, head_ref,
                u_ref, n_ref, qk_ref, r_ref, v_ref, a_ref, o_ref, hid_ref, raw_ref, sum_ref):
    d = recv_ref.shape[-1]
    gain_ref = gain_ref.at[1]
    w_ref = w_ref.at[1]
    wo_ref = wo_ref.at[1]
    u = spatial_rows(recv_ref, kinds)
    u_ref[...] = u
    rows = u.shape[0]
    n = (u * norm_scale(u) * gain_ref[...]).astype(BF16)
    n_ref[...] = n
    ones = head_ones(d)
    hm = head_mask(d)
    qkv = mm(n, w_ref[...])
    qn, rq = unit(qkv[:, :d], ones)
    kn, rk = unit(qkv[:, d : 2 * d], ones)
    v = qkv[:, 2 * d :].astype(BF16)
    qk_ref[0] = qn
    qk_ref[1] = kn
    r_ref[0] = rq
    r_ref[1] = rk
    v_ref[...] = v
    per = rows // kinds
    patches = per // (recv_ref.shape[0] * tiles)
    ri = (lax.broadcasted_iota(jnp.int32, (per, per), 0) // patches) % tiles
    ci = (lax.broadcasted_iota(jnp.int32, (per, per), 1) // patches) % tiles
    tm = jnp.concatenate([(ri == ci).astype(F32)] * HEADS, axis=0)
    outs = []
    for k in range(kinds):
        rs = slice(k * per, (k + 1) * per)
        e = jnp.exp(normalizer_sharpness * mm3(expand_heads(qn[rs], hm), kn[rs], 1, 1)) * tm
        a = e / jnp.sum(e, axis=-1, keepdims=True)
        a_ref[k] = a
        outs.append(fold_heads(mm(a.astype(BF16), v[rs]), hm))
    o = jnp.concatenate(outs, axis=0).astype(BF16)
    o_ref[...] = o
    hid = u + mm(o, wo_ref[...])
    hid_ref[...] = hid
    raw = jnp.sum(hid * head_ref[...], axis=-1, keepdims=True)
    raw = jnp.broadcast_to(raw, (rows, 128))
    raw_ref[...] = raw
    ex = jnp.exp(logit_cap * jnp.tanh(raw / logit_cap))
    sum_ref[...] = jnp.sum(ex.reshape(kinds, per, 128), axis=0)


def patch_columns(label_ref, slot_ref, sources, tiles, lanes):
    first = lax.axis_index("pipe") * tiles
    count = label_ref.shape[1]
    patches = count // sources
    shape = (sources * tiles * patches, count)
    row = lax.broadcasted_iota(jnp.int32, shape, 0)
    col = lax.broadcasted_iota(jnp.int32, shape, 1)
    tile = (row // patches) % tiles
    here = col == (row // (patches * tiles)) * patches + row % patches
    slot_shape = (shape[0], lanes)
    slot_tile = (lax.broadcasted_iota(jnp.int32, slot_shape, 0) // patches) % tiles
    lane = lax.broadcasted_iota(jnp.int32, slot_shape, 1)
    labels = jnp.zeros(shape, F32)
    slots = jnp.zeros(slot_shape, F32)
    for t in range(tiles):
        values = label_ref[pl.ds(first + t, 1), :].astype(F32)
        labels = labels + jnp.where(here & (tile == t), values, 0.0)
        slots = slots + ((slot_tile == t) & (lane == slot_ref[first + t])).astype(F32)
    return jnp.broadcast_to(jnp.sum(labels, axis=-1, keepdims=True), slot_shape), slots


def spatial_bwd(kinds, tiles, total_tiles, batch_norm, tot_ref, label_ref, slot_ref, gain_ref, w_ref, wo_ref, head_ref,
                u_ref, n_ref, qk_ref, r_ref, v_ref, a_ref, o_ref, hid_ref, raw_ref,
                send_ref, dw_ref, dgain_ref, dhead_ref, loss_ref):
    d = u_ref.shape[-1]
    gain_ref = gain_ref.at[1]
    w_ref = w_ref.at[1]
    wo_ref = wo_ref.at[1]
    rows = u_ref.shape[0]
    per = rows // kinds
    sources = tot_ref.shape[0]
    total = jnp.sum(tot_ref[...], axis=0)
    total = jnp.concatenate([total] * kinds, axis=0)
    th = jnp.tanh(raw_ref[...] / logit_cap)
    logits = logit_cap * th
    label, slot = patch_columns(label_ref, slot_ref, sources, tiles, 128)
    kind = lax.broadcasted_iota(jnp.int32, (rows, 128), 0) // per + lax.axis_index("inner") * kinds
    ind = (jnp.concatenate([label] * kinds, axis=0) == kind.astype(F32)).astype(F32)
    slot = jnp.concatenate([slot] * kinds, axis=0)
    loss = jnp.sum(ind * (jnp.log(total) - logits) * slot, axis=0, keepdims=True) * batch_norm
    loss_ref[...] = jnp.concatenate([loss] * (d // 128), axis=1)
    draw = (jnp.exp(logits) / total - ind) / total_tiles * (1.0 - th * th)
    dr = jnp.concatenate([draw] * (d // 128), axis=1)
    head = head_ref[...]
    dhead_ref[...] = jnp.sum(dr * hid_ref[...], axis=0, keepdims=True)
    col = mm2r(o_ref[...], draw, 0, 0)
    dw_ref[:, 3 * d :] = jnp.concatenate([col] * (d // 128), axis=1) * head
    head_back = mm2(jnp.broadcast_to(head, (8, d)), wo_ref[...], 1, 1)[:1]
    do = rounded(dr * head_back)
    ones = head_ones(d)
    hm = head_mask(d)
    dqs, dks, dvs = [], [], []
    for k in range(kinds):
        rs = slice(k * per, (k + 1) * per)
        a = a_ref[k]
        doe = expand_heads(do[rs], hm).astype(BF16)
        da = rounded(mm(doe, v_ref[rs, :], 1, 1))
        dvs.append(mm(a.astype(BF16), doe, 0, 0))
        ds = normalizer_sharpness * a * (da - jnp.sum(da * a, axis=-1, keepdims=True))
        qn = qk_ref[0, rs, :]
        kn = qk_ref[1, rs, :]
        dqs.append(unit_back(fold_heads(mm3(ds, kn), hm), qn, r_ref[0, rs, :], ones))
        dks.append(unit_back(mm3(ds, expand_heads(qn, hm), 0, 0), kn, r_ref[1, rs, :], ones))
    dq = jnp.concatenate(dqs, axis=0)
    dk = jnp.concatenate(dks, axis=0)
    dv = jnp.concatenate(dvs, axis=0).astype(BF16)
    n = n_ref[...]
    dw_ref[:, :d] = mm2r(n, dq, 0, 0)
    dw_ref[:, d : 2 * d] = mm2r(n, dk, 0, 0)
    dw_ref[:, 2 * d : 3 * d] = mm(n, dv, 0, 0)
    w = w_ref[...]
    dn = rounded(rounded(mm(dv, w[:, 2 * d :], 1, 1)) + rounded(mm2(dk, w[:, d : 2 * d], 1, 1)))
    dn = rounded(dn + rounded(mm2(dq, w[:, :d], 1, 1)))
    u = u_ref[...]
    inv = norm_scale(u)
    dgain_ref[...] = jnp.sum(dn * u * inv, axis=0, keepdims=True)
    t = dn * gain_ref[...]
    du = dr * head + inv * (t - u * (inv * inv * jnp.mean(t * u, axis=-1, keepdims=True)))
    m = per // sources
    for s in range(sources):
        parts = [du[k * per + s * m : k * per + (s + 1) * m] for k in range(kinds)]
        send_ref[s] = jnp.concatenate(parts, axis=0).astype(BF16)


MESH = pl.DeviceIdType.MESH


def enter(devices):
    barrier = pltpu.get_barrier_semaphore()
    for dev in devices:
        pl.semaphore_signal(barrier, inc=1, device_id=dev, device_id_type=MESH)
    pl.semaphore_wait(barrier, len(devices))


def swap_kernel(count, whole, x_ref, o_ref, send_sem, recv_sem, own_sem):
    me = lax.axis_index("inner")
    others = [lax.rem(me + k, count) for k in range(1, count)]
    own = pltpu.make_async_copy(x_ref if whole else x_ref.at[me], o_ref.at[me], own_sem)
    own.start()
    enter([{"inner": dev} for dev in others])
    copies = []
    for k, dev in enumerate(others):
        copy = pltpu.make_async_remote_copy(
            src_ref=x_ref if whole else x_ref.at[dev], dst_ref=o_ref.at[me],
            send_sem=send_sem.at[k], recv_sem=recv_sem.at[k],
            device_id={"inner": dev}, device_id_type=MESH,
        )
        copy.start()
        copies.append(copy)
    own.wait()
    for copy in copies:
        copy.wait()


def swap(x, count, whole, cid):
    shape = ((count,) + x.shape) if whole else x.shape
    return pl.pallas_call(
        functools.partial(swap_kernel, count, whole),
        out_shape=jax.ShapeDtypeStruct(shape, x.dtype),
        in_specs=vmem(1),
        out_specs=vmem(1)[0],
        scratch_shapes=[
            pltpu.SemaphoreType.DMA((count - 1,)),
            pltpu.SemaphoreType.DMA((count - 1,)),
            pltpu.SemaphoreType.DMA,
        ],
        compiler_params=params(collective_id=cid, has_side_effects=True),
    )(x)


def weights_kernel(wq_ref, wo_ref, g_ref, oq_ref, oo_ref, og_ref, send_sem, recv_sem, own_sem):
    pipe = lax.axis_index("pipe")
    dp = lax.axis_index("dp")
    core = lax.rem(dp, 2)
    far = {"pipe": 1 - pipe}
    near = {"dp": dp + 1 - 2 * core}
    half = wq_ref.shape[1] // 2
    mine = pl.ds(pl.multiple_of(core * half, half), half)
    owns = []
    for k, (src, dst) in enumerate(((wq_ref, oq_ref), (wo_ref, oo_ref))):
        own = pltpu.make_async_copy(src.at[0], dst.at[pipe], own_sem.at[k])
        own.start()
        owns.append(own)
    og_ref[pipe] = g_ref[...]
    enter([far, near])
    gains = pltpu.make_async_remote_copy(
        src_ref=g_ref, dst_ref=og_ref.at[pipe],
        send_sem=send_sem.at[4], recv_sem=recv_sem.at[4],
        device_id=far, device_id_type=MESH,
    )
    gains.start()
    firsts = []
    for k, (src, dst) in enumerate(((wq_ref, oq_ref), (wo_ref, oo_ref))):
        copy = pltpu.make_async_remote_copy(
            src_ref=src.at[0, mine], dst_ref=dst.at[pipe, mine],
            send_sem=send_sem.at[k], recv_sem=recv_sem.at[k],
            device_id=far, device_id_type=MESH,
        )
        copy.start()
        firsts.append(copy)
    seconds = []
    for k, dst in enumerate((oq_ref, oo_ref)):
        firsts[k].wait_recv()
        copy = pltpu.make_async_remote_copy(
            src_ref=dst.at[1 - pipe, mine], dst_ref=dst.at[1 - pipe, mine],
            send_sem=send_sem.at[2 + k], recv_sem=recv_sem.at[2 + k],
            device_id=near, device_id_type=MESH,
        )
        copy.start()
        seconds.append(copy)
    for copy in firsts:
        copy.wait_send()
    for copy in seconds:
        copy.wait()
    for own in owns:
        own.wait()
    gains.wait()


def bring_weights(wqkv, wout, gain, cid):
    return pl.pallas_call(
        weights_kernel,
        out_shape=[
            jax.ShapeDtypeStruct((2,) + wqkv.shape[1:], wqkv.dtype),
            jax.ShapeDtypeStruct((2,) + wout.shape[1:], wout.dtype),
            jax.ShapeDtypeStruct((2,) + gain.shape, gain.dtype),
        ],
        in_specs=vmem(3),
        out_specs=vmem(3),
        scratch_shapes=[
            pltpu.SemaphoreType.DMA((5,)),
            pltpu.SemaphoreType.DMA((5,)),
            pltpu.SemaphoreType.DMA((2,)),
        ],
        compiler_params=params(collective_id=cid, has_side_effects=True),
    )(wqkv, wout, gain)


def total_kernel(dw0, dw1, dcls, dg0, dg1, dhead, loss, oqkv, oout, ocls, ogain, ohead, oloss,
                 b0, a0, s1, b1, a1, s2, b2, a2, b3, a3, b4, a4, res, x0, xs, xr, send_sem, recv_sem):
    pipe = lax.axis_index("pipe")
    dp = lax.axis_index("dp")
    inner = lax.axis_index("inner")
    core = lax.rem(dp, 2)
    y = dp // 2
    z_hi = inner // 2
    z_lo = lax.rem(inner, 2)
    rows, width = dw0.shape
    cols = width // 2
    partners = [
        {"dp": dp + 1 - 2 * core},
        {"pipe": 1 - pipe},
        {"dp": dp + 2 - 4 * y},
        {"inner": inner + 1 - 2 * z_lo},
        {"inner": inner + 2 - 4 * z_hi},
    ]
    started = []

    def send(k, src, dst, sem):
        copy = pltpu.make_async_remote_copy(
            src_ref=src, dst_ref=dst, send_sem=send_sem.at[sem], recv_sem=recv_sem.at[sem],
            device_id=partners[k], device_id_type=MESH,
        )
        copy.start()
        started.append(copy)
        return copy

    def part(bit, size):
        return pl.ds(pl.multiple_of(bit * size, size), size)

    def span(c):
        return pl.ds(c * cols, cols)

    nc = dcls.shape[0]
    x0[...] = jnp.zeros_like(x0)
    for k, gain in enumerate((dg0, dg1)):
        x0[k, :nc, :] = dcls[...]
        x0[k, nc : nc + 1, :] = gain[...]
        x0[k, nc + 1 : nc + 2, :] = dhead[...]
        x0[k, nc + 2 : nc + 3, :] = loss[...]
    enter(partners)
    half = rows // 2
    quarter = half // 2
    going = [
        [send(0, dw.at[part(1 - core, half), span(c)], b0.at[c, k], 10 * c + k) for k, dw in enumerate((dw0, dw1))]
        for c in range(2)
    ]
    small = send(0, x0, xr.at[pl.ds(0, 2)], 20)
    mine = part(core, half)
    hops = []
    for c in range(2):
        for copy in going[c]:
            copy.wait_recv()
        for k, dw in enumerate((dw0, dw1)):
            a0[c, k] = dw[mine, span(c)] + b0[c, k]
        if c == 0:
            s1[0] = a0[0, 1 - pipe].astype(s1.dtype)
            hops.append(send(1, s1.at[0], b1.at[0], 2))
        else:
            for k in range(2):
                s1[1, pl.ds(k * quarter, quarter)] = a0[1, k, part(1 - y, quarter)].astype(s1.dtype)
            hops.append(send(2, s1.at[1], b1.at[1], 12))
    small.wait_recv()
    xs[pl.ds(0, 2)] = x0[...] + xr[pl.ds(0, 2)]
    small = send(1, xs.at[1 - pipe], xr.at[2], 21)
    hops[0].wait_recv()
    a1[0] = a0[0, pipe] + b1[0].astype(F32)
    s2[0] = a1[0, part(1 - y, quarter)].astype(s2.dtype)
    hops[0] = send(2, s2.at[0], b2.at[0], 3)
    hops[1].wait_recv()
    for k in range(2):
        there = pl.ds(k * quarter, quarter)
        a1[1, there] = a0[1, k, part(y, quarter)] + b1[1, there].astype(F32)
    s2[1] = a1[1, part(1 - pipe, quarter)].astype(s2.dtype)
    hops[1] = send(1, s2.at[1], b2.at[1], 13)
    small.wait_recv()
    xs[2] = xs[pipe] + xr[2]
    small = send(2, xs.at[2], xr.at[3], 22)
    source, bits, size = a1, (y, pipe), quarter
    for k, nxt, acc, got in ((3, z_lo, a2, b2), (4, z_hi, a3, b3), (5, None, a4, b4)):
        for c in range(2):
            hops[c].wait_recv()
            acc[c] = source[c, part(bits[c], size)] + got[c].astype(F32)
            if nxt is not None:
                smaller = size // 2
                landing = b3 if k == 3 else b4
                hops[c] = send(k, acc.at[c, part(1 - nxt, smaller)], landing.at[c], 10 * c + k + 1)
        small.wait_recv()
        xs[k] = xs[k - 1] + xr[k]
        if nxt is not None:
            small = send(k, xs.at[k], xr.at[k + 1], 20 + k)
            source, bits, size = acc, (nxt, nxt), size // 2
    start = core * half + y * quarter + z_lo * (quarter // 2) + z_hi * size
    gathers = [None, None]
    for n, (k, bit) in enumerate(((4, z_hi), (3, z_lo), (2, y), (0, core))):
        here = pl.ds(pl.multiple_of(start, size), size)
        for c in range(2):
            if n == 0:
                res[c, here] = a4[c]
            else:
                gathers[c].wait_recv()
            gathers[c] = send(k, res.at[c, here], res.at[c, here], 10 * c + 6 + n)
        start = start - bit * size
        size *= 2
    last = xs[5]
    ocls[...] = last[:nc]
    ogain[...] = last[nc : nc + 1]
    ohead[...] = last[nc + 1 : nc + 2]
    oloss[...] = last[nc + 2 : nc + 3]
    for copy in gathers:
        copy.wait_recv()
    first = oqkv.shape[2] - cols
    oqkv[0, :, :cols] = res[0]
    oqkv[0, :, cols:] = res[1, :, :first]
    oout[0] = res[1, :, first:]
    for copy in started:
        copy.wait_send()


def total_scratch(rows, width, classes):
    half, cols = rows // 2, width // 2
    extra = (-(-(classes + 3) // 8) * 8, width // 4)
    return [
        pltpu.VMEM((2, 2, half, cols), F32),
        pltpu.VMEM((2, 2, half, cols), F32),
        pltpu.VMEM((2, half, cols), BF16),
        pltpu.VMEM((2, half, cols), BF16),
        pltpu.VMEM((2, half, cols), F32),
        pltpu.VMEM((2, half // 2, cols), BF16),
        pltpu.VMEM((2, half // 2, cols), BF16),
        pltpu.VMEM((2, half // 2, cols), F32),
        pltpu.VMEM((2, half // 4, cols), F32),
        pltpu.VMEM((2, half // 4, cols), F32),
        pltpu.VMEM((2, half // 8, cols), F32),
        pltpu.VMEM((2, half // 8, cols), F32),
        pltpu.VMEM((2, rows, cols), F32),
        pltpu.VMEM((2,) + extra, F32),
        pltpu.VMEM((6,) + extra, F32),
        pltpu.VMEM((6,) + extra, F32),
        pltpu.SemaphoreType.DMA((25,)),
        pltpu.SemaphoreType.DMA((25,)),
    ]


def total_outs(rows, width, classes):
    d = width // 4
    shapes = [(1, rows, 3 * d), (1, rows, d), (classes, d), (1, d), (1, d), (1, d)]
    return [jax.ShapeDtypeStruct(s, F32) for s in shapes]


def total(cid, *args):
    rows, width = args[0].shape
    classes = args[2].shape[0]
    return pl.pallas_call(
        total_kernel,
        out_shape=total_outs(rows, width, classes),
        in_specs=vmem(len(args)),
        out_specs=vmem(6),
        scratch_shapes=total_scratch(rows, width, classes),
        compiler_params=params(collective_id=cid, has_side_effects=True),
    )(*args)


def local(fn, outs, scalars, *args):
    specs = vmem(len(args))
    for k in scalars:
        specs[k] = pl.BlockSpec(memory_space=pltpu.SMEM)
    return pl.pallas_call(
        fn,
        out_shape=[jax.ShapeDtypeStruct(s, t) for s, t in outs],
        in_specs=specs,
        out_specs=vmem(len(outs)),
        compiler_params=params(),
    )(*args)


def date_encoding(date_days, width):
    channel = jnp.arange(width)
    frequency = jnp.exp((channel // 2 * 2).astype(F32) * (-math.log(10000.0) / width))
    phases = date_days.astype(F32)[:, :, None] * frequency
    return jnp.where(channel % 2 == 0, jnp.sin(phases), jnp.cos(phases))


def saved_shapes(rows, width):
    hq = HEADS * CLASSES
    f, b = F32, BF16
    return [((rows, width), b), ((rows, width), f), ((rows, width), f), ((rows, width), b),
            ((hq, rows), f), ((hq, rows), f), ((rows, width), b), ((5, CLASSES, width), f)]


def kept_shapes(kinds, per, width):
    srows = kinds * per
    f, b = F32, BF16
    return [((srows, width), f), ((srows, width), b), ((2, srows, width), f), ((2, srows, width), f),
            ((srows, width), b), ((kinds, HEADS * per, per), f), ((srows, width), b), ((srows, width), f),
            ((srows, 128), f)]


def grad_shapes(width):
    return [((width, 4 * width), F32), ((1, width), F32)]


def shards(pixels, date_days, clear_count, batch_slot, labels, class_tokens, section_gain,
           segment_probe_lookup_content, section_out, head_vec):
    tiles_dev, patches_dev, dates, width = pixels.shape
    inner_count = lax.axis_size("inner")
    kinds = CLASSES // inner_count
    total_tiles = tiles_dev * lax.axis_size("dp")
    tiles = tiles_dev // 2
    rows = tiles * patches_dev * dates
    batch_norm = 1.0 / (total_tiles // MICRO * PATCHES)
    w, wo, gains = bring_weights(segment_probe_lookup_content, section_out, section_gain, 0)
    enc = date_encoding(date_days, width)
    head = head_vec.reshape(1, width)
    per = inner_count * tiles * patches_dev
    exchanged = (inner_count, rows // inner_count, width)
    send, *saved = local(
        functools.partial(temporal_fwd, tiles),
        [(exchanged, BF16)] + saved_shapes(rows, width), (2,),
        pixels, enc, clear_count, class_tokens, gains, w, wo,
    )
    recv = swap(send, inner_count, False, 1)
    *kept, sums = local(
        functools.partial(spatial_fwd, kinds, tiles),
        kept_shapes(kinds, per, width) + [((per, 128), F32)], (),
        recv, gains, w, wo, head,
    )
    totals = swap(sums, inner_count, True, 2)
    back, dw1, dg1, dhead, loss = local(
        functools.partial(spatial_bwd, kinds, tiles, total_tiles, batch_norm),
        [(exchanged, BF16)] + grad_shapes(width) + [((1, width), F32)] * 2, (2,),
        totals, labels, batch_slot, gains, w, wo, head, *kept,
    )
    returned = swap(back, inner_count, False, 3)
    dw0, dg0, dcls = local(
        functools.partial(temporal_bwd, tiles),
        grad_shapes(width) + [((CLASSES, width), F32)], (),
        returned, pixels, enc, class_tokens, gains, w, wo, *saved,
    )
    gqkv, gout, gcls, ggain, ghead, gloss = total(4, dw0, dw1, dcls, dg0, dg1, dhead, loss)
    return gloss[0, :MICRO], gcls, ggain, gqkv, gout, ghead.reshape(width)


def solution(mesh):
    placed = (
        P("dp", "inner", None, None),
        P("dp", None),
        P("dp"),
        P("dp"),
        P("dp", None),
        P(),
        P("pipe", None),
        P("pipe", None, None),
        P("pipe", None, None),
        P(),
    )

    def body(*args):
        tiles_dev, patches_dev, dates, width = args[0].shape
        pairs = tiles_dev // 2 * patches_dev
        sizes = tuple(mesh.shape[a] for a in ("pipe", "dp", "inner"))
        fits = sizes == (2, 4, 4) and pairs % 8 == 0 and dates == CLASSES and width == 256
        return (shards if fits else shards_general)(*args)

    return jax.shard_map(
        body,
        mesh=mesh,
        in_specs=placed,
        out_specs=(P(), P(), P("pipe", None), P("pipe", None, None), P("pipe", None, None), P()),
        check_vma=False,
    )
```

```python
import functools
import math

import jax
import jax.numpy as jnp
from jax import lax
from jax.experimental import pallas as pl
from jax.experimental.pallas import tpu as pltpu
from jax.sharding import PartitionSpec as P

HEADS = 8
CLASSES = 16
PATCHES = 48
MICRO = 4


normalizer_sharpness = 10.0
logit_cap = 15.0
norm_eps = 1e-05
head_eps = 1e-06


def matmul_f32(left_side, right_side):
    return jnp.einsum(
        "...d,de->...e",
        left_side,
        right_side.astype(jnp.bfloat16),
        preferred_element_type=jnp.float32,
    )


def rms_norm(inputs, gain_vec):
    inverse_rms = lax.rsqrt(jnp.mean(inputs * inputs, axis=-1, keepdims=True) + norm_eps)
    return inputs * inverse_rms * gain_vec


def unit_heads(values):
    shaped = values.reshape(values.shape[:-1] + (HEADS, values.shape[-1] // HEADS))
    return shaped * lax.rsqrt(jnp.sum(shaped * shaped, axis=-1, keepdims=True) + head_eps)


def temporal(pixel_rows, date_days, counts, params):
    class_init, gain_vec, w_qkv, w_out = params
    batch_count, patches, dates_max, model_width = pixel_rows.shape
    classes = class_init.shape[0]
    band_channel = jnp.arange(model_width)
    frequency = jnp.exp(
        (band_channel // 2 * 2).astype(jnp.float32) * (-math.log(10000.0) / model_width)
    )
    phases = date_days.astype(jnp.float32)[:, :, None] * frequency
    encoding = jnp.where(band_channel % 2 == 0, jnp.sin(phases), jnp.cos(phases))
    date_rows = pixel_rows.astype(jnp.float32) + encoding[:, None]
    class_rows = jnp.broadcast_to(class_init, (batch_count, patches, classes, model_width))
    sequence = jnp.concatenate([class_rows, date_rows], axis=2)
    normed = rms_norm(sequence, gain_vec).astype(jnp.bfloat16)
    probe_entry_lines = unit_heads(matmul_f32(normed[:, :, :classes], w_qkv[:, :model_width]))
    lookup_entry_lines = unit_heads(matmul_f32(normed, w_qkv[:, model_width : 2 * model_width]))
    value_rows = matmul_f32(normed, w_qkv[:, 2 * model_width :]).astype(jnp.bfloat16)
    value_heads = value_rows.reshape(
        batch_count, patches, classes + dates_max, HEADS, model_width // HEADS
    )
    affinity_logit_grid = normalizer_sharpness * jnp.einsum(
        "ohbyv,ohsyv->ohybs", probe_entry_lines, lookup_entry_lines, precision=lax.Precision.HIGHEST
    )
    position = jnp.arange(classes + dates_max)
    key_mask = (
        (position[None, :] < classes) | (position[None, :] - classes < counts[:, None])
    ).astype(jnp.float32)
    raised = jnp.exp(affinity_logit_grid) * key_mask[:, None, None, None, :]
    weights = (raised / jnp.sum(raised, axis=-1, keepdims=True)).astype(jnp.bfloat16)
    attended = jnp.einsum(
        "bphqk,bpkhe->bpqhe", weights, value_heads, preferred_element_type=jnp.float32
    )
    attended = attended.reshape(batch_count, patches, classes, model_width).astype(jnp.bfloat16)
    updated = sequence[:, :, :classes] + matmul_f32(attended, w_out)
    return jnp.swapaxes(updated, 1, 2).astype(jnp.bfloat16)


def spatial(inputs, params):
    gain_vec, w_qkv, w_out, head_vec = params
    batch_count, groups, classes, patches, model_width = inputs.shape
    class_seq = (
        jnp.swapaxes(inputs, 1, 2)
        .reshape(batch_count, classes, groups * patches, model_width)
        .astype(jnp.float32)
    )
    normed = rms_norm(class_seq, gain_vec).astype(jnp.bfloat16)
    probe_entry_lines = unit_heads(matmul_f32(normed, w_qkv[:, :model_width]))
    lookup_entry_lines = unit_heads(matmul_f32(normed, w_qkv[:, model_width : 2 * model_width]))
    value_rows = matmul_f32(normed, w_qkv[:, 2 * model_width :]).astype(jnp.bfloat16)
    value_heads = value_rows.reshape(
        batch_count, classes, groups * patches, HEADS, model_width // HEADS
    )
    affinity_logit_grid = normalizer_sharpness * jnp.einsum(
        "wisbx,wiqbx->wibsq", probe_entry_lines, lookup_entry_lines, precision=lax.Precision.HIGHEST
    )
    raised = jnp.exp(affinity_logit_grid)
    weights = (raised / jnp.sum(raised, axis=-1, keepdims=True)).astype(jnp.bfloat16)
    attended = jnp.einsum(
        "bchqk,bckhe->bcqhe", weights, value_heads, preferred_element_type=jnp.float32
    )
    attended = attended.reshape(batch_count, classes, groups * patches, model_width).astype(
        jnp.bfloat16
    )
    hidden = class_seq + matmul_f32(attended, w_out)
    raw_logits = jnp.einsum("bcpd,d->bcp", hidden, head_vec, precision=lax.Precision.HIGHEST)
    logits = logit_cap * jnp.tanh(raw_logits / logit_cap)
    return logits.reshape(batch_count, classes, groups, patches)


def shards_general(
    pixels,
    date_days,
    clear_count,
    batch_slot,
    labels,
    class_tokens,
    section_gain,
    segment_probe_lookup_content,
    section_out,
    head_vec,
):
    tiles_dev = pixels.shape[0]
    patches_dev = pixels.shape[1]
    model_width = pixels.shape[3]
    inner_count = lax.axis_size("inner")
    classes_dev = CLASSES // inner_count
    total_tiles = tiles_dev * lax.axis_size("dp")
    my_group = lax.axis_index("inner")
    class_ids = my_group * classes_dev + jnp.arange(classes_dev, dtype=jnp.int32)
    batch_norm = 1.0 / (total_tiles // MICRO * PATCHES)
    gains, qkv_all, out_all = (
        lax.all_gather(section_gain, "pipe", axis=0, tiled=True),
        lax.all_gather(
            segment_probe_lookup_content.astype(jnp.float32), "pipe", axis=0, tiled=True
        ),
        lax.all_gather(section_out.astype(jnp.float32), "pipe", axis=0, tiled=True),
    )
    pipe_pos = lax.axis_index("pipe")
    half_tiles = tiles_dev // 2
    first_params = (class_tokens.astype(jnp.float32), gains[0], qkv_all[0], out_all[0])
    second_params = (gains[1], qkv_all[1], out_all[1], head_vec)
    fold_shape = (1, inner_count, classes_dev, patches_dev, model_width)
    first_gradients = jax.tree.map(jnp.zeros_like, first_params)
    grads_second = jax.tree.map(jnp.zeros_like, second_params)
    loss_vec = jnp.zeros((MICRO,), jnp.float32)
    for tile_step in range(half_tiles):
        start = pipe_pos * half_tiles + tile_step
        single_pixel = lax.dynamic_slice_in_dim(pixels, start, 1, 0)
        days_one = lax.dynamic_slice_in_dim(date_days, start, 1, 0)
        count_one = lax.dynamic_slice_in_dim(clear_count, start, 1, 0)
        label_one = lax.dynamic_slice_in_dim(labels, start, 1, 0)
        slot_one = lax.dynamic_slice_in_dim(batch_slot, start, 1, 0)
        encoded, pull_first = jax.vjp(
            lambda params: temporal(single_pixel, days_one, count_one, params), first_params
        )
        arrived = lax.all_to_all(
            encoded.reshape(fold_shape), "inner", split_axis=1, concat_axis=1, tiled=True
        )
        logits, pull_second = jax.vjp(spatial, arrived, second_params)
        exp_logits = jnp.exp(logits)
        class_total = lax.psum(jnp.sum(exp_logits, axis=1), "inner")
        label_rows = label_one.reshape(1, 1, inner_count, patches_dev)
        indicator_rows = (label_rows == class_ids[None, :, None, None]).astype(jnp.float32)
        dlogit = (exp_logits / class_total[:, None] - indicator_rows) / total_tiles
        grad_in, grad_two = pull_second(dlogit)
        returned = lax.all_to_all(grad_in, "inner", split_axis=1, concat_axis=1, tiled=True)
        (derivative_lone,) = pull_first(returned.reshape(encoded.shape))
        first_gradients = jax.tree.map(
            lambda total, extra: total + extra, first_gradients, derivative_lone
        )
        grads_second = jax.tree.map(lambda total, extra: total + extra, grads_second, grad_two)
        loss_term = jnp.sum(indicator_rows * (jnp.log(class_total)[:, None] - logits)) * batch_norm
        loss_vec = loss_vec + loss_term * (jnp.arange(MICRO) == slot_one[0]).astype(jnp.float32)
    stacked = (
        jnp.stack([first_gradients[1], grads_second[0]]),
        jnp.stack([first_gradients[2], grads_second[1]]),
        jnp.stack([first_gradients[3], grads_second[2]]),
        first_gradients[0],
        grads_second[3],
        loss_vec,
    )
    summed = lax.psum(
        (stacked[0], stacked[1], stacked[2], stacked[3], stacked[4], stacked[5]),
        ("pipe", "dp", "inner"),
    )
    gain_grad = lax.dynamic_slice_in_dim(summed[0], pipe_pos, 1, 0)
    qkv_grad = lax.dynamic_slice_in_dim(summed[1], pipe_pos, 1, 0)
    out_grad = lax.dynamic_slice_in_dim(summed[2], pipe_pos, 1, 0)
    return (summed[5], summed[3], gain_grad, qkv_grad, out_grad, summed[4])


F32 = jnp.float32
BF16 = jnp.bfloat16
VMEM_LIMIT = 56 * 2**20


def params(**kw):
    return pltpu.CompilerParams(vmem_limit_bytes=VMEM_LIMIT, **kw)


def vmem(count):
    return [pl.BlockSpec(memory_space=pltpu.VMEM)] * count


def mm(a, b, ca=1, cb=0):
    return lax.dot_general(a, b, (((ca,), (cb,)), ((), ())), preferred_element_type=F32)


def split(a):
    hi = a.astype(BF16)
    return hi, (a - hi.astype(F32)).astype(BF16)


def mm2(a, b, ca=1, cb=0):
    hi, lo = split(a)
    return mm(hi, b, ca, cb) + mm(lo, b, ca, cb)


def mm2r(a, b, ca=1, cb=0):
    hi, lo = split(b)
    return mm(a, hi, ca, cb) + mm(a, lo, ca, cb)


def mm3(a, b, ca=1, cb=0):
    ah, al = split(a)
    bh, bl = split(b)
    return mm(ah, bh, ca, cb) + (mm(ah, bl, ca, cb) + mm(al, bh, ca, cb))


def same_block(rows, cols, size):
    r = lax.broadcasted_iota(jnp.int32, (rows, cols), 0) // size
    c = lax.broadcasted_iota(jnp.int32, (rows, cols), 1) // size
    return (r == c).astype(F32)


def head_ones(width):
    return same_block(width, width, width // HEADS).astype(BF16)


def head_mask(width):
    h = lax.broadcasted_iota(jnp.int32, (HEADS, 1, width), 0)
    c = lax.broadcasted_iota(jnp.int32, (HEADS, 1, width), 2) // (width // HEADS)
    return (h == c).astype(F32)


def unit(x, ones):
    r = lax.rsqrt(mm2(x * x, ones) + head_eps)
    return x * r, r


def unit_back(dxn, xn, r, ones):
    return r * (dxn - xn * mm2(dxn * xn, ones))


def norm_scale(x):
    return lax.rsqrt(jnp.mean(x * x, axis=-1, keepdims=True) + norm_eps)


def rounded(x):
    return x.astype(BF16).astype(F32)


def expand_heads(x, hm):
    n, d = x.shape
    return (x[None] * hm).reshape(HEADS * n, d)


def fold_heads(x, hm):
    n = x.shape[0] // HEADS
    return jnp.sum(x.reshape(HEADS, n, x.shape[1]) * hm, axis=0)


def permutation(n, outer):
    inner = n // outer
    r = lax.broadcasted_iota(jnp.int32, (n, n), 0)
    c = lax.broadcasted_iota(jnp.int32, (n, n), 1)
    return (c == (r % inner) * outer + r // inner).astype(F32).astype(BF16)


def date_sequence(pix, enc):
    return (pix.astype(F32) + enc[:, None]).reshape(-1, pix.shape[-1])


def own_tiles(tiles):
    return pl.ds(lax.axis_index("pipe") * tiles, tiles)


def clear_mask(count_ref, tiles, rows, dates):
    lane = lax.broadcasted_iota(jnp.int32, (1, rows), 1)
    first = lax.axis_index("pipe") * tiles
    mask = jnp.zeros((1, rows), F32)
    for t in range(tiles):
        clear = (lane // (rows // tiles) == t) & (lane % dates < count_ref[first + t])
        mask = mask + clear.astype(F32)
    return mask


def temporal_fwd(tiles, pix_ref, enc_ref, count_ref, cls_ref, gain_ref, w_ref, wo_ref,
                 send_ref, nd_ref, kn_ref, rk_ref, v_ref, ad_ref, ac_ref, att_ref, cq_ref):
    d = pix_ref.shape[-1]
    dates = pix_ref.shape[2]
    classes = cls_ref.shape[0]
    gain = gain_ref[0]
    w_ref = w_ref.at[0]
    wo_ref = wo_ref.at[0]
    x = date_sequence(pix_ref[own_tiles(tiles)], enc_ref[own_tiles(tiles)])
    rows = x.shape[0]
    bps = rows // dates
    mask = clear_mask(count_ref, tiles, rows, dates)
    nd = (x * norm_scale(x) * gain).astype(BF16)
    nd_ref[...] = nd
    cls = cls_ref[...].astype(F32)
    nc = (cls * norm_scale(cls) * gain).astype(BF16)
    ones = head_ones(d)
    hm = head_mask(d)
    kv = mm(nd, w_ref[:, d:])
    qkvc = mm(nc, w_ref[...])
    kn, rk = unit(kv[:, :d], ones)
    kn_ref[...] = kn
    rk_ref[...] = rk
    v = kv[:, d:].astype(BF16)
    v_ref[...] = v
    qn, rq = unit(qkvc[:, :d], ones)
    kcn, rkc = unit(qkvc[:, d : 2 * d], ones)
    vc = qkvc[:, 2 * d :].astype(BF16)
    cq_ref[0] = qn
    cq_ref[1] = rq
    cq_ref[2] = kcn
    cq_ref[3] = rkc
    cq_ref[4] = vc.astype(F32)
    group = 128 // dates
    qe = expand_heads(qn, hm)
    kct = jnp.concatenate([kcn] * group, axis=0)
    ed = jnp.exp(normalizer_sharpness * mm3(qe, kn, 1, 1)) * mask
    ec = jnp.exp(normalizer_sharpness * mm3(qe, kct, 1, 1))
    seg = same_block(128, 128, dates).astype(BF16)
    sum_c = mm2(ec, seg)
    vct = jnp.concatenate([vc] * group, axis=0)
    bm = group_mask(group, dates)
    atts = []
    for g in range(bps // group):
        lanes = slice(g * 128, (g + 1) * 128)
        e = ed[:, lanes]
        den = mm2(e, seg) + sum_c
        ad = e / den
        ac = ec / den
        ad_ref[:, lanes] = ad
        ac_ref[:, lanes] = ac
        aexp = (jnp.concatenate([ad, ac], axis=1)[None] * bm).reshape(-1, 256).astype(BF16)
        vst = jnp.concatenate([v[lanes], vct], axis=0)
        o = mm(aexp, vst).reshape(group, HEADS, classes, d)
        atts.append(jnp.sum(o * hm[None], axis=1).reshape(group * classes, d))
    att = jnp.concatenate(atts, axis=0).astype(BF16)
    att_ref[...] = att
    upd = jnp.concatenate([cls] * bps, axis=0) + mm(att, wo_ref[...])
    send = mm(permutation(rows, classes), upd.astype(BF16)).astype(BF16)
    part = send_ref.shape[1]
    for k in range(send_ref.shape[0]):
        send_ref[k] = send[k * part : (k + 1) * part]


def group_mask(group, dates):
    g = lax.broadcasted_iota(jnp.int32, (group, 1, 256), 0)
    c = (lax.broadcasted_iota(jnp.int32, (group, 1, 256), 2) % 128) // dates
    return (g == c).astype(F32)


def temporal_bwd(tiles, back_ref, pix_ref, enc_ref, cls_ref, gain_ref, w_ref, wo_ref,
                 nd_ref, kn_ref, rk_ref, v_ref, ad_ref, ac_ref, att_ref, cq_ref,
                 dw_ref, dgain_ref, dcls_ref):
    d = pix_ref.shape[-1]
    dates = pix_ref.shape[2]
    classes = cls_ref.shape[0]
    gain = gain_ref[0]
    w_ref = w_ref.at[0]
    wo_ref = wo_ref.at[0]
    x = date_sequence(pix_ref[own_tiles(tiles)], enc_ref[own_tiles(tiles)])
    rows = x.shape[0]
    bps = rows // dates
    cls = cls_ref[...].astype(F32)
    inv_c = norm_scale(cls)
    nc = (cls * inv_c * gain).astype(BF16)
    nd = nd_ref[...]
    ones = head_ones(d)
    hm = head_mask(d)
    group = 128 // dates
    back = jnp.concatenate([back_ref[k] for k in range(back_ref.shape[0])], axis=0)
    du = mm(permutation(rows, rows // classes), back).astype(BF16)
    dw_ref[:, 3 * d :] = mm(att_ref[...], du, 0, 0)
    do = rounded(mm(du, wo_ref[...], 1, 1))
    qn = cq_ref[0]
    rq = cq_ref[1]
    kcn = cq_ref[2]
    rkc = cq_ref[3]
    vct = jnp.concatenate([cq_ref[4].astype(BF16)] * group, axis=0)
    kct = jnp.concatenate([kcn] * group, axis=0)
    qe = expand_heads(qn, hm)
    seg = same_block(128, 128, dates).astype(BF16)
    bm = group_mask(group, dates)
    qnt = jnp.concatenate([qn] * group, axis=0)
    rqt = jnp.concatenate([rq] * group, axis=0)
    rkct = jnp.concatenate([rkc] * group, axis=0)
    w = w_ref[...]
    wq, wk, wv = w[:, :d], w[:, d : 2 * d], w[:, 2 * d :]
    nct = jnp.concatenate([nc] * group, axis=0)
    dwq = jnp.zeros((d, d), F32)
    dwk = jnp.zeros((d, d), F32)
    dwv = jnp.zeros((d, d), F32)
    dnc = jnp.zeros((classes, d), F32)
    dgain = jnp.zeros((1, d), F32)
    xhat = x * norm_scale(x)
    for g in range(bps // group):
        lanes = slice(g * 128, (g + 1) * 128)
        ad = ad_ref[:, lanes]
        ac = ac_ref[:, lanes]
        a2 = jnp.concatenate([ad, ac], axis=1)
        aexp = (a2[None] * bm).reshape(-1, 256).astype(BF16)
        vst = jnp.concatenate([v_ref[lanes, :], vct], axis=0)
        doe = (do[lanes].reshape(group, 1, classes, d) * hm[None]).reshape(-1, d).astype(BF16)
        da = jnp.sum(mm(doe, vst, 1, 1).reshape(group, -1, 256) * bm, axis=0)
        da = rounded(da)
        dvst = mm(aexp, doe, 0, 0).astype(BF16)
        prod = da * a2
        dot = mm2(prod[:, :128] + prod[:, 128:], seg)
        ds = normalizer_sharpness * a2 * (da - jnp.concatenate([dot, dot], axis=1))
        kn = kn_ref[lanes, :]
        kst = jnp.concatenate([kn, kct], axis=0)
        dse = (ds[None] * bm).reshape(-1, 256)
        dqn = jnp.sum(mm3(dse, kst).reshape(group, HEADS, classes, d) * hm[None], axis=1)
        dqn = dqn.reshape(group * classes, d)
        dkst = mm3(ds, qe, 0, 0)
        dq = unit_back(dqn, qnt, rqt, ones)
        dk = unit_back(dkst[:128], kn, rk_ref[lanes, :], ones)
        dkc = unit_back(dkst[128:], kct, rkct, ones)
        ndg = nd[lanes]
        dwq += mm2r(nct, dq, 0, 0)
        dwk += mm2r(ndg, dk, 0, 0) + mm2r(nct, dkc, 0, 0)
        dwv += mm(ndg, dvst[:128], 0, 0) + mm(nct, dvst[128:], 0, 0)
        dn_k = rounded(mm2(jnp.concatenate([dk, dkc], axis=0), wk, 1, 1))
        dn = rounded(rounded(mm(dvst, wv, 1, 1)) + dn_k)
        dn_c = rounded(dn[128:] + rounded(mm2(dq, wq, 1, 1)))
        dgain += jnp.sum(dn[:128] * xhat[lanes], axis=0, keepdims=True)
        dnc += jnp.sum(dn_c.reshape(group, classes, d), axis=0)
    dw_ref[:, :d] = dwq
    dw_ref[:, d : 2 * d] = dwk
    dw_ref[:, 2 * d : 3 * d] = dwv
    dgain_ref[...] = dgain + jnp.sum(dnc * cls * inv_c, axis=0, keepdims=True)
    t = dnc * gain
    dcls = inv_c * (t - cls * (inv_c * inv_c * jnp.mean(t * cls, axis=-1, keepdims=True)))
    dcls_ref[...] = dcls + jnp.sum(du.astype(F32).reshape(bps, classes, d), axis=0)


def spatial_rows(recv_ref, kinds):
    sources, rows, d = recv_ref.shape
    n = rows // kinds
    blocks = [recv_ref[s].astype(F32) for s in range(sources)]
    return jnp.concatenate(
        [blocks[s][k * n : (k + 1) * n] for k in range(kinds) for s in range(sources)], axis=0
    )


def spatial_fwd(kinds, tiles, recv_ref, gain_ref, w_ref, wo_ref, head_ref,
                u_ref, n_ref, qk_ref, r_ref, v_ref, a_ref, o_ref, hid_ref, raw_ref, sum_ref):
    d = recv_ref.shape[-1]
    gain_ref = gain_ref.at[1]
    w_ref = w_ref.at[1]
    wo_ref = wo_ref.at[1]
    u = spatial_rows(recv_ref, kinds)
    u_ref[...] = u
    rows = u.shape[0]
    n = (u * norm_scale(u) * gain_ref[...]).astype(BF16)
    n_ref[...] = n
    ones = head_ones(d)
    hm = head_mask(d)
    qkv = mm(n, w_ref[...])
    qn, rq = unit(qkv[:, :d], ones)
    kn, rk = unit(qkv[:, d : 2 * d], ones)
    v = qkv[:, 2 * d :].astype(BF16)
    qk_ref[0] = qn
    qk_ref[1] = kn
    r_ref[0] = rq
    r_ref[1] = rk
    v_ref[...] = v
    per = rows // kinds
    patches = per // (recv_ref.shape[0] * tiles)
    ri = (lax.broadcasted_iota(jnp.int32, (per, per), 0) // patches) % tiles
    ci = (lax.broadcasted_iota(jnp.int32, (per, per), 1) // patches) % tiles
    tm = jnp.concatenate([(ri == ci).astype(F32)] * HEADS, axis=0)
    outs = []
    for k in range(kinds):
        rs = slice(k * per, (k + 1) * per)
        e = jnp.exp(normalizer_sharpness * mm3(expand_heads(qn[rs], hm), kn[rs], 1, 1)) * tm
        a = e / jnp.sum(e, axis=-1, keepdims=True)
        a_ref[k] = a
        outs.append(fold_heads(mm(a.astype(BF16), v[rs]), hm))
    o = jnp.concatenate(outs, axis=0).astype(BF16)
    o_ref[...] = o
    hid = u + mm(o, wo_ref[...])
    hid_ref[...] = hid
    raw = jnp.sum(hid * head_ref[...], axis=-1, keepdims=True)
    raw = jnp.broadcast_to(raw, (rows, 128))
    raw_ref[...] = raw
    ex = jnp.exp(logit_cap * jnp.tanh(raw / logit_cap))
    sum_ref[...] = jnp.sum(ex.reshape(kinds, per, 128), axis=0)


def patch_columns(label_ref, slot_ref, sources, tiles, lanes):
    first = lax.axis_index("pipe") * tiles
    count = label_ref.shape[1]
    patches = count // sources
    shape = (sources * tiles * patches, count)
    row = lax.broadcasted_iota(jnp.int32, shape, 0)
    col = lax.broadcasted_iota(jnp.int32, shape, 1)
    tile = (row // patches) % tiles
    here = col == (row // (patches * tiles)) * patches + row % patches
    slot_shape = (shape[0], lanes)
    slot_tile = (lax.broadcasted_iota(jnp.int32, slot_shape, 0) // patches) % tiles
    lane = lax.broadcasted_iota(jnp.int32, slot_shape, 1)
    labels = jnp.zeros(shape, F32)
    slots = jnp.zeros(slot_shape, F32)
    for t in range(tiles):
        values = label_ref[pl.ds(first + t, 1), :].astype(F32)
        labels = labels + jnp.where(here & (tile == t), values, 0.0)
        slots = slots + ((slot_tile == t) & (lane == slot_ref[first + t])).astype(F32)
    return jnp.broadcast_to(jnp.sum(labels, axis=-1, keepdims=True), slot_shape), slots


def spatial_bwd(kinds, tiles, total_tiles, batch_norm, tot_ref, label_ref, slot_ref, gain_ref, w_ref, wo_ref, head_ref,
                u_ref, n_ref, qk_ref, r_ref, v_ref, a_ref, o_ref, hid_ref, raw_ref,
                send_ref, dw_ref, dgain_ref, dhead_ref, loss_ref):
    d = u_ref.shape[-1]
    gain_ref = gain_ref.at[1]
    w_ref = w_ref.at[1]
    wo_ref = wo_ref.at[1]
    rows = u_ref.shape[0]
    per = rows // kinds
    sources = tot_ref.shape[0]
    total = jnp.sum(tot_ref[...], axis=0)
    total = jnp.concatenate([total] * kinds, axis=0)
    th = jnp.tanh(raw_ref[...] / logit_cap)
    logits = logit_cap * th
    label, slot = patch_columns(label_ref, slot_ref, sources, tiles, 128)
    kind = lax.broadcasted_iota(jnp.int32, (rows, 128), 0) // per + lax.axis_index("inner") * kinds
    ind = (jnp.concatenate([label] * kinds, axis=0) == kind.astype(F32)).astype(F32)
    slot = jnp.concatenate([slot] * kinds, axis=0)
    loss = jnp.sum(ind * (jnp.log(total) - logits) * slot, axis=0, keepdims=True) * batch_norm
    loss_ref[...] = jnp.concatenate([loss] * (d // 128), axis=1)
    draw = (jnp.exp(logits) / total - ind) / total_tiles * (1.0 - th * th)
    dr = jnp.concatenate([draw] * (d // 128), axis=1)
    head = head_ref[...]
    dhead_ref[...] = jnp.sum(dr * hid_ref[...], axis=0, keepdims=True)
    col = mm2r(o_ref[...], draw, 0, 0)
    dw_ref[:, 3 * d :] = jnp.concatenate([col] * (d // 128), axis=1) * head
    head_back = mm2(jnp.broadcast_to(head, (8, d)), wo_ref[...], 1, 1)[:1]
    do = rounded(dr * head_back)
    ones = head_ones(d)
    hm = head_mask(d)
    dqs, dks, dvs = [], [], []
    for k in range(kinds):
        rs = slice(k * per, (k + 1) * per)
        a = a_ref[k]
        doe = expand_heads(do[rs], hm).astype(BF16)
        da = rounded(mm(doe, v_ref[rs, :], 1, 1))
        dvs.append(mm(a.astype(BF16), doe, 0, 0))
        ds = normalizer_sharpness * a * (da - jnp.sum(da * a, axis=-1, keepdims=True))
        qn = qk_ref[0, rs, :]
        kn = qk_ref[1, rs, :]
        dqs.append(unit_back(fold_heads(mm3(ds, kn), hm), qn, r_ref[0, rs, :], ones))
        dks.append(unit_back(mm3(ds, expand_heads(qn, hm), 0, 0), kn, r_ref[1, rs, :], ones))
    dq = jnp.concatenate(dqs, axis=0)
    dk = jnp.concatenate(dks, axis=0)
    dv = jnp.concatenate(dvs, axis=0).astype(BF16)
    n = n_ref[...]
    dw_ref[:, :d] = mm2r(n, dq, 0, 0)
    dw_ref[:, d : 2 * d] = mm2r(n, dk, 0, 0)
    dw_ref[:, 2 * d : 3 * d] = mm(n, dv, 0, 0)
    w = w_ref[...]
    dn = rounded(rounded(mm(dv, w[:, 2 * d :], 1, 1)) + rounded(mm2(dk, w[:, d : 2 * d], 1, 1)))
    dn = rounded(dn + rounded(mm2(dq, w[:, :d], 1, 1)))
    u = u_ref[...]
    inv = norm_scale(u)
    dgain_ref[...] = jnp.sum(dn * u * inv, axis=0, keepdims=True)
    t = dn * gain_ref[...]
    du = dr * head + inv * (t - u * (inv * inv * jnp.mean(t * u, axis=-1, keepdims=True)))
    m = per // sources
    for s in range(sources):
        parts = [du[k * per + s * m : k * per + (s + 1) * m] for k in range(kinds)]
        send_ref[s] = jnp.concatenate(parts, axis=0).astype(BF16)


MESH = pl.DeviceIdType.MESH


def enter(devices):
    barrier = pltpu.get_barrier_semaphore()
    for dev in devices:
        pl.semaphore_signal(barrier, inc=1, device_id=dev, device_id_type=MESH)
    pl.semaphore_wait(barrier, len(devices))


def push(src, dst, sems, k, dev):
    copy = pltpu.make_async_remote_copy(
        src_ref=src, dst_ref=dst, send_sem=sems[0].at[k], recv_sem=sems[1].at[k],
        device_id=dev, device_id_type=MESH,
    )
    copy.start()
    return copy


def swap(src, dst, sems, first, whole):
    count = dst.shape[0]
    me = lax.axis_index("inner")
    copies = []
    for k in range(1, count):
        dev = lax.rem(me + k, count)
        block = src if whole else src.at[dev]
        copies.append(push(block, dst.at[me], sems, first + k - 1, {"inner": dev}))
    dst[me] = src[...] if whole else src[me]
    return copies


def bring_weights(wq_ref, wo_ref, g_ref, oq_ref, oo_ref, og_ref, sems, first):
    pipe = lax.axis_index("pipe")
    dp = lax.axis_index("dp")
    core = lax.rem(dp, 2)
    far = {"pipe": 1 - pipe}
    near = {"dp": dp + 1 - 2 * core}
    half = wq_ref.shape[1] // 2
    mine = pl.ds(pl.multiple_of(core * half, half), half)
    both = ((wq_ref, oq_ref), (wo_ref, oo_ref))
    started = [
        push(src.at[0, mine], dst.at[pipe, mine], sems, first + k, far) for k, (src, dst) in enumerate(both)
    ]
    gains = push(g_ref, og_ref.at[pipe], sems, first + 4, far)
    oq_ref[pipe] = wq_ref[0]
    oo_ref[pipe] = wo_ref[0]
    og_ref[pipe] = g_ref[...]
    passed = []
    for k, dst in enumerate((oq_ref, oo_ref)):
        started[k].wait_recv()
        there = dst.at[1 - pipe, mine]
        passed.append(push(there, there, sems, first + 2 + k, near))
    for copy in passed:
        copy.wait_recv()
    gains.wait_recv()
    return started + passed + [gains]


def total_partners():
    dp = lax.axis_index("dp")
    inner = lax.axis_index("inner")
    return [
        {"dp": dp + 1 - 2 * lax.rem(dp, 2)},
        {"pipe": 1 - lax.axis_index("pipe")},
        {"dp": dp + 2 - 4 * (dp // 2)},
        {"inner": inner + 1 - 2 * lax.rem(inner, 2)},
        {"inner": inner + 2 - 4 * (inner // 2)},
    ]


def first_hop(layer, dw, b0, sems):
    core = lax.rem(lax.axis_index("dp"), 2)
    rows, width = dw.shape
    half, cols = rows // 2, width // 2
    there = pl.ds(pl.multiple_of((1 - core) * half, half), half)
    return [
        push(dw.at[there, pl.ds(c * cols, cols)], b0.at[c, layer], sems, 10 * c + layer, total_partners()[0])
        for c in range(2)
    ]


def total(early, dw0, dw1, dcls, dg0, dg1, dhead, loss, res, osmall,
          b0, a0, s1, b1, a1, s2, b2, a2, b3, a3, b4, a4, x0, xs, xr, sems):
    pipe = lax.axis_index("pipe")
    dp = lax.axis_index("dp")
    inner = lax.axis_index("inner")
    core = lax.rem(dp, 2)
    y = dp // 2
    z_hi = inner // 2
    z_lo = lax.rem(inner, 2)
    rows, width = dw0.shape
    cols = width // 2
    partners = total_partners()
    started = []

    def send(k, src, dst, sem):
        started.append(push(src, dst, sems, sem, partners[k]))
        return started[-1]

    def part(bit, size):
        return pl.ds(pl.multiple_of(bit * size, size), size)

    def span(c):
        return pl.ds(c * cols, cols)

    nc = dcls.shape[0]
    x0[...] = jnp.zeros_like(x0)
    for k, gain in enumerate((dg0, dg1)):
        x0[k, :nc, :] = dcls[...]
        x0[k, nc : nc + 1, :] = gain[...]
        x0[k, nc + 1 : nc + 2, :] = dhead[...]
        x0[k, nc + 2 : nc + 3, :] = loss[...]
    half = rows // 2
    quarter = half // 2
    late = first_hop(0, dw0, b0, sems)
    started += early + late
    going = list(zip(late, early))
    small = send(0, x0, xr.at[pl.ds(0, 2)], 20)
    mine = part(core, half)
    hops = []
    for c in range(2):
        for copy in going[c]:
            copy.wait_recv()
        for k, dw in enumerate((dw0, dw1)):
            a0[c, k] = dw[mine, span(c)] + b0[c, k]
        if c == 0:
            s1[0] = a0[0, 1 - pipe].astype(s1.dtype)
            hops.append(send(1, s1.at[0], b1.at[0], 2))
        else:
            for k in range(2):
                s1[1, pl.ds(k * quarter, quarter)] = a0[1, k, part(1 - y, quarter)].astype(s1.dtype)
            hops.append(send(2, s1.at[1], b1.at[1], 12))
    small.wait_recv()
    xs[pl.ds(0, 2)] = x0[...] + xr[pl.ds(0, 2)]
    small = send(1, xs.at[1 - pipe], xr.at[2], 21)
    hops[0].wait_recv()
    a1[0] = a0[0, pipe] + b1[0].astype(F32)
    s2[0] = a1[0, part(1 - y, quarter)].astype(s2.dtype)
    hops[0] = send(2, s2.at[0], b2.at[0], 3)
    hops[1].wait_recv()
    for k in range(2):
        there = pl.ds(k * quarter, quarter)
        a1[1, there] = a0[1, k, part(y, quarter)] + b1[1, there].astype(F32)
    s2[1] = a1[1, part(1 - pipe, quarter)].astype(s2.dtype)
    hops[1] = send(1, s2.at[1], b2.at[1], 13)
    small.wait_recv()
    xs[2] = xs[pipe] + xr[2]
    small = send(2, xs.at[2], xr.at[3], 22)
    source, bits, size = a1, (y, pipe), quarter
    for k, nxt, acc, got in ((3, z_lo, a2, b2), (4, z_hi, a3, b3), (5, None, a4, b4)):
        for c in range(2):
            hops[c].wait_recv()
            acc[c] = source[c, part(bits[c], size)] + got[c].astype(F32)
            if nxt is not None:
                smaller = size // 2
                landing = b3 if k == 3 else b4
                hops[c] = send(k, acc.at[c, part(1 - nxt, smaller)], landing.at[c], 10 * c + k + 1)
        small.wait_recv()
        xs[k] = xs[k - 1] + xr[k]
        if nxt is not None:
            small = send(k, xs.at[k], xr.at[k + 1], 20 + k)
            source, bits, size = acc, (nxt, nxt), size // 2
    start = core * half + y * quarter + z_lo * (quarter // 2) + z_hi * size
    gathers = [None, None]
    for n, (k, bit) in enumerate(((4, z_hi), (3, z_lo), (2, y), (0, core))):
        here = pl.ds(pl.multiple_of(start, size), size)
        for c in range(2):
            if n == 0:
                res[c, here] = a4[c]
            else:
                gathers[c].wait_recv()
            gathers[c] = send(k, res.at[c, here], res.at[c, here], 10 * c + 6 + n)
        start = start - bit * size
        size *= 2
    osmall[...] = xs[5]
    for copy in gathers:
        copy.wait_recv()
    for copy in started:
        copy.wait_send()


def finish(res, small, oqkv, oout, ocls, ogain, ohead, oloss):
    cols = res.shape[2]
    nc = ocls.shape[0]
    first = oqkv.shape[2] - cols
    oqkv[0, :, :cols] = res[0]
    oqkv[0, :, cols:] = res[1, :, :first]
    oout[0] = res[1, :, first:]
    ocls[...] = small[:nc, :]
    ogain[...] = small[nc : nc + 1, :]
    ohead[...] = small[nc + 1 : nc + 2, :]
    oloss[...] = small[nc + 2 : nc + 3, : oloss.shape[1]]


def small_shape(classes, width):
    return (-(-(classes + 3) // 8) * 8, width)


def total_scratch(rows, width, classes):
    half, cols = rows // 2, width // 2
    extra = small_shape(classes, width // 4)
    return [
        pltpu.VMEM((2, 2, half, cols), F32),
        pltpu.VMEM((2, 2, half, cols), F32),
        pltpu.VMEM((2, half, cols), BF16),
        pltpu.VMEM((2, half, cols), BF16),
        pltpu.VMEM((2, half, cols), F32),
        pltpu.VMEM((2, half // 2, cols), BF16),
        pltpu.VMEM((2, half // 2, cols), BF16),
        pltpu.VMEM((2, half // 2, cols), F32),
        pltpu.VMEM((2, half // 4, cols), F32),
        pltpu.VMEM((2, half // 4, cols), F32),
        pltpu.VMEM((2, half // 8, cols), F32),
        pltpu.VMEM((2, half // 8, cols), F32),
        pltpu.VMEM((2,) + extra, F32),
        pltpu.VMEM((6,) + extra, F32),
        pltpu.VMEM((6,) + extra, F32),
    ]


def local(fn, outs, scalars, *args):
    specs = vmem(len(args))
    for k in scalars:
        specs[k] = pl.BlockSpec(memory_space=pltpu.SMEM)
    return pl.pallas_call(
        fn,
        out_shape=[jax.ShapeDtypeStruct(s, t) for s, t in outs],
        in_specs=specs,
        out_specs=vmem(len(outs)),
        compiler_params=params(),
    )(*args)


def date_encoding(date_days, width):
    channel = jnp.arange(width)
    frequency = jnp.exp((channel // 2 * 2).astype(F32) * (-math.log(10000.0) / width))
    phases = date_days.astype(F32)[:, :, None] * frequency
    return jnp.where(channel % 2 == 0, jnp.sin(phases), jnp.cos(phases))


def saved_shapes(rows, width):
    hq = HEADS * CLASSES
    f, b = F32, BF16
    return [((rows, width), b), ((rows, width), f), ((rows, width), f), ((rows, width), b),
            ((hq, rows), f), ((hq, rows), f), ((rows, width), b), ((5, CLASSES, width), f)]


def kept_shapes(kinds, per, width):
    srows = kinds * per
    f, b = F32, BF16
    return [((srows, width), f), ((srows, width), b), ((2, srows, width), f), ((2, srows, width), f),
            ((srows, width), b), ((kinds, HEADS * per, per), f), ((srows, width), b), ((srows, width), f),
            ((srows, 128), f)]


def grad_shapes(width):
    return [((width, 4 * width), F32), ((1, width), F32)]


def everything(tiles, kinds, total_tiles, batch_norm,
               wq_own, wo_own, g_own, pix_ref, enc_ref, count_ref, slot_ref, label_ref, cls_ref, head_ref,
               res_ref, small_ref, w_ref, wo_ref, g_ref, *refs):
    refs = list(refs)

    def take(count):
        taken, refs[:count] = refs[:count], []
        return taken

    send_ref, recv_ref, back_ref, returned_ref, sums_ref, totals_ref = take(6)
    saved = take(8)
    kept = take(9)
    dw0, dg0, dw1, dg1, dcls, dhead, loss = take(7)
    parts = take(15)
    sems = take(2)
    inner = lax.axis_index("inner")
    count = recv_ref.shape[0]
    along = total_partners()
    enter(along[:3] + [{"inner": lax.rem(inner + k, count)} for k in range(1, count)])
    started = bring_weights(wq_own, wo_own, g_own, w_ref, wo_ref, g_ref, sems, 25)
    temporal_fwd(tiles, pix_ref, enc_ref, count_ref, cls_ref, g_ref, w_ref, wo_ref, send_ref, *saved)
    copies = swap(send_ref, recv_ref, sems, 30, False)
    for copy in copies:
        copy.wait_recv()
    started += copies
    spatial_fwd(kinds, tiles, recv_ref, g_ref, w_ref, wo_ref, head_ref, *kept, sums_ref)
    copies = swap(sums_ref, totals_ref, sems, 30 + count, True)
    for copy in copies:
        copy.wait_recv()
    started += copies
    spatial_bwd(kinds, tiles, total_tiles, batch_norm, totals_ref, label_ref, slot_ref,
                g_ref, w_ref, wo_ref, head_ref, *kept, back_ref, dw1, dg1, dhead, loss)
    copies = swap(back_ref, returned_ref, sems, 30 + 2 * count, False)
    early = first_hop(1, dw1, parts[0], sems)
    for copy in copies:
        copy.wait_recv()
    started += copies
    temporal_bwd(tiles, returned_ref, pix_ref, enc_ref, cls_ref, g_ref, w_ref, wo_ref, *saved, dw0, dg0, dcls)
    total(early, dw0, dw1, dcls, dg0, dg1, dhead, loss, res_ref, small_ref, *parts, sems)
    for copy in started:
        copy.wait_send()


def shards(pixels, date_days, clear_count, batch_slot, labels, class_tokens, section_gain,
           segment_probe_lookup_content, section_out, head_vec):
    tiles_dev, patches_dev, dates, width = pixels.shape
    inner_count = lax.axis_size("inner")
    kinds = CLASSES // inner_count
    total_tiles = tiles_dev * lax.axis_size("dp")
    tiles = tiles_dev // 2
    rows = tiles * patches_dev * dates
    batch_norm = 1.0 / (total_tiles // MICRO * PATCHES)
    enc = date_encoding(date_days, width)
    head = head_vec.reshape(1, width)
    per = inner_count * tiles * patches_dev
    exchanged = ((inner_count, rows // inner_count, width), BF16)
    shapes = [
        ((2,) + segment_probe_lookup_content.shape[1:], BF16),
        ((2,) + section_out.shape[1:], BF16),
        ((2,) + section_gain.shape, F32),
        exchanged, exchanged, exchanged, exchanged,
        ((per, 128), F32), ((inner_count, per, 128), F32),
    ]
    shapes += saved_shapes(rows, width) + kept_shapes(kinds, per, width) + grad_shapes(width) * 2
    shapes += [((CLASSES, width), F32), ((1, width), F32), ((1, width), F32)]
    specs = vmem(10)
    specs[5] = specs[6] = pl.BlockSpec(memory_space=pltpu.SMEM)
    sems = 30 + 3 * inner_count
    grads, small = pl.pallas_call(
        functools.partial(everything, tiles, kinds, total_tiles, batch_norm),
        out_shape=[
            jax.ShapeDtypeStruct((2, width, 2 * width), F32),
            jax.ShapeDtypeStruct(small_shape(CLASSES, width), F32),
        ],
        in_specs=specs,
        out_specs=vmem(2),
        scratch_shapes=[pltpu.VMEM(s, t) for s, t in shapes]
        + total_scratch(width, 4 * width, CLASSES)
        + [pltpu.SemaphoreType.DMA((sems,))] * 2,
        compiler_params=params(collective_id=0, has_side_effects=True),
    )(segment_probe_lookup_content, section_out, section_gain, pixels, enc, clear_count, batch_slot,
      labels, class_tokens, head)
    gqkv, gout, gcls, ggain, ghead, gloss = local(
        finish,
        [((1, width, 3 * width), F32), ((1, width, width), F32), ((CLASSES, width), F32), ((1, width), F32),
         ((1, width), F32), ((1, MICRO), F32)], (),
        grads, small,
    )
    return gloss.reshape(MICRO), gcls, ggain, gqkv, gout, ghead.reshape(width)


def solution(mesh):
    placed = (
        P("dp", "inner", None, None),
        P("dp", None),
        P("dp"),
        P("dp"),
        P("dp", None),
        P(),
        P("pipe", None),
        P("pipe", None, None),
        P("pipe", None, None),
        P(),
    )

    def body(*args):
        tiles_dev, patches_dev, dates, width = args[0].shape
        pairs = tiles_dev // 2 * patches_dev
        sizes = tuple(mesh.shape[a] for a in ("pipe", "dp", "inner"))
        fits = sizes == (2, 4, 4) and pairs % 8 == 0 and dates == CLASSES and width == 256
        return (shards if fits else shards_general)(*args)

    return jax.shard_map(
        body,
        mesh=mesh,
        in_specs=placed,
        out_specs=(P(), P(), P("pipe", None), P("pipe", None, None), P("pipe", None, None), P()),
        check_vma=False,
    )
```

```python
import functools
import math

import jax
import jax.numpy as jnp
from jax import lax
from jax.experimental import pallas as pl
from jax.experimental.pallas import tpu as pltpu
from jax.sharding import PartitionSpec as P

HEADS = 8
CLASSES = 16
PATCHES = 48
MICRO = 4


normalizer_sharpness = 10.0
logit_cap = 15.0
norm_eps = 1e-05
head_eps = 1e-06


def matmul_f32(left_side, right_side):
    return jnp.einsum(
        "...d,de->...e",
        left_side,
        right_side.astype(jnp.bfloat16),
        preferred_element_type=jnp.float32,
    )


def rms_norm(inputs, gain_vec):
    inverse_rms = lax.rsqrt(jnp.mean(inputs * inputs, axis=-1, keepdims=True) + norm_eps)
    return inputs * inverse_rms * gain_vec


def unit_heads(values):
    shaped = values.reshape(values.shape[:-1] + (HEADS, values.shape[-1] // HEADS))
    return shaped * lax.rsqrt(jnp.sum(shaped * shaped, axis=-1, keepdims=True) + head_eps)


def temporal(pixel_rows, date_days, counts, params):
    class_init, gain_vec, w_qkv, w_out = params
    batch_count, patches, dates_max, model_width = pixel_rows.shape
    classes = class_init.shape[0]
    band_channel = jnp.arange(model_width)
    frequency = jnp.exp(
        (band_channel // 2 * 2).astype(jnp.float32) * (-math.log(10000.0) / model_width)
    )
    phases = date_days.astype(jnp.float32)[:, :, None] * frequency
    encoding = jnp.where(band_channel % 2 == 0, jnp.sin(phases), jnp.cos(phases))
    date_rows = pixel_rows.astype(jnp.float32) + encoding[:, None]
    class_rows = jnp.broadcast_to(class_init, (batch_count, patches, classes, model_width))
    sequence = jnp.concatenate([class_rows, date_rows], axis=2)
    normed = rms_norm(sequence, gain_vec).astype(jnp.bfloat16)
    probe_entry_lines = unit_heads(matmul_f32(normed[:, :, :classes], w_qkv[:, :model_width]))
    lookup_entry_lines = unit_heads(matmul_f32(normed, w_qkv[:, model_width : 2 * model_width]))
    value_rows = matmul_f32(normed, w_qkv[:, 2 * model_width :]).astype(jnp.bfloat16)
    value_heads = value_rows.reshape(
        batch_count, patches, classes + dates_max, HEADS, model_width // HEADS
    )
    affinity_logit_grid = normalizer_sharpness * jnp.einsum(
        "ohbyv,ohsyv->ohybs", probe_entry_lines, lookup_entry_lines, precision=lax.Precision.HIGHEST
    )
    position = jnp.arange(classes + dates_max)
    key_mask = (
        (position[None, :] < classes) | (position[None, :] - classes < counts[:, None])
    ).astype(jnp.float32)
    raised = jnp.exp(affinity_logit_grid) * key_mask[:, None, None, None, :]
    weights = (raised / jnp.sum(raised, axis=-1, keepdims=True)).astype(jnp.bfloat16)
    attended = jnp.einsum(
        "bphqk,bpkhe->bpqhe", weights, value_heads, preferred_element_type=jnp.float32
    )
    attended = attended.reshape(batch_count, patches, classes, model_width).astype(jnp.bfloat16)
    updated = sequence[:, :, :classes] + matmul_f32(attended, w_out)
    return jnp.swapaxes(updated, 1, 2).astype(jnp.bfloat16)


def spatial(inputs, params):
    gain_vec, w_qkv, w_out, head_vec = params
    batch_count, groups, classes, patches, model_width = inputs.shape
    class_seq = (
        jnp.swapaxes(inputs, 1, 2)
        .reshape(batch_count, classes, groups * patches, model_width)
        .astype(jnp.float32)
    )
    normed = rms_norm(class_seq, gain_vec).astype(jnp.bfloat16)
    probe_entry_lines = unit_heads(matmul_f32(normed, w_qkv[:, :model_width]))
    lookup_entry_lines = unit_heads(matmul_f32(normed, w_qkv[:, model_width : 2 * model_width]))
    value_rows = matmul_f32(normed, w_qkv[:, 2 * model_width :]).astype(jnp.bfloat16)
    value_heads = value_rows.reshape(
        batch_count, classes, groups * patches, HEADS, model_width // HEADS
    )
    affinity_logit_grid = normalizer_sharpness * jnp.einsum(
        "wisbx,wiqbx->wibsq", probe_entry_lines, lookup_entry_lines, precision=lax.Precision.HIGHEST
    )
    raised = jnp.exp(affinity_logit_grid)
    weights = (raised / jnp.sum(raised, axis=-1, keepdims=True)).astype(jnp.bfloat16)
    attended = jnp.einsum(
        "bchqk,bckhe->bcqhe", weights, value_heads, preferred_element_type=jnp.float32
    )
    attended = attended.reshape(batch_count, classes, groups * patches, model_width).astype(
        jnp.bfloat16
    )
    hidden = class_seq + matmul_f32(attended, w_out)
    raw_logits = jnp.einsum("bcpd,d->bcp", hidden, head_vec, precision=lax.Precision.HIGHEST)
    logits = logit_cap * jnp.tanh(raw_logits / logit_cap)
    return logits.reshape(batch_count, classes, groups, patches)


def shards_general(
    pixels,
    date_days,
    clear_count,
    batch_slot,
    labels,
    class_tokens,
    section_gain,
    segment_probe_lookup_content,
    section_out,
    head_vec,
):
    tiles_dev = pixels.shape[0]
    patches_dev = pixels.shape[1]
    model_width = pixels.shape[3]
    inner_count = lax.axis_size("inner")
    classes_dev = CLASSES // inner_count
    total_tiles = tiles_dev * lax.axis_size("dp")
    my_group = lax.axis_index("inner")
    class_ids = my_group * classes_dev + jnp.arange(classes_dev, dtype=jnp.int32)
    batch_norm = 1.0 / (total_tiles // MICRO * PATCHES)
    gains, qkv_all, out_all = (
        lax.all_gather(section_gain, "pipe", axis=0, tiled=True),
        lax.all_gather(
            segment_probe_lookup_content.astype(jnp.float32), "pipe", axis=0, tiled=True
        ),
        lax.all_gather(section_out.astype(jnp.float32), "pipe", axis=0, tiled=True),
    )
    pipe_pos = lax.axis_index("pipe")
    half_tiles = tiles_dev // 2
    first_params = (class_tokens.astype(jnp.float32), gains[0], qkv_all[0], out_all[0])
    second_params = (gains[1], qkv_all[1], out_all[1], head_vec)
    fold_shape = (1, inner_count, classes_dev, patches_dev, model_width)
    first_gradients = jax.tree.map(jnp.zeros_like, first_params)
    grads_second = jax.tree.map(jnp.zeros_like, second_params)
    loss_vec = jnp.zeros((MICRO,), jnp.float32)
    for tile_step in range(half_tiles):
        start = pipe_pos * half_tiles + tile_step
        single_pixel = lax.dynamic_slice_in_dim(pixels, start, 1, 0)
        days_one = lax.dynamic_slice_in_dim(date_days, start, 1, 0)
        count_one = lax.dynamic_slice_in_dim(clear_count, start, 1, 0)
        label_one = lax.dynamic_slice_in_dim(labels, start, 1, 0)
        slot_one = lax.dynamic_slice_in_dim(batch_slot, start, 1, 0)
        encoded, pull_first = jax.vjp(
            lambda params: temporal(single_pixel, days_one, count_one, params), first_params
        )
        arrived = lax.all_to_all(
            encoded.reshape(fold_shape), "inner", split_axis=1, concat_axis=1, tiled=True
        )
        logits, pull_second = jax.vjp(spatial, arrived, second_params)
        exp_logits = jnp.exp(logits)
        class_total = lax.psum(jnp.sum(exp_logits, axis=1), "inner")
        label_rows = label_one.reshape(1, 1, inner_count, patches_dev)
        indicator_rows = (label_rows == class_ids[None, :, None, None]).astype(jnp.float32)
        dlogit = (exp_logits / class_total[:, None] - indicator_rows) / total_tiles
        grad_in, grad_two = pull_second(dlogit)
        returned = lax.all_to_all(grad_in, "inner", split_axis=1, concat_axis=1, tiled=True)
        (derivative_lone,) = pull_first(returned.reshape(encoded.shape))
        first_gradients = jax.tree.map(
            lambda total, extra: total + extra, first_gradients, derivative_lone
        )
        grads_second = jax.tree.map(lambda total, extra: total + extra, grads_second, grad_two)
        loss_term = jnp.sum(indicator_rows * (jnp.log(class_total)[:, None] - logits)) * batch_norm
        loss_vec = loss_vec + loss_term * (jnp.arange(MICRO) == slot_one[0]).astype(jnp.float32)
    stacked = (
        jnp.stack([first_gradients[1], grads_second[0]]),
        jnp.stack([first_gradients[2], grads_second[1]]),
        jnp.stack([first_gradients[3], grads_second[2]]),
        first_gradients[0],
        grads_second[3],
        loss_vec,
    )
    summed = lax.psum(
        (stacked[0], stacked[1], stacked[2], stacked[3], stacked[4], stacked[5]),
        ("pipe", "dp", "inner"),
    )
    gain_grad = lax.dynamic_slice_in_dim(summed[0], pipe_pos, 1, 0)
    qkv_grad = lax.dynamic_slice_in_dim(summed[1], pipe_pos, 1, 0)
    out_grad = lax.dynamic_slice_in_dim(summed[2], pipe_pos, 1, 0)
    return (summed[5], summed[3], gain_grad, qkv_grad, out_grad, summed[4])


F32 = jnp.float32
BF16 = jnp.bfloat16
VMEM_LIMIT = 56 * 2**20


def params(**kw):
    return pltpu.CompilerParams(vmem_limit_bytes=VMEM_LIMIT, **kw)


def vmem(count):
    return [pl.BlockSpec(memory_space=pltpu.VMEM)] * count


def mm(a, b, ca=1, cb=0):
    return lax.dot_general(a, b, (((ca,), (cb,)), ((), ())), preferred_element_type=F32)


def split(a):
    hi = a.astype(BF16)
    return hi, (a - hi.astype(F32)).astype(BF16)


def mm2(a, b, ca=1, cb=0):
    hi, lo = split(a)
    return mm(hi, b, ca, cb) + mm(lo, b, ca, cb)


def mm2r(a, b, ca=1, cb=0):
    hi, lo = split(b)
    return mm(a, hi, ca, cb) + mm(a, lo, ca, cb)


def mm3(a, b, ca=1, cb=0):
    ah, al = split(a)
    bh, bl = split(b)
    return mm(ah, bh, ca, cb) + (mm(ah, bl, ca, cb) + mm(al, bh, ca, cb))


def same_block(rows, cols, size):
    r = lax.broadcasted_iota(jnp.int32, (rows, cols), 0) // size
    c = lax.broadcasted_iota(jnp.int32, (rows, cols), 1) // size
    return (r == c).astype(F32)


def head_ones(width):
    return same_block(width, width, width // HEADS).astype(BF16)


def head_mask(width):
    h = lax.broadcasted_iota(jnp.int32, (HEADS, 1, width), 0)
    c = lax.broadcasted_iota(jnp.int32, (HEADS, 1, width), 2) // (width // HEADS)
    return (h == c).astype(F32)


def unit(x, ones):
    r = lax.rsqrt(mm2(x * x, ones) + head_eps)
    return x * r, r


def unit_back(dxn, xn, r, ones):
    return r * (dxn - xn * mm2(dxn * xn, ones))


def norm_scale(x):
    return lax.rsqrt(jnp.mean(x * x, axis=-1, keepdims=True) + norm_eps)


def rounded(x):
    return x.astype(BF16).astype(F32)


def expand_heads(x, hmb):
    n, d = x.shape
    return (x[None] * hmb).reshape(HEADS * n, d)


def head_sum(pairs, hmb):
    out = None
    for h in range(HEADS):
        for a, b in pairs:
            term = mm(a[h], b * hmb[h])
            out = term if out is None else out + term
    return out


def by_head(x):
    n = x.shape[0] // HEADS
    return [x[h * n : (h + 1) * n] for h in range(HEADS)]


def scores(qs, ks):
    return mm(qs[0], ks[0], 1, 1) + (mm(qs[0], ks[1], 1, 1) + mm(qs[1], ks[0], 1, 1))


def key_back(ds, qs):
    d = qs[0].shape[1]
    both = mm(ds[0], jnp.concatenate(qs, axis=1), 0, 0)
    return both[:, :d] + (both[:, d:] + mm(ds[1], qs[0], 0, 0))


def permutation(n, outer):
    inner = n // outer
    r = lax.broadcasted_iota(jnp.int32, (n, n), 0)
    c = lax.broadcasted_iota(jnp.int32, (n, n), 1)
    return (c == (r % inner) * outer + r // inner).astype(F32).astype(BF16)


def date_sequence(pix, enc):
    return (pix.astype(F32) + enc[:, None]).reshape(-1, pix.shape[-1])


def own_tiles(tiles):
    return pl.ds(lax.axis_index("pipe") * tiles, tiles)


def clear_mask(count_ref, tiles, rows, dates):
    lane = lax.broadcasted_iota(jnp.int32, (1, rows), 1)
    first = lax.axis_index("pipe") * tiles
    mask = jnp.zeros((1, rows), F32)
    for t in range(tiles):
        clear = (lane // (rows // tiles) == t) & (lane % dates < count_ref[first + t])
        mask = mask + clear.astype(F32)
    return mask


def temporal_fwd(before_out, tiles, pix_ref, enc_ref, count_ref, cls_ref, gain_ref, w_ref, wo_ref,
                 send_ref, nd_ref, kn_ref, rk_ref, v_ref, ad_ref, ac_ref, att_ref, cq_ref):
    d = pix_ref.shape[-1]
    dates = pix_ref.shape[2]
    classes = cls_ref.shape[0]
    gain = gain_ref[0]
    w_ref = w_ref.at[0]
    wo_ref = wo_ref.at[0]
    x = date_sequence(pix_ref[own_tiles(tiles)], enc_ref[own_tiles(tiles)])
    rows = x.shape[0]
    bps = rows // dates
    mask = clear_mask(count_ref, tiles, rows, dates)
    nd = (x * norm_scale(x) * gain).astype(BF16)
    nd_ref[...] = nd
    cls = cls_ref[...].astype(F32)
    nc = (cls * norm_scale(cls) * gain).astype(BF16)
    ones = head_ones(d)
    hmb = head_mask(d).astype(BF16)
    kv = mm(nd, w_ref[:, d:])
    qkvc = mm(nc, w_ref[...])
    kn, rk = unit(kv[:, :d], ones)
    kn_ref[...] = kn
    rk_ref[...] = rk
    v = kv[:, d:].astype(BF16)
    v_ref[...] = v
    qn, rq = unit(qkvc[:, :d], ones)
    kcn, rkc = unit(qkvc[:, d : 2 * d], ones)
    vc = qkvc[:, 2 * d :].astype(BF16)
    cq_ref[0] = qn
    cq_ref[1] = rq
    cq_ref[2] = kcn
    cq_ref[3] = rkc
    cq_ref[4] = vc.astype(F32)
    group = 128 // dates
    qe = [expand_heads(p, hmb) for p in split(qn)]
    kct = jnp.concatenate([kcn] * group, axis=0)
    ed = jnp.exp(normalizer_sharpness * scores(qe, split(kn))) * mask
    ec = jnp.exp(normalizer_sharpness * scores(qe, split(kct)))
    seg = same_block(128, 128, dates).astype(BF16)
    sum_c = mm2(ec, seg)
    vct = jnp.concatenate([vc] * group, axis=0)
    bmb = group_mask(group, dates).astype(BF16)
    atts = []
    for g in range(bps // group):
        lanes = slice(g * 128, (g + 1) * 128)
        e = ed[:, lanes]
        den = mm2(e, seg) + sum_c
        ad = e / den
        ac = ec / den
        ad_ref[:, lanes] = ad
        ac_ref[:, lanes] = ac
        a2 = jnp.concatenate([ad, ac], axis=1).astype(BF16)
        vst = jnp.concatenate([v[lanes], vct], axis=0)
        atts.append(head_sum([(by_head(expand_patches(a2, bmb)), vst)], hmb))
    att = jnp.concatenate(atts, axis=0).astype(BF16)
    att_ref[...] = att
    before_out()
    upd = jnp.concatenate([cls] * bps, axis=0) + mm(att, wo_ref[...])
    send = mm(permutation(rows, classes), upd.astype(BF16)).astype(BF16)
    part = send_ref.shape[1]
    for k in range(send_ref.shape[0]):
        send_ref[k] = send[k * part : (k + 1) * part]


def expand_patches(x, bmb):
    group, _, lanes = bmb.shape
    n = x.shape[0] // HEADS
    return (x.reshape(HEADS, 1, n, lanes) * bmb[None]).reshape(HEADS * group * n, lanes)


def group_mask(group, dates):
    g = lax.broadcasted_iota(jnp.int32, (group, 1, 256), 0)
    c = (lax.broadcasted_iota(jnp.int32, (group, 1, 256), 2) % 128) // dates
    return (g == c).astype(F32)


def temporal_bwd(tiles, back_ref, pix_ref, enc_ref, cls_ref, gain_ref, w_ref, wo_ref,
                 nd_ref, kn_ref, rk_ref, v_ref, ad_ref, ac_ref, att_ref, cq_ref,
                 dw_ref, dgain_ref, dcls_ref):
    d = pix_ref.shape[-1]
    dates = pix_ref.shape[2]
    classes = cls_ref.shape[0]
    gain = gain_ref[0]
    w_ref = w_ref.at[0]
    wo_ref = wo_ref.at[0]
    x = date_sequence(pix_ref[own_tiles(tiles)], enc_ref[own_tiles(tiles)])
    rows = x.shape[0]
    bps = rows // dates
    cls = cls_ref[...].astype(F32)
    inv_c = norm_scale(cls)
    nc = (cls * inv_c * gain).astype(BF16)
    nd = nd_ref[...]
    ones = head_ones(d)
    hmb = head_mask(d).astype(BF16)
    group = 128 // dates
    back = jnp.concatenate([back_ref[k] for k in range(back_ref.shape[0])], axis=0)
    du = mm(permutation(rows, rows // classes), back).astype(BF16)
    dw_ref[:, 3 * d :] = mm(att_ref[...], du, 0, 0)
    do = mm(du, wo_ref[...], 1, 1).astype(BF16)
    qn = cq_ref[0]
    rq = cq_ref[1]
    kcn = cq_ref[2]
    rkc = cq_ref[3]
    vct = jnp.concatenate([cq_ref[4].astype(BF16)] * group, axis=0)
    kct = jnp.concatenate([kcn] * group, axis=0)
    qe = [expand_heads(p, hmb) for p in split(qn)]
    seg = same_block(128, 128, dates).astype(BF16)
    bm = group_mask(group, dates)
    bmb = bm.astype(BF16)
    qnt = jnp.concatenate([qn] * group, axis=0)
    rqt = jnp.concatenate([rq] * group, axis=0)
    rkct = jnp.concatenate([rkc] * group, axis=0)
    w = w_ref[...]
    wq, wk, wv = w[:, :d], w[:, d : 2 * d], w[:, 2 * d :]
    nct = jnp.concatenate([nc] * group, axis=0)
    dwq = jnp.zeros((d, d), F32)
    dwk = jnp.zeros((d, d), F32)
    dwv = jnp.zeros((d, d), F32)
    dnc = jnp.zeros((classes, d), F32)
    dgain = jnp.zeros((1, d), F32)
    xhat = x * norm_scale(x)
    for g in range(bps // group):
        lanes = slice(g * 128, (g + 1) * 128)
        ad = ad_ref[:, lanes]
        ac = ac_ref[:, lanes]
        a2 = jnp.concatenate([ad, ac], axis=1)
        aexp = expand_patches(a2.astype(BF16), bmb)
        vst = jnp.concatenate([v_ref[lanes, :], vct], axis=0)
        doe = expand_heads(do[lanes], hmb)
        da = jnp.sum(mm(doe, vst, 1, 1).reshape(HEADS, group, classes, 256) * bm[None], axis=1)
        da = rounded(da.reshape(HEADS * classes, 256))
        dvst = mm(aexp, doe, 0, 0).astype(BF16)
        prod = da * a2
        dot = mm2(prod[:, :128] + prod[:, 128:], seg)
        ds = normalizer_sharpness * a2 * (da - jnp.concatenate([dot, dot], axis=1))
        kn = kn_ref[lanes, :]
        kst = jnp.concatenate([kn, kct], axis=0)
        ds = split(ds)
        dh, dl = [by_head(expand_patches(p, bmb)) for p in ds]
        kh, kl = split(kst)
        dqn = head_sum([(dh, kh), (dh, kl), (dl, kh)], hmb)
        dkst = key_back(ds, qe)
        dq = unit_back(dqn, qnt, rqt, ones)
        dk = unit_back(dkst[:128], kn, rk_ref[lanes, :], ones)
        dkc = unit_back(dkst[128:], kct, rkct, ones)
        ndg = nd[lanes]
        dwq += mm2r(nct, dq, 0, 0)
        dwk += mm2r(ndg, dk, 0, 0) + mm2r(nct, dkc, 0, 0)
        dwv += mm(ndg, dvst[:128], 0, 0) + mm(nct, dvst[128:], 0, 0)
        dn_k = rounded(mm2(jnp.concatenate([dk, dkc], axis=0), wk, 1, 1))
        dn = rounded(rounded(mm(dvst, wv, 1, 1)) + dn_k)
        dn_c = rounded(dn[128:] + rounded(mm2(dq, wq, 1, 1)))
        dgain += jnp.sum(dn[:128] * xhat[lanes], axis=0, keepdims=True)
        dnc += jnp.sum(dn_c.reshape(group, classes, d), axis=0)
    dw_ref[:, :d] = dwq
    dw_ref[:, d : 2 * d] = dwk
    dw_ref[:, 2 * d : 3 * d] = dwv
    dgain_ref[...] = dgain + jnp.sum(dnc * cls * inv_c, axis=0, keepdims=True)
    t = dnc * gain
    dcls = inv_c * (t - cls * (inv_c * inv_c * jnp.mean(t * cls, axis=-1, keepdims=True)))
    dcls_ref[...] = dcls + jnp.sum(du.astype(F32).reshape(bps, classes, d), axis=0)


def spatial_rows(recv_ref, kinds):
    sources, rows, d = recv_ref.shape
    n = rows // kinds
    blocks = [recv_ref[s].astype(F32) for s in range(sources)]
    return jnp.concatenate(
        [blocks[s][k * n : (k + 1) * n] for k in range(kinds) for s in range(sources)], axis=0
    )


def spatial_fwd(kinds, tiles, recv_ref, gain_ref, w_ref, wo_ref, head_ref,
                u_ref, n_ref, qk_ref, r_ref, v_ref, a_ref, o_ref, hid_ref, raw_ref, sum_ref):
    d = recv_ref.shape[-1]
    gain_ref = gain_ref.at[1]
    w_ref = w_ref.at[1]
    wo_ref = wo_ref.at[1]
    u = spatial_rows(recv_ref, kinds)
    u_ref[...] = u
    rows = u.shape[0]
    n = (u * norm_scale(u) * gain_ref[...]).astype(BF16)
    n_ref[...] = n
    ones = head_ones(d)
    hmb = head_mask(d).astype(BF16)
    qkv = mm(n, w_ref[...])
    qn, rq = unit(qkv[:, :d], ones)
    kn, rk = unit(qkv[:, d : 2 * d], ones)
    v = qkv[:, 2 * d :].astype(BF16)
    qk_ref[0] = qn
    qk_ref[1] = kn
    r_ref[0] = rq
    r_ref[1] = rk
    v_ref[...] = v
    per = rows // kinds
    patches = per // (recv_ref.shape[0] * tiles)
    ri = (lax.broadcasted_iota(jnp.int32, (per, per), 0) // patches) % tiles
    ci = (lax.broadcasted_iota(jnp.int32, (per, per), 1) // patches) % tiles
    tm = jnp.concatenate([(ri == ci).astype(F32)] * HEADS, axis=0)
    outs = []
    for k in range(kinds):
        rs = slice(k * per, (k + 1) * per)
        qe = [expand_heads(p, hmb) for p in split(qn[rs])]
        e = jnp.exp(normalizer_sharpness * scores(qe, split(kn[rs]))) * tm
        a = e / jnp.sum(e, axis=-1, keepdims=True)
        a_ref[k] = a
        outs.append(head_sum([(by_head(a.astype(BF16)), v[rs])], hmb))
    o = jnp.concatenate(outs, axis=0).astype(BF16)
    o_ref[...] = o
    hid = u + mm(o, wo_ref[...])
    hid_ref[...] = hid
    raw = jnp.sum(hid * head_ref[...], axis=-1, keepdims=True)
    raw = jnp.broadcast_to(raw, (rows, 128))
    raw_ref[...] = raw
    ex = jnp.exp(logit_cap * jnp.tanh(raw / logit_cap))
    total = jnp.sum(ex.reshape(kinds, per, 128), axis=0)
    total = jnp.where(diagonal(per), total, 0.0)
    sum_ref[...] = jnp.broadcast_to(jnp.sum(total, axis=0, keepdims=True), sum_ref.shape)


def diagonal(rows):
    r = lax.broadcasted_iota(jnp.int32, (rows, 128), 0)
    return r == lax.broadcasted_iota(jnp.int32, (rows, 128), 1)


def patch_columns(label_ref, slot_ref, sources, tiles, lanes):
    first = lax.axis_index("pipe") * tiles
    count = label_ref.shape[1]
    patches = count // sources
    shape = (sources * tiles * patches, count)
    row = lax.broadcasted_iota(jnp.int32, shape, 0)
    col = lax.broadcasted_iota(jnp.int32, shape, 1)
    tile = (row // patches) % tiles
    here = col == (row // (patches * tiles)) * patches + row % patches
    slot_shape = (shape[0], lanes)
    slot_tile = (lax.broadcasted_iota(jnp.int32, slot_shape, 0) // patches) % tiles
    lane = lax.broadcasted_iota(jnp.int32, slot_shape, 1)
    labels = jnp.zeros(shape, F32)
    slots = jnp.zeros(slot_shape, F32)
    for t in range(tiles):
        values = label_ref[pl.ds(first + t, 1), :].astype(F32)
        labels = labels + jnp.where(here & (tile == t), values, 0.0)
        slots = slots + ((slot_tile == t) & (lane == slot_ref[first + t])).astype(F32)
    return jnp.broadcast_to(jnp.sum(labels, axis=-1, keepdims=True), slot_shape), slots


def spatial_bwd(kinds, tiles, total_tiles, batch_norm, tot_ref, label_ref, slot_ref, gain_ref, w_ref, wo_ref, head_ref,
                u_ref, n_ref, qk_ref, r_ref, v_ref, a_ref, o_ref, hid_ref, raw_ref,
                send_ref, dw_ref, dgain_ref, dhead_ref, loss_ref):
    d = u_ref.shape[-1]
    gain_ref = gain_ref.at[1]
    w_ref = w_ref.at[1]
    wo_ref = wo_ref.at[1]
    rows = u_ref.shape[0]
    per = rows // kinds
    sources = tot_ref.shape[0]
    total = jnp.sum(tot_ref[...], axis=0)[:1]
    total = jnp.sum(jnp.where(diagonal(per), total, 0.0), axis=-1, keepdims=True)
    total = jnp.broadcast_to(total, (per, 128))
    total = jnp.concatenate([total] * kinds, axis=0)
    th = jnp.tanh(raw_ref[...] / logit_cap)
    logits = logit_cap * th
    label, slot = patch_columns(label_ref, slot_ref, sources, tiles, 128)
    kind = lax.broadcasted_iota(jnp.int32, (rows, 128), 0) // per + lax.axis_index("inner") * kinds
    ind = (jnp.concatenate([label] * kinds, axis=0) == kind.astype(F32)).astype(F32)
    slot = jnp.concatenate([slot] * kinds, axis=0)
    loss = jnp.sum(ind * (jnp.log(total) - logits) * slot, axis=0, keepdims=True) * batch_norm
    loss_ref[...] = jnp.concatenate([loss] * (d // 128), axis=1)
    draw = (jnp.exp(logits) / total - ind) / total_tiles * (1.0 - th * th)
    dr = jnp.concatenate([draw] * (d // 128), axis=1)
    head = head_ref[...]
    dhead_ref[...] = jnp.sum(dr * hid_ref[...], axis=0, keepdims=True)
    col = mm2r(o_ref[...], draw, 0, 0)
    dw_ref[:, 3 * d :] = jnp.concatenate([col] * (d // 128), axis=1) * head
    head_back = mm2(jnp.broadcast_to(head, (8, d)), wo_ref[...], 1, 1)[:1]
    do = (dr * head_back).astype(BF16)
    ones = head_ones(d)
    hmb = head_mask(d).astype(BF16)
    dqs, dks, dvs = [], [], []
    for k in range(kinds):
        rs = slice(k * per, (k + 1) * per)
        a = a_ref[k]
        doe = expand_heads(do[rs], hmb)
        da = rounded(mm(doe, v_ref[rs, :], 1, 1))
        dvs.append(mm(a.astype(BF16), doe, 0, 0))
        ds = normalizer_sharpness * a * (da - jnp.sum(da * a, axis=-1, keepdims=True))
        qn = qk_ref[0, rs, :]
        kn = qk_ref[1, rs, :]
        ds = split(ds)
        dh, dl = [by_head(p) for p in ds]
        kh, kl = split(kn)
        qe = [expand_heads(p, hmb) for p in split(qn)]
        dqs.append(unit_back(head_sum([(dh, kh), (dh, kl), (dl, kh)], hmb), qn, r_ref[0, rs, :], ones))
        dks.append(unit_back(key_back(ds, qe), kn, r_ref[1, rs, :], ones))
    dq = jnp.concatenate(dqs, axis=0)
    dk = jnp.concatenate(dks, axis=0)
    dv = jnp.concatenate(dvs, axis=0).astype(BF16)
    n = n_ref[...]
    dw_ref[:, :d] = mm2r(n, dq, 0, 0)
    dw_ref[:, d : 2 * d] = mm2r(n, dk, 0, 0)
    dw_ref[:, 2 * d : 3 * d] = mm(n, dv, 0, 0)
    w = w_ref[...]
    dn = rounded(rounded(mm(dv, w[:, 2 * d :], 1, 1)) + rounded(mm2(dk, w[:, d : 2 * d], 1, 1)))
    dn = rounded(dn + rounded(mm2(dq, w[:, :d], 1, 1)))
    u = u_ref[...]
    inv = norm_scale(u)
    dgain_ref[...] = jnp.sum(dn * u * inv, axis=0, keepdims=True)
    t = dn * gain_ref[...]
    du = dr * head + inv * (t - u * (inv * inv * jnp.mean(t * u, axis=-1, keepdims=True)))
    m = per // sources
    for s in range(sources):
        parts = [du[k * per + s * m : k * per + (s + 1) * m] for k in range(kinds)]
        send_ref[s] = jnp.concatenate(parts, axis=0).astype(BF16)


MESH = pl.DeviceIdType.MESH


def enter(devices):
    barrier = pltpu.get_barrier_semaphore()
    for dev in devices:
        pl.semaphore_signal(barrier, inc=1, device_id=dev, device_id_type=MESH)
    pl.semaphore_wait(barrier, len(devices))


def push(src, dst, sems, k, dev):
    copy = pltpu.make_async_remote_copy(
        src_ref=src, dst_ref=dst, send_sem=sems[0].at[k], recv_sem=sems[1].at[k],
        device_id=dev, device_id_type=MESH,
    )
    copy.start()
    return copy


def swap(src, dst, sems, first, whole):
    count = dst.shape[0]
    me = lax.axis_index("inner")
    copies = []
    for k in range(1, count):
        dev = lax.rem(me + k, count)
        block = src if whole else src.at[dev]
        copies.append(push(block, dst.at[me], sems, first + k - 1, {"inner": dev}))
    dst[me] = src[...] if whole else src[me]
    return copies


def bring_weights(wq_ref, wo_ref, g_ref, oq_ref, oo_ref, og_ref, sems, first):
    pipe = lax.axis_index("pipe")
    dp = lax.axis_index("dp")
    core = lax.rem(dp, 2)
    far = {"pipe": 1 - pipe}
    near = {"dp": dp + 1 - 2 * core}
    half = wq_ref.shape[1] // 2
    mine = pl.ds(pl.multiple_of(core * half, half), half)
    both = ((wq_ref, oq_ref), (wo_ref, oo_ref))
    started = [
        push(src.at[0, mine], dst.at[pipe, mine], sems, first + k, far) for k, (src, dst) in enumerate(both)
    ]
    gains = push(g_ref, og_ref.at[pipe], sems, first + 4, far)
    oq_ref[pipe] = wq_ref[0]
    oo_ref[pipe] = wo_ref[0]
    og_ref[pipe] = g_ref[...]

    def pass_on(k):
        started[k].wait_recv()
        there = both[k][1].at[1 - pipe, mine]
        copy = push(there, there, sems, first + 2 + k, near)
        started.append(copy)
        copy.wait_recv()

    pass_on(0)
    gains.wait_recv()
    started.append(gains)
    return started, lambda: pass_on(1)


def total_partners():
    dp = lax.axis_index("dp")
    inner = lax.axis_index("inner")
    return [
        {"dp": dp + 1 - 2 * lax.rem(dp, 2)},
        {"pipe": 1 - lax.axis_index("pipe")},
        {"dp": dp + 2 - 4 * (dp // 2)},
        {"inner": inner + 1 - 2 * lax.rem(inner, 2)},
        {"inner": inner + 2 - 4 * (inner // 2)},
    ]


def first_hop(layer, dw, b0, sems):
    core = lax.rem(lax.axis_index("dp"), 2)
    rows, width = dw.shape
    half, cols = rows // 2, width // 2
    there = pl.ds(pl.multiple_of((1 - core) * half, half), half)
    return [
        push(dw.at[there, pl.ds(c * cols, cols)], b0.at[c, layer], sems, 16 * c + layer, total_partners()[0])
        for c in range(2)
    ]


def total(early, dw0, dw1, dcls, dg0, dg1, dhead, loss, res, osmall,
          b0, a0, s1, b1, a1, s2, b2, a2, b3, a4, x0, xs, xr, sems):
    pipe = lax.axis_index("pipe")
    dp = lax.axis_index("dp")
    inner = lax.axis_index("inner")
    core = lax.rem(dp, 2)
    y = dp // 2
    rows, width = dw0.shape
    cols = width // 2
    partners = total_partners()
    started = []

    def send(k, src, dst, sem):
        started.append(push(src, dst, sems, sem, partners[k]))
        return started[-1]

    def part(bit, size):
        return pl.ds(pl.multiple_of(bit * size, size), size)

    def span(c):
        return pl.ds(c * cols, cols)

    nc = dcls.shape[0]
    x0[...] = jnp.zeros_like(x0)
    for k, gain in enumerate((dg0, dg1)):
        x0[k, :nc, :] = dcls[...]
        x0[k, nc : nc + 1, :] = gain[...]
        x0[k, nc + 1 : nc + 2, :] = dhead[...]
        x0[k, nc + 2 : nc + 3, :] = loss[...]
    half = rows // 2
    quarter = half // 2
    late = first_hop(0, dw0, b0, sems)
    started += early + late
    going = list(zip(late, early))
    small = send(0, x0, xr.at[pl.ds(0, 2)], 32)
    mine = part(core, half)
    hops = []
    for c in range(2):
        for copy in going[c]:
            copy.wait_recv()
        for k, dw in enumerate((dw0, dw1)):
            a0[c, k] = dw[mine, span(c)] + b0[c, k]
        if c == 0:
            s1[0] = a0[0, 1 - pipe].astype(s1.dtype)
            hops.append(send(1, s1.at[0], b1.at[0], 2))
        else:
            for k in range(2):
                s1[1, pl.ds(k * quarter, quarter)] = a0[1, k, part(1 - y, quarter)].astype(s1.dtype)
            hops.append(send(2, s1.at[1], b1.at[1], 19))
    small.wait_recv()
    xs[pl.ds(0, 2)] = x0[...] + xr[pl.ds(0, 2)]
    small = send(1, xs.at[1 - pipe], xr.at[2], 33)
    hops[0].wait_recv()
    a1[0] = a0[0, pipe] + b1[0].astype(F32)
    s2[0] = a1[0, part(1 - y, quarter)].astype(s2.dtype)
    hops[0] = send(2, s2.at[0], b2.at[0], 3)
    hops[1].wait_recv()
    for k in range(2):
        there = pl.ds(k * quarter, quarter)
        a1[1, there] = a0[1, k, part(y, quarter)] + b1[1, there].astype(F32)
    s2[1] = a1[1, part(1 - pipe, quarter)].astype(s2.dtype)
    hops[1] = send(1, s2.at[1], b2.at[1], 18)
    small.wait_recv()
    xs[2] = xs[pipe] + xr[2]
    small = send(2, xs.at[2], xr.at[3], 34)
    count = b3.shape[1] + 1
    size = quarter // count
    peers = [lax.rem(inner + k, count) for k in range(1, count)]
    hops_in = [[], []]
    for c, bit in enumerate((y, pipe)):
        hops[c].wait_recv()
        a2[c] = a1[c, part(bit, quarter)] + b2[c].astype(F32)
        for k, dev in enumerate(peers):
            copy = push(a2.at[c, part(dev, size)], b3.at[c, k], sems, 16 * c + 4 + k, {"inner": dev})
            hops_in[c].append(copy)
    small.wait_recv()
    xs[3] = xs[2] + xr[3]
    small = send(3, xs.at[3], xr.at[4], 35)

    def shard(y_at, inner_at):
        return pl.ds(pl.multiple_of(core * half + y_at * quarter + inner_at * size, size), size)

    ins = [[], []]
    ys = [[], []]
    for c in range(2):
        for copy in hops_in[c]:
            copy.wait_recv()
        own = a2[c, part(inner, size)]
        for k in range(count - 1):
            own = own + b3[c, k]
        a4[c] = own
        here = shard(y, inner)
        res[c, here] = own
        for k, dev in enumerate(peers):
            ins[c].append(push(a4.at[c], res.at[c, here], sems, 16 * c + 7 + k, {"inner": dev}))
        ys[c].append(send(2, a4.at[c], res.at[c, here], 16 * c + 10))
    started += hops_in[0] + hops_in[1] + ins[0] + ins[1]
    small.wait_recv()
    xs[4] = xs[3] + xr[4]
    small = send(4, xs.at[4], xr.at[5], 36)
    for k in range(1, count):
        here = shard(y, lax.rem(inner + count - k, count))
        for c in range(2):
            ins[c][k - 1].wait_recv()
            ys[c].append(send(2, res.at[c, here], res.at[c, here], 16 * c + 10 + k))
    gathers = []

    def to_core(c, y_at, sem):
        here = pl.ds(pl.multiple_of(core * half + y_at * quarter, quarter), quarter)
        gathers.append(send(0, res.at[c, here], res.at[c, here], 16 * c + sem))

    for c in range(2):
        to_core(c, y, 14)
    small.wait_recv()
    xs[5] = xs[4] + xr[5]
    for c in range(2):
        for copy in ys[c]:
            copy.wait_recv()
        to_core(c, 1 - y, 15)
    osmall[...] = xs[5]
    for copy in gathers:
        copy.wait_recv()
    for copy in started:
        copy.wait_send()


def finish(res, small, oqkv, oout, ocls, ogain, ohead, oloss):
    cols = res.shape[2]
    nc = ocls.shape[0]
    first = oqkv.shape[2] - cols
    oqkv[0, :, :cols] = res[0]
    oqkv[0, :, cols:] = res[1, :, :first]
    oout[0] = res[1, :, first:]
    ocls[...] = small[:nc, :]
    ogain[...] = small[nc : nc + 1, :]
    ohead[...] = small[nc + 1 : nc + 2, :]
    oloss[...] = small[nc + 2 : nc + 3, : oloss.shape[1]]


def small_shape(classes, width):
    return (-(-(classes + 3) // 8) * 8, width)


def total_scratch(rows, width, classes, inner_count):
    half, cols = rows // 2, width // 2
    extra = small_shape(classes, width // 4)
    return [
        pltpu.VMEM((2, 2, half, cols), F32),
        pltpu.VMEM((2, 2, half, cols), F32),
        pltpu.VMEM((2, half, cols), BF16),
        pltpu.VMEM((2, half, cols), BF16),
        pltpu.VMEM((2, half, cols), F32),
        pltpu.VMEM((2, half // 2, cols), BF16),
        pltpu.VMEM((2, half // 2, cols), BF16),
        pltpu.VMEM((2, half // 2, cols), F32),
        pltpu.VMEM((2, inner_count - 1, half // 2 // inner_count, cols), F32),
        pltpu.VMEM((2, half // 2 // inner_count, cols), F32),
        pltpu.VMEM((2,) + extra, F32),
        pltpu.VMEM((6,) + extra, F32),
        pltpu.VMEM((6,) + extra, F32),
    ]


def local(fn, outs, scalars, *args):
    specs = vmem(len(args))
    for k in scalars:
        specs[k] = pl.BlockSpec(memory_space=pltpu.SMEM)
    return pl.pallas_call(
        fn,
        out_shape=[jax.ShapeDtypeStruct(s, t) for s, t in outs],
        in_specs=specs,
        out_specs=vmem(len(outs)),
        compiler_params=params(),
    )(*args)


def date_encoding(date_days, width):
    channel = jnp.arange(width)
    frequency = jnp.exp((channel // 2 * 2).astype(F32) * (-math.log(10000.0) / width))
    phases = date_days.astype(F32)[:, :, None] * frequency
    return jnp.where(channel % 2 == 0, jnp.sin(phases), jnp.cos(phases))


def saved_shapes(rows, width):
    hq = HEADS * CLASSES
    f, b = F32, BF16
    return [((rows, width), b), ((rows, width), f), ((rows, width), f), ((rows, width), b),
            ((hq, rows), f), ((hq, rows), f), ((rows, width), b), ((5, CLASSES, width), f)]


def kept_shapes(kinds, per, width):
    srows = kinds * per
    f, b = F32, BF16
    return [((srows, width), f), ((srows, width), b), ((2, srows, width), f), ((2, srows, width), f),
            ((srows, width), b), ((kinds, HEADS * per, per), f), ((srows, width), b), ((srows, width), f),
            ((srows, 128), f)]


def grad_shapes(width):
    return [((width, 4 * width), F32), ((1, width), F32)]


def everything(tiles, kinds, total_tiles, batch_norm,
               wq_own, wo_own, g_own, pix_ref, enc_ref, count_ref, slot_ref, label_ref, cls_ref, head_ref,
               res_ref, small_ref, w_ref, wo_ref, g_ref, *refs):
    refs = list(refs)

    def take(count):
        taken, refs[:count] = refs[:count], []
        return taken

    send_ref, recv_ref, back_ref, returned_ref, sums_ref, totals_ref = take(6)
    saved = take(8)
    kept = take(9)
    dw0, dg0, dw1, dg1, dcls, dhead, loss = take(7)
    parts = take(13)
    sems = take(2)
    inner = lax.axis_index("inner")
    count = recv_ref.shape[0]
    along = total_partners()
    enter(along[:3] + [{"inner": lax.rem(inner + k, count)} for k in range(1, count)])
    started, before_out = bring_weights(wq_own, wo_own, g_own, w_ref, wo_ref, g_ref, sems, 37)
    temporal_fwd(before_out, tiles, pix_ref, enc_ref, count_ref, cls_ref, g_ref, w_ref, wo_ref, send_ref, *saved)
    copies = swap(send_ref, recv_ref, sems, 42, False)
    for copy in copies:
        copy.wait_recv()
    started += copies
    spatial_fwd(kinds, tiles, recv_ref, g_ref, w_ref, wo_ref, head_ref, *kept, sums_ref)
    copies = swap(sums_ref, totals_ref, sems, 42 + count, True)
    for copy in copies:
        copy.wait_recv()
    started += copies
    spatial_bwd(kinds, tiles, total_tiles, batch_norm, totals_ref, label_ref, slot_ref,
                g_ref, w_ref, wo_ref, head_ref, *kept, back_ref, dw1, dg1, dhead, loss)
    copies = swap(back_ref, returned_ref, sems, 42 + 2 * count, False)
    early = first_hop(1, dw1, parts[0], sems)
    for copy in copies:
        copy.wait_recv()
    started += copies
    temporal_bwd(tiles, returned_ref, pix_ref, enc_ref, cls_ref, g_ref, w_ref, wo_ref, *saved, dw0, dg0, dcls)
    total(early, dw0, dw1, dcls, dg0, dg1, dhead, loss, res_ref, small_ref, *parts, sems)
    for copy in started:
        copy.wait_send()


def shards(pixels, date_days, clear_count, batch_slot, labels, class_tokens, section_gain,
           segment_probe_lookup_content, section_out, head_vec):
    tiles_dev, patches_dev, dates, width = pixels.shape
    inner_count = lax.axis_size("inner")
    kinds = CLASSES // inner_count
    total_tiles = tiles_dev * lax.axis_size("dp")
    tiles = tiles_dev // 2
    rows = tiles * patches_dev * dates
    batch_norm = 1.0 / (total_tiles // MICRO * PATCHES)
    enc = date_encoding(date_days, width)
    head = head_vec.reshape(1, width)
    per = inner_count * tiles * patches_dev
    exchanged = ((inner_count, rows // inner_count, width), BF16)
    shapes = [
        ((2,) + segment_probe_lookup_content.shape[1:], BF16),
        ((2,) + section_out.shape[1:], BF16),
        ((2,) + section_gain.shape, F32),
        exchanged, exchanged, exchanged, exchanged,
        ((8, 128), F32), ((inner_count, 8, 128), F32),
    ]
    shapes += saved_shapes(rows, width) + kept_shapes(kinds, per, width) + grad_shapes(width) * 2
    shapes += [((CLASSES, width), F32), ((1, width), F32), ((1, width), F32)]
    specs = vmem(10)
    specs[5] = specs[6] = pl.BlockSpec(memory_space=pltpu.SMEM)
    sems = 42 + 3 * inner_count
    grads, small = pl.pallas_call(
        functools.partial(everything, tiles, kinds, total_tiles, batch_norm),
        out_shape=[
            jax.ShapeDtypeStruct((2, width, 2 * width), F32),
            jax.ShapeDtypeStruct(small_shape(CLASSES, width), F32),
        ],
        in_specs=specs,
        out_specs=vmem(2),
        scratch_shapes=[pltpu.VMEM(s, t) for s, t in shapes]
        + total_scratch(width, 4 * width, CLASSES, inner_count)
        + [pltpu.SemaphoreType.DMA((sems,))] * 2,
        compiler_params=params(collective_id=0, has_side_effects=True),
    )(segment_probe_lookup_content, section_out, section_gain, pixels, enc, clear_count, batch_slot,
      labels, class_tokens, head)
    gqkv, gout, gcls, ggain, ghead, gloss = local(
        finish,
        [((1, width, 3 * width), F32), ((1, width, width), F32), ((CLASSES, width), F32), ((1, width), F32),
         ((1, width), F32), ((1, MICRO), F32)], (),
        grads, small,
    )
    return gloss.reshape(MICRO), gcls, ggain, gqkv, gout, ghead.reshape(width)


def solution(mesh):
    placed = (
        P("dp", "inner", None, None),
        P("dp", None),
        P("dp"),
        P("dp"),
        P("dp", None),
        P(),
        P("pipe", None),
        P("pipe", None, None),
        P("pipe", None, None),
        P(),
    )

    def body(*args):
        tiles_dev, patches_dev, dates, width = args[0].shape
        pairs = tiles_dev // 2 * patches_dev
        sizes = tuple(mesh.shape[a] for a in ("pipe", "dp", "inner"))
        fits = sizes == (2, 4, 4) and pairs % 8 == 0 and dates == CLASSES and width == 256
        fits = fits and tiles_dev // 2 * PATCHES <= 128
        return (shards if fits else shards_general)(*args)

    return jax.shard_map(
        body,
        mesh=mesh,
        in_specs=placed,
        out_specs=(P(), P(), P("pipe", None), P("pipe", None, None), P("pipe", None, None), P()),
        check_vma=False,
    )
```

```python
import functools
import math

import jax
import jax.numpy as jnp
from jax import lax
from jax.experimental import pallas as pl
from jax.experimental.pallas import tpu as pltpu
from jax.sharding import PartitionSpec as P

HEADS = 8
CLASSES = 16
PATCHES = 48
MICRO = 4


normalizer_sharpness = 10.0
logit_cap = 15.0
norm_eps = 1e-05
head_eps = 1e-06


def matmul_f32(left_side, right_side):
    return jnp.einsum(
        "...d,de->...e",
        left_side,
        right_side.astype(jnp.bfloat16),
        preferred_element_type=jnp.float32,
    )


def rms_norm(inputs, gain_vec):
    inverse_rms = lax.rsqrt(jnp.mean(inputs * inputs, axis=-1, keepdims=True) + norm_eps)
    return inputs * inverse_rms * gain_vec


def unit_heads(values):
    shaped = values.reshape(values.shape[:-1] + (HEADS, values.shape[-1] // HEADS))
    return shaped * lax.rsqrt(jnp.sum(shaped * shaped, axis=-1, keepdims=True) + head_eps)


def temporal(pixel_rows, date_days, counts, params):
    class_init, gain_vec, w_qkv, w_out = params
    batch_count, patches, dates_max, model_width = pixel_rows.shape
    classes = class_init.shape[0]
    band_channel = jnp.arange(model_width)
    frequency = jnp.exp(
        (band_channel // 2 * 2).astype(jnp.float32) * (-math.log(10000.0) / model_width)
    )
    phases = date_days.astype(jnp.float32)[:, :, None] * frequency
    encoding = jnp.where(band_channel % 2 == 0, jnp.sin(phases), jnp.cos(phases))
    date_rows = pixel_rows.astype(jnp.float32) + encoding[:, None]
    class_rows = jnp.broadcast_to(class_init, (batch_count, patches, classes, model_width))
    sequence = jnp.concatenate([class_rows, date_rows], axis=2)
    normed = rms_norm(sequence, gain_vec).astype(jnp.bfloat16)
    probe_entry_lines = unit_heads(matmul_f32(normed[:, :, :classes], w_qkv[:, :model_width]))
    lookup_entry_lines = unit_heads(matmul_f32(normed, w_qkv[:, model_width : 2 * model_width]))
    value_rows = matmul_f32(normed, w_qkv[:, 2 * model_width :]).astype(jnp.bfloat16)
    value_heads = value_rows.reshape(
        batch_count, patches, classes + dates_max, HEADS, model_width // HEADS
    )
    affinity_logit_grid = normalizer_sharpness * jnp.einsum(
        "ohbyv,ohsyv->ohybs", probe_entry_lines, lookup_entry_lines, precision=lax.Precision.HIGHEST
    )
    position = jnp.arange(classes + dates_max)
    key_mask = (
        (position[None, :] < classes) | (position[None, :] - classes < counts[:, None])
    ).astype(jnp.float32)
    raised = jnp.exp(affinity_logit_grid) * key_mask[:, None, None, None, :]
    weights = (raised / jnp.sum(raised, axis=-1, keepdims=True)).astype(jnp.bfloat16)
    attended = jnp.einsum(
        "bphqk,bpkhe->bpqhe", weights, value_heads, preferred_element_type=jnp.float32
    )
    attended = attended.reshape(batch_count, patches, classes, model_width).astype(jnp.bfloat16)
    updated = sequence[:, :, :classes] + matmul_f32(attended, w_out)
    return jnp.swapaxes(updated, 1, 2).astype(jnp.bfloat16)


def spatial(inputs, params):
    gain_vec, w_qkv, w_out, head_vec = params
    batch_count, groups, classes, patches, model_width = inputs.shape
    class_seq = (
        jnp.swapaxes(inputs, 1, 2)
        .reshape(batch_count, classes, groups * patches, model_width)
        .astype(jnp.float32)
    )
    normed = rms_norm(class_seq, gain_vec).astype(jnp.bfloat16)
    probe_entry_lines = unit_heads(matmul_f32(normed, w_qkv[:, :model_width]))
    lookup_entry_lines = unit_heads(matmul_f32(normed, w_qkv[:, model_width : 2 * model_width]))
    value_rows = matmul_f32(normed, w_qkv[:, 2 * model_width :]).astype(jnp.bfloat16)
    value_heads = value_rows.reshape(
        batch_count, classes, groups * patches, HEADS, model_width // HEADS
    )
    affinity_logit_grid = normalizer_sharpness * jnp.einsum(
        "wisbx,wiqbx->wibsq", probe_entry_lines, lookup_entry_lines, precision=lax.Precision.HIGHEST
    )
    raised = jnp.exp(affinity_logit_grid)
    weights = (raised / jnp.sum(raised, axis=-1, keepdims=True)).astype(jnp.bfloat16)
    attended = jnp.einsum(
        "bchqk,bckhe->bcqhe", weights, value_heads, preferred_element_type=jnp.float32
    )
    attended = attended.reshape(batch_count, classes, groups * patches, model_width).astype(
        jnp.bfloat16
    )
    hidden = class_seq + matmul_f32(attended, w_out)
    raw_logits = jnp.einsum("bcpd,d->bcp", hidden, head_vec, precision=lax.Precision.HIGHEST)
    logits = logit_cap * jnp.tanh(raw_logits / logit_cap)
    return logits.reshape(batch_count, classes, groups, patches)


def shards_general(
    pixels,
    date_days,
    clear_count,
    batch_slot,
    labels,
    class_tokens,
    section_gain,
    segment_probe_lookup_content,
    section_out,
    head_vec,
):
    tiles_dev = pixels.shape[0]
    patches_dev = pixels.shape[1]
    model_width = pixels.shape[3]
    inner_count = lax.axis_size("inner")
    classes_dev = CLASSES // inner_count
    total_tiles = tiles_dev * lax.axis_size("dp")
    my_group = lax.axis_index("inner")
    class_ids = my_group * classes_dev + jnp.arange(classes_dev, dtype=jnp.int32)
    batch_norm = 1.0 / (total_tiles // MICRO * PATCHES)
    gains, qkv_all, out_all = (
        lax.all_gather(section_gain, "pipe", axis=0, tiled=True),
        lax.all_gather(
            segment_probe_lookup_content.astype(jnp.float32), "pipe", axis=0, tiled=True
        ),
        lax.all_gather(section_out.astype(jnp.float32), "pipe", axis=0, tiled=True),
    )
    pipe_pos = lax.axis_index("pipe")
    half_tiles = tiles_dev // 2
    first_params = (class_tokens.astype(jnp.float32), gains[0], qkv_all[0], out_all[0])
    second_params = (gains[1], qkv_all[1], out_all[1], head_vec)
    fold_shape = (1, inner_count, classes_dev, patches_dev, model_width)
    first_gradients = jax.tree.map(jnp.zeros_like, first_params)
    grads_second = jax.tree.map(jnp.zeros_like, second_params)
    loss_vec = jnp.zeros((MICRO,), jnp.float32)
    for tile_step in range(half_tiles):
        start = pipe_pos * half_tiles + tile_step
        single_pixel = lax.dynamic_slice_in_dim(pixels, start, 1, 0)
        days_one = lax.dynamic_slice_in_dim(date_days, start, 1, 0)
        count_one = lax.dynamic_slice_in_dim(clear_count, start, 1, 0)
        label_one = lax.dynamic_slice_in_dim(labels, start, 1, 0)
        slot_one = lax.dynamic_slice_in_dim(batch_slot, start, 1, 0)
        encoded, pull_first = jax.vjp(
            lambda params: temporal(single_pixel, days_one, count_one, params), first_params
        )
        arrived = lax.all_to_all(
            encoded.reshape(fold_shape), "inner", split_axis=1, concat_axis=1, tiled=True
        )
        logits, pull_second = jax.vjp(spatial, arrived, second_params)
        exp_logits = jnp.exp(logits)
        class_total = lax.psum(jnp.sum(exp_logits, axis=1), "inner")
        label_rows = label_one.reshape(1, 1, inner_count, patches_dev)
        indicator_rows = (label_rows == class_ids[None, :, None, None]).astype(jnp.float32)
        dlogit = (exp_logits / class_total[:, None] - indicator_rows) / total_tiles
        grad_in, grad_two = pull_second(dlogit)
        returned = lax.all_to_all(grad_in, "inner", split_axis=1, concat_axis=1, tiled=True)
        (derivative_lone,) = pull_first(returned.reshape(encoded.shape))
        first_gradients = jax.tree.map(
            lambda total, extra: total + extra, first_gradients, derivative_lone
        )
        grads_second = jax.tree.map(lambda total, extra: total + extra, grads_second, grad_two)
        loss_term = jnp.sum(indicator_rows * (jnp.log(class_total)[:, None] - logits)) * batch_norm
        loss_vec = loss_vec + loss_term * (jnp.arange(MICRO) == slot_one[0]).astype(jnp.float32)
    stacked = (
        jnp.stack([first_gradients[1], grads_second[0]]),
        jnp.stack([first_gradients[2], grads_second[1]]),
        jnp.stack([first_gradients[3], grads_second[2]]),
        first_gradients[0],
        grads_second[3],
        loss_vec,
    )
    summed = lax.psum(
        (stacked[0], stacked[1], stacked[2], stacked[3], stacked[4], stacked[5]),
        ("pipe", "dp", "inner"),
    )
    gain_grad = lax.dynamic_slice_in_dim(summed[0], pipe_pos, 1, 0)
    qkv_grad = lax.dynamic_slice_in_dim(summed[1], pipe_pos, 1, 0)
    out_grad = lax.dynamic_slice_in_dim(summed[2], pipe_pos, 1, 0)
    return (summed[5], summed[3], gain_grad, qkv_grad, out_grad, summed[4])


F32 = jnp.float32
BF16 = jnp.bfloat16
VMEM_LIMIT = 56 * 2**20


def params(**kw):
    return pltpu.CompilerParams(vmem_limit_bytes=VMEM_LIMIT, **kw)


def vmem(count):
    return [pl.BlockSpec(memory_space=pltpu.VMEM)] * count


def mm(a, b, ca=1, cb=0):
    return lax.dot_general(a, b, (((ca,), (cb,)), ((), ())), preferred_element_type=F32)


def split(a):
    hi = a.astype(BF16)
    return hi, (a - hi.astype(F32)).astype(BF16)


def mm2(a, b, ca=1, cb=0):
    hi, lo = split(a)
    return mm(hi, b, ca, cb) + mm(lo, b, ca, cb)


def mm2r(a, b, ca=1, cb=0):
    hi, lo = split(b)
    return mm(a, hi, ca, cb) + mm(a, lo, ca, cb)


def mm3(a, b, ca=1, cb=0):
    ah, al = split(a)
    bh, bl = split(b)
    return mm(ah, bh, ca, cb) + (mm(ah, bl, ca, cb) + mm(al, bh, ca, cb))


def same_block(rows, cols, size):
    r = lax.broadcasted_iota(jnp.int32, (rows, cols), 0) // size
    c = lax.broadcasted_iota(jnp.int32, (rows, cols), 1) // size
    return (r == c).astype(F32)


def head_ones(width):
    return same_block(width, width, width // HEADS).astype(BF16)


def head_mask(width):
    h = lax.broadcasted_iota(jnp.int32, (HEADS, 1, width), 0)
    c = lax.broadcasted_iota(jnp.int32, (HEADS, 1, width), 2) // (width // HEADS)
    return (h == c).astype(F32)


def unit(x, ones):
    r = lax.rsqrt(mm2(x * x, ones) + head_eps)
    return x * r, r


def unit_back(dxn, xn, r, ones):
    return r * (dxn - xn * mm2(dxn * xn, ones))


def norm_scale(x):
    return lax.rsqrt(jnp.mean(x * x, axis=-1, keepdims=True) + norm_eps)


def rounded(x):
    return x.astype(BF16).astype(F32)


def expand_heads(x, hmb):
    n, d = x.shape
    return (x[None] * hmb).reshape(HEADS * n, d)


def head_sum(pairs, hmb):
    out = None
    for h in range(HEADS):
        for a, b in pairs:
            term = mm(a[h], b * hmb[h])
            out = term if out is None else out + term
    return out


def by_head(x):
    n = x.shape[0] // HEADS
    return [x[h * n : (h + 1) * n] for h in range(HEADS)]


def scores(qs, ks):
    return mm(qs[0], ks[0], 1, 1) + (mm(qs[0], ks[1], 1, 1) + mm(qs[1], ks[0], 1, 1))


def key_back(ds, qs):
    d = qs[0].shape[1]
    both = mm(ds[0], jnp.concatenate(qs, axis=1), 0, 0)
    return both[:, :d] + (both[:, d:] + mm(ds[1], qs[0], 0, 0))


def permutation(n, outer):
    inner = n // outer
    r = lax.broadcasted_iota(jnp.int32, (n, n), 0)
    c = lax.broadcasted_iota(jnp.int32, (n, n), 1)
    return (c == (r % inner) * outer + r // inner).astype(F32).astype(BF16)


def date_sequence(pix, enc):
    return (pix.astype(F32) + enc[:, None]).reshape(-1, pix.shape[-1])


def own_tiles(tiles):
    return pl.ds(lax.axis_index("pipe") * tiles, tiles)


def clear_mask(count_ref, tiles, rows, dates):
    lane = lax.broadcasted_iota(jnp.int32, (1, rows), 1)
    first = lax.axis_index("pipe") * tiles
    mask = jnp.zeros((1, rows), F32)
    for t in range(tiles):
        clear = (lane // (rows // tiles) == t) & (lane % dates < count_ref[first + t])
        mask = mask + clear.astype(F32)
    return mask


def temporal_fwd(before_out, tiles, pix_ref, enc_ref, count_ref, cls_ref, gain_ref, w_ref, wo_ref,
                 send_ref, nd_ref, kn_ref, rk_ref, v_ref, ad_ref, ac_ref, att_ref, cq_ref):
    d = pix_ref.shape[-1]
    dates = pix_ref.shape[2]
    classes = cls_ref.shape[0]
    gain = gain_ref[0]
    w_ref = w_ref.at[0]
    wo_ref = wo_ref.at[0]
    x = date_sequence(pix_ref[own_tiles(tiles)], enc_ref[own_tiles(tiles)])
    rows = x.shape[0]
    bps = rows // dates
    mask = clear_mask(count_ref, tiles, rows, dates)
    nd = (x * norm_scale(x) * gain).astype(BF16)
    nd_ref[...] = nd
    cls = cls_ref[...].astype(F32)
    nc = (cls * norm_scale(cls) * gain).astype(BF16)
    ones = head_ones(d)
    hmb = head_mask(d).astype(BF16)
    kv = mm(nd, w_ref[:, d:])
    qkvc = mm(nc, w_ref[...])
    kn, rk = unit(kv[:, :d], ones)
    kn_ref[...] = kn
    rk_ref[...] = rk
    v = kv[:, d:].astype(BF16)
    v_ref[...] = v
    qn, rq = unit(qkvc[:, :d], ones)
    kcn, rkc = unit(qkvc[:, d : 2 * d], ones)
    vc = qkvc[:, 2 * d :].astype(BF16)
    cq_ref[0] = qn
    cq_ref[1] = rq
    cq_ref[2] = kcn
    cq_ref[3] = rkc
    cq_ref[4] = vc.astype(F32)
    group = 128 // dates
    qe = [expand_heads(p, hmb) for p in split(qn)]
    kct = jnp.concatenate([kcn] * group, axis=0)
    ed = jnp.exp(normalizer_sharpness * scores(qe, split(kn))) * mask
    ec = jnp.exp(normalizer_sharpness * scores(qe, split(kct)))
    seg = same_block(128, 128, dates).astype(BF16)
    sum_c = mm2(ec, seg)
    vct = jnp.concatenate([vc] * group, axis=0)
    bmb = group_mask(group, dates).astype(BF16)
    atts = []
    for g in range(bps // group):
        lanes = slice(g * 128, (g + 1) * 128)
        e = ed[:, lanes]
        den = mm2(e, seg) + sum_c
        ad = e / den
        ac = ec / den
        ad_ref[:, lanes] = ad
        ac_ref[:, lanes] = ac
        a2 = jnp.concatenate([ad, ac], axis=1).astype(BF16)
        vst = jnp.concatenate([v[lanes], vct], axis=0)
        atts.append(head_sum([(by_head(expand_patches(a2, bmb)), vst)], hmb))
    att = jnp.concatenate(atts, axis=0).astype(BF16)
    att_ref[...] = att
    before_out()
    upd = jnp.concatenate([cls] * bps, axis=0) + mm(att, wo_ref[...])
    send = mm(permutation(rows, classes), upd.astype(BF16)).astype(BF16)
    part = send_ref.shape[1]
    for k in range(send_ref.shape[0]):
        send_ref[k] = send[k * part : (k + 1) * part]


def expand_patches(x, bmb):
    group, _, lanes = bmb.shape
    n = x.shape[0] // HEADS
    return (x.reshape(HEADS, 1, n, lanes) * bmb[None]).reshape(HEADS * group * n, lanes)


def group_mask(group, dates):
    g = lax.broadcasted_iota(jnp.int32, (group, 1, 256), 0)
    c = (lax.broadcasted_iota(jnp.int32, (group, 1, 256), 2) % 128) // dates
    return (g == c).astype(F32)


def temporal_bwd(advance, tiles, back_ref, pix_ref, enc_ref, cls_ref, gain_ref, w_ref, wo_ref,
                 nd_ref, kn_ref, rk_ref, v_ref, ad_ref, ac_ref, att_ref, cq_ref,
                 dw_ref, dgain_ref, dcls_ref):
    d = pix_ref.shape[-1]
    dates = pix_ref.shape[2]
    classes = cls_ref.shape[0]
    gain = gain_ref[0]
    w_ref = w_ref.at[0]
    wo_ref = wo_ref.at[0]
    x = date_sequence(pix_ref[own_tiles(tiles)], enc_ref[own_tiles(tiles)])
    rows = x.shape[0]
    bps = rows // dates
    cls = cls_ref[...].astype(F32)
    inv_c = norm_scale(cls)
    nc = (cls * inv_c * gain).astype(BF16)
    nd = nd_ref[...]
    ones = head_ones(d)
    hmb = head_mask(d).astype(BF16)
    group = 128 // dates
    back = jnp.concatenate([back_ref[k] for k in range(back_ref.shape[0])], axis=0)
    du = mm(permutation(rows, rows // classes), back).astype(BF16)
    dw_ref[:, 3 * d :] = mm(att_ref[...], du, 0, 0)
    do = mm(du, wo_ref[...], 1, 1).astype(BF16)
    qn = cq_ref[0]
    rq = cq_ref[1]
    kcn = cq_ref[2]
    rkc = cq_ref[3]
    vct = jnp.concatenate([cq_ref[4].astype(BF16)] * group, axis=0)
    kct = jnp.concatenate([kcn] * group, axis=0)
    qe = [expand_heads(p, hmb) for p in split(qn)]
    seg = same_block(128, 128, dates).astype(BF16)
    bm = group_mask(group, dates)
    bmb = bm.astype(BF16)
    qnt = jnp.concatenate([qn] * group, axis=0)
    rqt = jnp.concatenate([rq] * group, axis=0)
    rkct = jnp.concatenate([rkc] * group, axis=0)
    w = w_ref[...]
    wq, wk, wv = w[:, :d], w[:, d : 2 * d], w[:, 2 * d :]
    nct = jnp.concatenate([nc] * group, axis=0)
    dwq = jnp.zeros((d, d), F32)
    dwk = jnp.zeros((d, d), F32)
    dwv = jnp.zeros((d, d), F32)
    dnc = jnp.zeros((classes, d), F32)
    dgain = jnp.zeros((1, d), F32)
    xhat = x * norm_scale(x)
    das, dvs = [], []
    for g in range(bps // group):
        lanes = slice(g * 128, (g + 1) * 128)
        ad = ad_ref[:, lanes]
        ac = ac_ref[:, lanes]
        a2 = jnp.concatenate([ad, ac], axis=1)
        aexp = expand_patches(a2.astype(BF16), bmb)
        vst = jnp.concatenate([v_ref[lanes, :], vct], axis=0)
        doe = expand_heads(do[lanes], hmb)
        da = jnp.sum(mm(doe, vst, 1, 1).reshape(HEADS, group, classes, 256) * bm[None], axis=1)
        das.append(rounded(da.reshape(HEADS * classes, 256)))
        dvst = mm(aexp, doe, 0, 0).astype(BF16)
        dvs.append(dvst)
        dwv += mm(nd[lanes], dvst[:128], 0, 0) + mm(nct, dvst[128:], 0, 0)
    dw_ref[:, 2 * d : 3 * d] = dwv
    advance()
    for g in range(bps // group):
        lanes = slice(g * 128, (g + 1) * 128)
        a2 = jnp.concatenate([ad_ref[:, lanes], ac_ref[:, lanes]], axis=1)
        da, dvst = das[g], dvs[g]
        prod = da * a2
        dot = mm2(prod[:, :128] + prod[:, 128:], seg)
        ds = normalizer_sharpness * a2 * (da - jnp.concatenate([dot, dot], axis=1))
        kn = kn_ref[lanes, :]
        kst = jnp.concatenate([kn, kct], axis=0)
        ds = split(ds)
        dh, dl = [by_head(expand_patches(p, bmb)) for p in ds]
        kh, kl = split(kst)
        dqn = head_sum([(dh, kh), (dh, kl), (dl, kh)], hmb)
        dkst = key_back(ds, qe)
        dq = unit_back(dqn, qnt, rqt, ones)
        dk = unit_back(dkst[:128], kn, rk_ref[lanes, :], ones)
        dkc = unit_back(dkst[128:], kct, rkct, ones)
        ndg = nd[lanes]
        dwq += mm2r(nct, dq, 0, 0)
        dwk += mm2r(ndg, dk, 0, 0) + mm2r(nct, dkc, 0, 0)
        dn_k = rounded(mm2(jnp.concatenate([dk, dkc], axis=0), wk, 1, 1))
        dn = rounded(rounded(mm(dvst, wv, 1, 1)) + dn_k)
        dn_c = rounded(dn[128:] + rounded(mm2(dq, wq, 1, 1)))
        dgain += jnp.sum(dn[:128] * xhat[lanes], axis=0, keepdims=True)
        dnc += jnp.sum(dn_c.reshape(group, classes, d), axis=0)
        advance()
    dw_ref[:, :d] = dwq
    dw_ref[:, d : 2 * d] = dwk
    dgain_ref[...] = dgain + jnp.sum(dnc * cls * inv_c, axis=0, keepdims=True)
    t = dnc * gain
    dcls = inv_c * (t - cls * (inv_c * inv_c * jnp.mean(t * cls, axis=-1, keepdims=True)))
    dcls_ref[...] = dcls + jnp.sum(du.astype(F32).reshape(bps, classes, d), axis=0)


def spatial_rows(recv_ref, kinds):
    sources, rows, d = recv_ref.shape
    n = rows // kinds
    blocks = [recv_ref[s].astype(F32) for s in range(sources)]
    return jnp.concatenate(
        [blocks[s][k * n : (k + 1) * n] for k in range(kinds) for s in range(sources)], axis=0
    )


def spatial_fwd(kinds, tiles, recv_ref, gain_ref, w_ref, wo_ref, head_ref,
                u_ref, n_ref, qk_ref, r_ref, v_ref, a_ref, o_ref, hid_ref, raw_ref, sum_ref):
    d = recv_ref.shape[-1]
    gain_ref = gain_ref.at[1]
    w_ref = w_ref.at[1]
    wo_ref = wo_ref.at[1]
    u = spatial_rows(recv_ref, kinds)
    u_ref[...] = u
    rows = u.shape[0]
    n = (u * norm_scale(u) * gain_ref[...]).astype(BF16)
    n_ref[...] = n
    ones = head_ones(d)
    hmb = head_mask(d).astype(BF16)
    qkv = mm(n, w_ref[...])
    qn, rq = unit(qkv[:, :d], ones)
    kn, rk = unit(qkv[:, d : 2 * d], ones)
    v = qkv[:, 2 * d :].astype(BF16)
    qk_ref[0] = qn
    qk_ref[1] = kn
    r_ref[0] = rq
    r_ref[1] = rk
    v_ref[...] = v
    per = rows // kinds
    patches = per // (recv_ref.shape[0] * tiles)
    ri = (lax.broadcasted_iota(jnp.int32, (per, per), 0) // patches) % tiles
    ci = (lax.broadcasted_iota(jnp.int32, (per, per), 1) // patches) % tiles
    tm = jnp.concatenate([(ri == ci).astype(F32)] * HEADS, axis=0)
    outs = []
    for k in range(kinds):
        rs = slice(k * per, (k + 1) * per)
        qe = [expand_heads(p, hmb) for p in split(qn[rs])]
        e = jnp.exp(normalizer_sharpness * scores(qe, split(kn[rs]))) * tm
        a = e / jnp.sum(e, axis=-1, keepdims=True)
        a_ref[k] = a
        outs.append(head_sum([(by_head(a.astype(BF16)), v[rs])], hmb))
    o = jnp.concatenate(outs, axis=0).astype(BF16)
    o_ref[...] = o
    hid = u + mm(o, wo_ref[...])
    hid_ref[...] = hid
    raw = jnp.sum(hid * head_ref[...], axis=-1, keepdims=True)
    raw = jnp.broadcast_to(raw, (rows, 128))
    raw_ref[...] = raw
    ex = jnp.exp(logit_cap * jnp.tanh(raw / logit_cap))
    total = jnp.sum(ex.reshape(kinds, per, 128), axis=0)
    total = jnp.where(diagonal(per), total, 0.0)
    sum_ref[...] = jnp.broadcast_to(jnp.sum(total, axis=0, keepdims=True), sum_ref.shape)


def diagonal(rows):
    r = lax.broadcasted_iota(jnp.int32, (rows, 128), 0)
    return r == lax.broadcasted_iota(jnp.int32, (rows, 128), 1)


def patch_columns(label_ref, slot_ref, sources, tiles, lanes):
    first = lax.axis_index("pipe") * tiles
    count = label_ref.shape[1]
    patches = count // sources
    shape = (sources * tiles * patches, count)
    row = lax.broadcasted_iota(jnp.int32, shape, 0)
    col = lax.broadcasted_iota(jnp.int32, shape, 1)
    tile = (row // patches) % tiles
    here = col == (row // (patches * tiles)) * patches + row % patches
    slot_shape = (shape[0], lanes)
    slot_tile = (lax.broadcasted_iota(jnp.int32, slot_shape, 0) // patches) % tiles
    lane = lax.broadcasted_iota(jnp.int32, slot_shape, 1)
    labels = jnp.zeros(shape, F32)
    slots = jnp.zeros(slot_shape, F32)
    for t in range(tiles):
        values = label_ref[pl.ds(first + t, 1), :].astype(F32)
        labels = labels + jnp.where(here & (tile == t), values, 0.0)
        slots = slots + ((slot_tile == t) & (lane == slot_ref[first + t])).astype(F32)
    return jnp.broadcast_to(jnp.sum(labels, axis=-1, keepdims=True), slot_shape), slots


def spatial_bwd(after_send, kinds, tiles, total_tiles, batch_norm, tot_ref, label_ref, slot_ref, gain_ref, w_ref, wo_ref, head_ref,
                u_ref, n_ref, qk_ref, r_ref, v_ref, a_ref, o_ref, hid_ref, raw_ref,
                send_ref, dw_ref, dgain_ref, dhead_ref, loss_ref):
    d = u_ref.shape[-1]
    gain_ref = gain_ref.at[1]
    w_ref = w_ref.at[1]
    wo_ref = wo_ref.at[1]
    rows = u_ref.shape[0]
    per = rows // kinds
    sources = tot_ref.shape[0]
    total = jnp.sum(tot_ref[...], axis=0)[:1]
    total = jnp.sum(jnp.where(diagonal(per), total, 0.0), axis=-1, keepdims=True)
    total = jnp.broadcast_to(total, (per, 128))
    total = jnp.concatenate([total] * kinds, axis=0)
    th = jnp.tanh(raw_ref[...] / logit_cap)
    logits = logit_cap * th
    label, slot = patch_columns(label_ref, slot_ref, sources, tiles, 128)
    kind = lax.broadcasted_iota(jnp.int32, (rows, 128), 0) // per + lax.axis_index("inner") * kinds
    ind = (jnp.concatenate([label] * kinds, axis=0) == kind.astype(F32)).astype(F32)
    slot = jnp.concatenate([slot] * kinds, axis=0)
    loss = jnp.sum(ind * (jnp.log(total) - logits) * slot, axis=0, keepdims=True) * batch_norm
    loss_ref[...] = jnp.concatenate([loss] * (d // 128), axis=1)
    draw = (jnp.exp(logits) / total - ind) / total_tiles * (1.0 - th * th)
    dr = jnp.concatenate([draw] * (d // 128), axis=1)
    head = head_ref[...]
    head_back = mm2(jnp.broadcast_to(head, (8, d)), wo_ref[...], 1, 1)[:1]
    do = (dr * head_back).astype(BF16)
    ones = head_ones(d)
    hmb = head_mask(d).astype(BF16)
    dqs, dks, dvs = [], [], []
    for k in range(kinds):
        rs = slice(k * per, (k + 1) * per)
        a = a_ref[k]
        doe = expand_heads(do[rs], hmb)
        da = rounded(mm(doe, v_ref[rs, :], 1, 1))
        dvs.append(mm(a.astype(BF16), doe, 0, 0))
        ds = normalizer_sharpness * a * (da - jnp.sum(da * a, axis=-1, keepdims=True))
        qn = qk_ref[0, rs, :]
        kn = qk_ref[1, rs, :]
        ds = split(ds)
        dh, dl = [by_head(p) for p in ds]
        kh, kl = split(kn)
        qe = [expand_heads(p, hmb) for p in split(qn)]
        dqs.append(unit_back(head_sum([(dh, kh), (dh, kl), (dl, kh)], hmb), qn, r_ref[0, rs, :], ones))
        dks.append(unit_back(key_back(ds, qe), kn, r_ref[1, rs, :], ones))
    dq = jnp.concatenate(dqs, axis=0)
    dk = jnp.concatenate(dks, axis=0)
    dv = jnp.concatenate(dvs, axis=0).astype(BF16)
    w = w_ref[...]
    dn = rounded(rounded(mm(dv, w[:, 2 * d :], 1, 1)) + rounded(mm2(dk, w[:, d : 2 * d], 1, 1)))
    dn = rounded(dn + rounded(mm2(dq, w[:, :d], 1, 1)))
    u = u_ref[...]
    inv = norm_scale(u)
    t = dn * gain_ref[...]
    du = dr * head + inv * (t - u * (inv * inv * jnp.mean(t * u, axis=-1, keepdims=True)))
    m = per // sources
    for s in range(sources):
        parts = [du[k * per + s * m : k * per + (s + 1) * m] for k in range(kinds)]
        send_ref[s] = jnp.concatenate(parts, axis=0).astype(BF16)
    after_send()
    n = n_ref[...]
    dw_ref[:, :d] = mm2r(n, dq, 0, 0)
    dw_ref[:, d : 2 * d] = mm2r(n, dk, 0, 0)
    dw_ref[:, 2 * d : 3 * d] = mm(n, dv, 0, 0)
    col = mm2r(o_ref[...], draw, 0, 0)
    dw_ref[:, 3 * d :] = jnp.concatenate([col] * (d // 128), axis=1) * head
    dgain_ref[...] = jnp.sum(dn * u * inv, axis=0, keepdims=True)
    dhead_ref[...] = jnp.sum(dr * hid_ref[...], axis=0, keepdims=True)


MESH = pl.DeviceIdType.MESH


def enter(devices):
    barrier = pltpu.get_barrier_semaphore()
    for dev in devices:
        pl.semaphore_signal(barrier, inc=1, device_id=dev, device_id_type=MESH)
    pl.semaphore_wait(barrier, len(devices))


def push(src, dst, sems, k, dev):
    copy = pltpu.make_async_remote_copy(
        src_ref=src, dst_ref=dst, send_sem=sems[0].at[k], recv_sem=sems[1].at[k],
        device_id=dev, device_id_type=MESH,
    )
    copy.start()
    return copy


def swap(src, dst, sems, first, whole):
    count = dst.shape[0]
    me = lax.axis_index("inner")
    copies = []
    for k in range(1, count):
        dev = lax.rem(me + k, count)
        block = src if whole else src.at[dev]
        copies.append(push(block, dst.at[me], sems, first + k - 1, {"inner": dev}))
    dst[me] = src[...] if whole else src[me]
    return copies


def bring_weights(wq_ref, wo_ref, g_ref, oq_ref, oo_ref, og_ref, sems, first):
    pipe = lax.axis_index("pipe")
    dp = lax.axis_index("dp")
    core = lax.rem(dp, 2)
    far = {"pipe": 1 - pipe}
    near = {"dp": dp + 1 - 2 * core}
    half = wq_ref.shape[1] // 2
    mine = pl.ds(pl.multiple_of(core * half, half), half)
    both = ((wq_ref, oq_ref), (wo_ref, oo_ref))
    started = [
        push(src.at[0, mine], dst.at[pipe, mine], sems, first + k, far) for k, (src, dst) in enumerate(both)
    ]
    gains = push(g_ref, og_ref.at[pipe], sems, first + 4, far)
    oq_ref[pipe] = wq_ref[0]
    oo_ref[pipe] = wo_ref[0]
    og_ref[pipe] = g_ref[...]

    def pass_on(k):
        started[k].wait_recv()
        there = both[k][1].at[1 - pipe, mine]
        copy = push(there, there, sems, first + 2 + k, near)
        started.append(copy)
        copy.wait_recv()

    pass_on(0)
    gains.wait_recv()
    started.append(gains)
    return started, lambda: pass_on(1)


def total_partners():
    dp = lax.axis_index("dp")
    inner = lax.axis_index("inner")
    return [
        {"dp": dp + 1 - 2 * lax.rem(dp, 2)},
        {"pipe": 1 - lax.axis_index("pipe")},
        {"dp": dp + 2 - 4 * (dp // 2)},
        {"inner": inner + 1 - 2 * lax.rem(inner, 2)},
        {"inner": inner + 2 - 4 * (inner // 2)},
    ]


def part(bit, size):
    return pl.ds(pl.multiple_of(bit * size, size), size)


def first_hop(c, layer, dw, b0, sems):
    core = lax.rem(lax.axis_index("dp"), 2)
    rows, width = dw.shape
    half, cols = rows // 2, width // 2
    there = dw.at[part(1 - core, half), pl.ds(c * cols, cols)]
    return push(there, b0.at[c, layer], sems, 16 * c + layer, total_partners()[0])


def chunk_chain(c, early, dw0, dw1, res, started, sems, b0, a0, s1, b1, a1, s2, b2, a2, b3, a4):
    pipe = lax.axis_index("pipe")
    dp = lax.axis_index("dp")
    inner = lax.axis_index("inner")
    core = lax.rem(dp, 2)
    y = dp // 2
    rows, width = dw0.shape
    cols = width // 2
    half = rows // 2
    quarter = half // 2
    partners = total_partners()
    count = b3.shape[1] + 1
    size = quarter // count
    peers = [lax.rem(inner + k, count) for k in range(1, count)]
    base = 16 * c

    def send(dev, src, dst, sem):
        started.append(push(src, dst, sems, base + sem, dev))
        return started[-1]

    def shard(y_at, inner_at):
        return pl.ds(pl.multiple_of(core * half + y_at * quarter + inner_at * size, size), size)

    def to_core(y_at, sem):
        here = res.at[c, pl.ds(pl.multiple_of(core * half + y_at * quarter, quarter), quarter)]
        return send(partners[0], here, here, sem)

    late = first_hop(c, 0, dw0, b0, sems)
    started += [late, early]
    yield
    for k, (copy, dw) in enumerate(((late, dw0), (early, dw1))):
        copy.wait_recv()
        a0[c, k] = dw[part(core, half), pl.ds(c * cols, cols)] + b0[c, k]
    if c == 0:
        s1[0] = a0[0, 1 - pipe].astype(s1.dtype)
        hop = send(partners[1], s1.at[0], b1.at[0], 2)
    else:
        for k in range(2):
            s1[1, pl.ds(k * quarter, quarter)] = a0[1, k, part(1 - y, quarter)].astype(s1.dtype)
        hop = send(partners[2], s1.at[1], b1.at[1], 3)
    yield
    hop.wait_recv()
    if c == 0:
        a1[0] = a0[0, pipe] + b1[0].astype(F32)
        s2[0] = a1[0, part(1 - y, quarter)].astype(s2.dtype)
        hop = send(partners[2], s2.at[0], b2.at[0], 3)
    else:
        for k in range(2):
            there = pl.ds(k * quarter, quarter)
            a1[1, there] = a0[1, k, part(y, quarter)] + b1[1, there].astype(F32)
        s2[1] = a1[1, part(1 - pipe, quarter)].astype(s2.dtype)
        hop = send(partners[1], s2.at[1], b2.at[1], 2)
    yield
    hop.wait_recv()
    a2[c] = a1[c, part(y if c == 0 else pipe, quarter)] + b2[c].astype(F32)
    hops = [
        send({"inner": dev}, a2.at[c, part(dev, size)], b3.at[c, k], 4 + k) for k, dev in enumerate(peers)
    ]
    yield
    for copy in hops:
        copy.wait_recv()
    own = a2[c, part(inner, size)]
    for k in range(count - 1):
        own = own + b3[c, k]
    a4[c] = own
    here = shard(y, inner)
    res[c, here] = own
    ins = [send({"inner": dev}, a4.at[c], res.at[c, here], 7 + k) for k, dev in enumerate(peers)]
    ys = [send(partners[2], a4.at[c], res.at[c, here], 10)]
    yield
    for k in range(1, count):
        here = shard(y, lax.rem(inner + count - k, count))
        ins[k - 1].wait_recv()
        ys.append(send(partners[2], res.at[c, here], res.at[c, here], 10 + k))
    gathers = [to_core(y, 14)]
    yield
    for copy in ys:
        copy.wait_recv()
    gathers.append(to_core(1 - y, 15))
    yield
    for copy in gathers:
        copy.wait_recv()


def small_chain(dcls, dg0, dg1, dhead, loss, osmall, started, sems, x0, xs, xr):
    pipe = lax.axis_index("pipe")
    nc = dcls.shape[0]
    partners = total_partners()

    def send(k, src, dst):
        started.append(push(src, dst, sems, 32 + k, partners[k]))
        return started[-1]

    x0[...] = jnp.zeros_like(x0)
    for k, gain in enumerate((dg0, dg1)):
        x0[k, :nc, :] = dcls[...]
        x0[k, nc : nc + 1, :] = gain[...]
        x0[k, nc + 1 : nc + 2, :] = dhead[...]
        x0[k, nc + 2 : nc + 3, :] = loss[...]
    copy = send(0, x0, xr.at[pl.ds(0, 2)])
    yield
    copy.wait_recv()
    xs[pl.ds(0, 2)] = x0[...] + xr[pl.ds(0, 2)]
    copy = send(1, xs.at[1 - pipe], xr.at[2])
    yield
    copy.wait_recv()
    xs[2] = xs[pipe] + xr[2]
    for k in (3, 4, 5):
        copy = send(k - 1, xs.at[k - 1], xr.at[k])
        yield
        copy.wait_recv()
        xs[k] = xs[k - 1] + xr[k]
    osmall[...] = xs[5]


def finish(res, small, oqkv, oout, ocls, ogain, ohead, oloss):
    cols = res.shape[2]
    nc = ocls.shape[0]
    first = oqkv.shape[2] - cols
    oqkv[0, :, :cols] = res[0]
    oqkv[0, :, cols:] = res[1, :, :first]
    oout[0] = res[1, :, first:]
    ocls[...] = small[:nc, :]
    ogain[...] = small[nc : nc + 1, :]
    ohead[...] = small[nc + 1 : nc + 2, :]
    oloss[...] = small[nc + 2 : nc + 3, : oloss.shape[1]]


def small_shape(classes, width):
    return (-(-(classes + 3) // 8) * 8, width)


def total_scratch(rows, width, classes, inner_count):
    half, cols = rows // 2, width // 2
    extra = small_shape(classes, width // 4)
    return [
        pltpu.VMEM((2, 2, half, cols), F32),
        pltpu.VMEM((2, 2, half, cols), F32),
        pltpu.VMEM((2, half, cols), BF16),
        pltpu.VMEM((2, half, cols), BF16),
        pltpu.VMEM((2, half, cols), F32),
        pltpu.VMEM((2, half // 2, cols), BF16),
        pltpu.VMEM((2, half // 2, cols), BF16),
        pltpu.VMEM((2, half // 2, cols), F32),
        pltpu.VMEM((2, inner_count - 1, half // 2 // inner_count, cols), F32),
        pltpu.VMEM((2, half // 2 // inner_count, cols), F32),
        pltpu.VMEM((2,) + extra, F32),
        pltpu.VMEM((6,) + extra, F32),
        pltpu.VMEM((6,) + extra, F32),
    ]


def local(fn, outs, scalars, *args):
    specs = vmem(len(args))
    for k in scalars:
        specs[k] = pl.BlockSpec(memory_space=pltpu.SMEM)
    return pl.pallas_call(
        fn,
        out_shape=[jax.ShapeDtypeStruct(s, t) for s, t in outs],
        in_specs=specs,
        out_specs=vmem(len(outs)),
        compiler_params=params(),
    )(*args)


def date_encoding(date_days, width):
    channel = jnp.arange(width)
    frequency = jnp.exp((channel // 2 * 2).astype(F32) * (-math.log(10000.0) / width))
    phases = date_days.astype(F32)[:, :, None] * frequency
    return jnp.where(channel % 2 == 0, jnp.sin(phases), jnp.cos(phases))


def saved_shapes(rows, width):
    hq = HEADS * CLASSES
    f, b = F32, BF16
    return [((rows, width), b), ((rows, width), f), ((rows, width), f), ((rows, width), b),
            ((hq, rows), f), ((hq, rows), f), ((rows, width), b), ((5, CLASSES, width), f)]


def kept_shapes(kinds, per, width):
    srows = kinds * per
    f, b = F32, BF16
    return [((srows, width), f), ((srows, width), b), ((2, srows, width), f), ((2, srows, width), f),
            ((srows, width), b), ((kinds, HEADS * per, per), f), ((srows, width), b), ((srows, width), f),
            ((srows, 128), f)]


def grad_shapes(width):
    return [((width, 4 * width), F32), ((1, width), F32)]


def everything(tiles, kinds, total_tiles, batch_norm,
               wq_own, wo_own, g_own, pix_ref, enc_ref, count_ref, slot_ref, label_ref, cls_ref, head_ref,
               res_ref, small_ref, w_ref, wo_ref, g_ref, *refs):
    refs = list(refs)

    def take(count):
        taken, refs[:count] = refs[:count], []
        return taken

    send_ref, recv_ref, back_ref, returned_ref, sums_ref, totals_ref = take(6)
    saved = take(8)
    kept = take(9)
    dw0, dg0, dw1, dg1, dcls, dhead, loss = take(7)
    parts = take(13)
    sems = take(2)
    inner = lax.axis_index("inner")
    count = recv_ref.shape[0]
    along = total_partners()
    enter(along[:3] + [{"inner": lax.rem(inner + k, count)} for k in range(1, count)])
    started, before_out = bring_weights(wq_own, wo_own, g_own, w_ref, wo_ref, g_ref, sems, 37)
    temporal_fwd(before_out, tiles, pix_ref, enc_ref, count_ref, cls_ref, g_ref, w_ref, wo_ref, send_ref, *saved)
    copies = swap(send_ref, recv_ref, sems, 42, False)
    for copy in copies:
        copy.wait_recv()
    started += copies
    spatial_fwd(kinds, tiles, recv_ref, g_ref, w_ref, wo_ref, head_ref, *kept, sums_ref)
    copies = swap(sums_ref, totals_ref, sems, 42 + count, True)
    for copy in copies:
        copy.wait_recv()
    started += copies
    copies = []
    spatial_bwd(lambda: copies.extend(swap(back_ref, returned_ref, sems, 42 + 2 * count, False)),
                kinds, tiles, total_tiles, batch_norm, totals_ref, label_ref, slot_ref,
                g_ref, w_ref, wo_ref, head_ref, *kept, back_ref, dw1, dg1, dhead, loss)
    early = [first_hop(c, 1, dw1, parts[0], sems) for c in range(2)]
    for copy in copies:
        copy.wait_recv()
    started += copies
    chains = [
        chunk_chain(c, early[c], dw0, dw1, res_ref, started, sems, *parts[:10]) for c in range(2)
    ]
    smalls = small_chain(dcls, dg0, dg1, dhead, loss, small_ref, started, sems, *parts[10:])
    temporal_bwd(lambda: next(chains[1]), tiles, returned_ref, pix_ref, enc_ref, cls_ref, g_ref, w_ref, wo_ref, *saved, dw0, dg0, dcls)
    chains.insert(1, smalls)
    while chains:
        chains = [chain for chain in chains if next(chain, True) is None]
    for copy in started:
        copy.wait_send()


def shards(pixels, date_days, clear_count, batch_slot, labels, class_tokens, section_gain,
           segment_probe_lookup_content, section_out, head_vec):
    tiles_dev, patches_dev, dates, width = pixels.shape
    inner_count = lax.axis_size("inner")
    kinds = CLASSES // inner_count
    total_tiles = tiles_dev * lax.axis_size("dp")
    tiles = tiles_dev // 2
    rows = tiles * patches_dev * dates
    batch_norm = 1.0 / (total_tiles // MICRO * PATCHES)
    enc = date_encoding(date_days, width)
    head = head_vec.reshape(1, width)
    per = inner_count * tiles * patches_dev
    exchanged = ((inner_count, rows // inner_count, width), BF16)
    shapes = [
        ((2,) + segment_probe_lookup_content.shape[1:], BF16),
        ((2,) + section_out.shape[1:], BF16),
        ((2,) + section_gain.shape, F32),
        exchanged, exchanged, exchanged, exchanged,
        ((8, 128), F32), ((inner_count, 8, 128), F32),
    ]
    shapes += saved_shapes(rows, width) + kept_shapes(kinds, per, width) + grad_shapes(width) * 2
    shapes += [((CLASSES, width), F32), ((1, width), F32), ((1, width), F32)]
    specs = vmem(10)
    specs[5] = specs[6] = pl.BlockSpec(memory_space=pltpu.SMEM)
    sems = 42 + 3 * inner_count
    grads, small = pl.pallas_call(
        functools.partial(everything, tiles, kinds, total_tiles, batch_norm),
        out_shape=[
            jax.ShapeDtypeStruct((2, width, 2 * width), F32),
            jax.ShapeDtypeStruct(small_shape(CLASSES, width), F32),
        ],
        in_specs=specs,
        out_specs=vmem(2),
        scratch_shapes=[pltpu.VMEM(s, t) for s, t in shapes]
        + total_scratch(width, 4 * width, CLASSES, inner_count)
        + [pltpu.SemaphoreType.DMA((sems,))] * 2,
        compiler_params=params(collective_id=0, has_side_effects=True),
    )(segment_probe_lookup_content, section_out, section_gain, pixels, enc, clear_count, batch_slot,
      labels, class_tokens, head)
    gqkv, gout, gcls, ggain, ghead, gloss = local(
        finish,
        [((1, width, 3 * width), F32), ((1, width, width), F32), ((CLASSES, width), F32), ((1, width), F32),
         ((1, width), F32), ((1, MICRO), F32)], (),
        grads, small,
    )
    return gloss.reshape(MICRO), gcls, ggain, gqkv, gout, ghead.reshape(width)


def solution(mesh):
    placed = (
        P("dp", "inner", None, None),
        P("dp", None),
        P("dp"),
        P("dp"),
        P("dp", None),
        P(),
        P("pipe", None),
        P("pipe", None, None),
        P("pipe", None, None),
        P(),
    )

    def body(*args):
        tiles_dev, patches_dev, dates, width = args[0].shape
        pairs = tiles_dev // 2 * patches_dev
        sizes = tuple(mesh.shape[a] for a in ("pipe", "dp", "inner"))
        fits = sizes == (2, 4, 4) and pairs % 8 == 0 and dates == CLASSES and width == 256
        fits = fits and tiles_dev // 2 * PATCHES <= 128
        return (shards if fits else shards_general)(*args)

    return jax.shard_map(
        body,
        mesh=mesh,
        in_specs=placed,
        out_specs=(P(), P(), P("pipe", None), P("pipe", None, None), P("pipe", None, None), P()),
        check_vma=False,
    )
```

```python
import functools
import math

import jax
import jax.numpy as jnp
from jax import lax
from jax.experimental import pallas as pl
from jax.experimental.pallas import tpu as pltpu
from jax.sharding import PartitionSpec as P

HEADS = 8
CLASSES = 16
PATCHES = 48
MICRO = 4


normalizer_sharpness = 10.0
logit_cap = 15.0
norm_eps = 1e-05
head_eps = 1e-06


def matmul_f32(left_side, right_side):
    return jnp.einsum(
        "...d,de->...e",
        left_side,
        right_side.astype(jnp.bfloat16),
        preferred_element_type=jnp.float32,
    )


def rms_norm(inputs, gain_vec):
    inverse_rms = lax.rsqrt(jnp.mean(inputs * inputs, axis=-1, keepdims=True) + norm_eps)
    return inputs * inverse_rms * gain_vec


def unit_heads(values):
    shaped = values.reshape(values.shape[:-1] + (HEADS, values.shape[-1] // HEADS))
    return shaped * lax.rsqrt(jnp.sum(shaped * shaped, axis=-1, keepdims=True) + head_eps)


def temporal(pixel_rows, date_days, counts, params):
    class_init, gain_vec, w_qkv, w_out = params
    batch_count, patches, dates_max, model_width = pixel_rows.shape
    classes = class_init.shape[0]
    band_channel = jnp.arange(model_width)
    frequency = jnp.exp(
        (band_channel // 2 * 2).astype(jnp.float32) * (-math.log(10000.0) / model_width)
    )
    phases = date_days.astype(jnp.float32)[:, :, None] * frequency
    encoding = jnp.where(band_channel % 2 == 0, jnp.sin(phases), jnp.cos(phases))
    date_rows = pixel_rows.astype(jnp.float32) + encoding[:, None]
    class_rows = jnp.broadcast_to(class_init, (batch_count, patches, classes, model_width))
    sequence = jnp.concatenate([class_rows, date_rows], axis=2)
    normed = rms_norm(sequence, gain_vec).astype(jnp.bfloat16)
    probe_entry_lines = unit_heads(matmul_f32(normed[:, :, :classes], w_qkv[:, :model_width]))
    lookup_entry_lines = unit_heads(matmul_f32(normed, w_qkv[:, model_width : 2 * model_width]))
    value_rows = matmul_f32(normed, w_qkv[:, 2 * model_width :]).astype(jnp.bfloat16)
    value_heads = value_rows.reshape(
        batch_count, patches, classes + dates_max, HEADS, model_width // HEADS
    )
    affinity_logit_grid = normalizer_sharpness * jnp.einsum(
        "ohbyv,ohsyv->ohybs", probe_entry_lines, lookup_entry_lines, precision=lax.Precision.HIGHEST
    )
    position = jnp.arange(classes + dates_max)
    key_mask = (
        (position[None, :] < classes) | (position[None, :] - classes < counts[:, None])
    ).astype(jnp.float32)
    raised = jnp.exp(affinity_logit_grid) * key_mask[:, None, None, None, :]
    weights = (raised / jnp.sum(raised, axis=-1, keepdims=True)).astype(jnp.bfloat16)
    attended = jnp.einsum(
        "bphqk,bpkhe->bpqhe", weights, value_heads, preferred_element_type=jnp.float32
    )
    attended = attended.reshape(batch_count, patches, classes, model_width).astype(jnp.bfloat16)
    updated = sequence[:, :, :classes] + matmul_f32(attended, w_out)
    return jnp.swapaxes(updated, 1, 2).astype(jnp.bfloat16)


def spatial(inputs, params):
    gain_vec, w_qkv, w_out, head_vec = params
    batch_count, groups, classes, patches, model_width = inputs.shape
    class_seq = (
        jnp.swapaxes(inputs, 1, 2)
        .reshape(batch_count, classes, groups * patches, model_width)
        .astype(jnp.float32)
    )
    normed = rms_norm(class_seq, gain_vec).astype(jnp.bfloat16)
    probe_entry_lines = unit_heads(matmul_f32(normed, w_qkv[:, :model_width]))
    lookup_entry_lines = unit_heads(matmul_f32(normed, w_qkv[:, model_width : 2 * model_width]))
    value_rows = matmul_f32(normed, w_qkv[:, 2 * model_width :]).astype(jnp.bfloat16)
    value_heads = value_rows.reshape(
        batch_count, classes, groups * patches, HEADS, model_width // HEADS
    )
    affinity_logit_grid = normalizer_sharpness * jnp.einsum(
        "wisbx,wiqbx->wibsq", probe_entry_lines, lookup_entry_lines, precision=lax.Precision.HIGHEST
    )
    raised = jnp.exp(affinity_logit_grid)
    weights = (raised / jnp.sum(raised, axis=-1, keepdims=True)).astype(jnp.bfloat16)
    attended = jnp.einsum(
        "bchqk,bckhe->bcqhe", weights, value_heads, preferred_element_type=jnp.float32
    )
    attended = attended.reshape(batch_count, classes, groups * patches, model_width).astype(
        jnp.bfloat16
    )
    hidden = class_seq + matmul_f32(attended, w_out)
    raw_logits = jnp.einsum("bcpd,d->bcp", hidden, head_vec, precision=lax.Precision.HIGHEST)
    logits = logit_cap * jnp.tanh(raw_logits / logit_cap)
    return logits.reshape(batch_count, classes, groups, patches)


def shards_general(
    pixels,
    date_days,
    clear_count,
    batch_slot,
    labels,
    class_tokens,
    section_gain,
    segment_probe_lookup_content,
    section_out,
    head_vec,
):
    tiles_dev = pixels.shape[0]
    patches_dev = pixels.shape[1]
    model_width = pixels.shape[3]
    inner_count = lax.axis_size("inner")
    classes_dev = CLASSES // inner_count
    total_tiles = tiles_dev * lax.axis_size("dp")
    my_group = lax.axis_index("inner")
    class_ids = my_group * classes_dev + jnp.arange(classes_dev, dtype=jnp.int32)
    batch_norm = 1.0 / (total_tiles // MICRO * PATCHES)
    gains, qkv_all, out_all = (
        lax.all_gather(section_gain, "pipe", axis=0, tiled=True),
        lax.all_gather(
            segment_probe_lookup_content.astype(jnp.float32), "pipe", axis=0, tiled=True
        ),
        lax.all_gather(section_out.astype(jnp.float32), "pipe", axis=0, tiled=True),
    )
    pipe_pos = lax.axis_index("pipe")
    half_tiles = tiles_dev // 2
    first_params = (class_tokens.astype(jnp.float32), gains[0], qkv_all[0], out_all[0])
    second_params = (gains[1], qkv_all[1], out_all[1], head_vec)
    fold_shape = (1, inner_count, classes_dev, patches_dev, model_width)
    first_gradients = jax.tree.map(jnp.zeros_like, first_params)
    grads_second = jax.tree.map(jnp.zeros_like, second_params)
    loss_vec = jnp.zeros((MICRO,), jnp.float32)
    for tile_step in range(half_tiles):
        start = pipe_pos * half_tiles + tile_step
        single_pixel = lax.dynamic_slice_in_dim(pixels, start, 1, 0)
        days_one = lax.dynamic_slice_in_dim(date_days, start, 1, 0)
        count_one = lax.dynamic_slice_in_dim(clear_count, start, 1, 0)
        label_one = lax.dynamic_slice_in_dim(labels, start, 1, 0)
        slot_one = lax.dynamic_slice_in_dim(batch_slot, start, 1, 0)
        encoded, pull_first = jax.vjp(
            lambda params: temporal(single_pixel, days_one, count_one, params), first_params
        )
        arrived = lax.all_to_all(
            encoded.reshape(fold_shape), "inner", split_axis=1, concat_axis=1, tiled=True
        )
        logits, pull_second = jax.vjp(spatial, arrived, second_params)
        exp_logits = jnp.exp(logits)
        class_total = lax.psum(jnp.sum(exp_logits, axis=1), "inner")
        label_rows = label_one.reshape(1, 1, inner_count, patches_dev)
        indicator_rows = (label_rows == class_ids[None, :, None, None]).astype(jnp.float32)
        dlogit = (exp_logits / class_total[:, None] - indicator_rows) / total_tiles
        grad_in, grad_two = pull_second(dlogit)
        returned = lax.all_to_all(grad_in, "inner", split_axis=1, concat_axis=1, tiled=True)
        (derivative_lone,) = pull_first(returned.reshape(encoded.shape))
        first_gradients = jax.tree.map(
            lambda total, extra: total + extra, first_gradients, derivative_lone
        )
        grads_second = jax.tree.map(lambda total, extra: total + extra, grads_second, grad_two)
        loss_term = jnp.sum(indicator_rows * (jnp.log(class_total)[:, None] - logits)) * batch_norm
        loss_vec = loss_vec + loss_term * (jnp.arange(MICRO) == slot_one[0]).astype(jnp.float32)
    stacked = (
        jnp.stack([first_gradients[1], grads_second[0]]),
        jnp.stack([first_gradients[2], grads_second[1]]),
        jnp.stack([first_gradients[3], grads_second[2]]),
        first_gradients[0],
        grads_second[3],
        loss_vec,
    )
    summed = lax.psum(
        (stacked[0], stacked[1], stacked[2], stacked[3], stacked[4], stacked[5]),
        ("pipe", "dp", "inner"),
    )
    gain_grad = lax.dynamic_slice_in_dim(summed[0], pipe_pos, 1, 0)
    qkv_grad = lax.dynamic_slice_in_dim(summed[1], pipe_pos, 1, 0)
    out_grad = lax.dynamic_slice_in_dim(summed[2], pipe_pos, 1, 0)
    return (summed[5], summed[3], gain_grad, qkv_grad, out_grad, summed[4])


F32 = jnp.float32
BF16 = jnp.bfloat16
VMEM_LIMIT = 56 * 2**20


def params(**kw):
    return pltpu.CompilerParams(vmem_limit_bytes=VMEM_LIMIT, **kw)


def vmem(count):
    return [pl.BlockSpec(memory_space=pltpu.VMEM)] * count


def mm(a, b, ca=1, cb=0):
    return lax.dot_general(a, b, (((ca,), (cb,)), ((), ())), preferred_element_type=F32)


def split(a):
    hi = a.astype(BF16)
    return hi, (a - hi.astype(F32)).astype(BF16)


def mm2(a, b, ca=1, cb=0):
    hi, lo = split(a)
    return mm(hi, b, ca, cb) + mm(lo, b, ca, cb)


def mm2r(a, b, ca=1, cb=0):
    hi, lo = split(b)
    return mm(a, hi, ca, cb) + mm(a, lo, ca, cb)


def mm3(a, b, ca=1, cb=0):
    ah, al = split(a)
    bh, bl = split(b)
    return mm(ah, bh, ca, cb) + (mm(ah, bl, ca, cb) + mm(al, bh, ca, cb))


def same_block(rows, cols, size):
    r = lax.broadcasted_iota(jnp.int32, (rows, cols), 0) // size
    c = lax.broadcasted_iota(jnp.int32, (rows, cols), 1) // size
    return (r == c).astype(F32)


def head_ones(width):
    return same_block(width, width, width // HEADS).astype(BF16)


def head_mask(width):
    h = lax.broadcasted_iota(jnp.int32, (HEADS, 1, width), 0)
    c = lax.broadcasted_iota(jnp.int32, (HEADS, 1, width), 2) // (width // HEADS)
    return (h == c).astype(F32)


def unit(x, ones):
    r = lax.rsqrt(mm2(x * x, ones) + head_eps)
    return x * r, r


def unit_back(dxn, xn, r, ones):
    return r * (dxn - xn * mm2(dxn * xn, ones))


def norm_scale(x):
    return lax.rsqrt(jnp.mean(x * x, axis=-1, keepdims=True) + norm_eps)


def rounded(x):
    return x.astype(BF16).astype(F32)


def expand_heads(x, hmb):
    n, d = x.shape
    return (x[None] * hmb).reshape(HEADS * n, d)


def head_sum(pairs, hmb):
    out = None
    for h in range(HEADS):
        for a, b in pairs:
            term = mm(a[h], b * hmb[h])
            out = term if out is None else out + term
    return out


def by_head(x):
    n = x.shape[0] // HEADS
    return [x[h * n : (h + 1) * n] for h in range(HEADS)]


def scores(qs, ks):
    return mm(qs[0], ks[0], 1, 1) + (mm(qs[0], ks[1], 1, 1) + mm(qs[1], ks[0], 1, 1))


def key_back(ds, qs):
    d = qs[0].shape[1]
    both = mm(ds[0], jnp.concatenate(qs, axis=1), 0, 0)
    return both[:, :d] + (both[:, d:] + mm(ds[1], qs[0], 0, 0))


def permutation(n, outer):
    inner = n // outer
    r = lax.broadcasted_iota(jnp.int32, (n, n), 0)
    c = lax.broadcasted_iota(jnp.int32, (n, n), 1)
    return (c == (r % inner) * outer + r // inner).astype(F32).astype(BF16)


def date_sequence(pix, enc):
    return (pix.astype(F32) + enc[:, None]).reshape(-1, pix.shape[-1])


def own_tiles(tiles):
    return pl.ds(lax.axis_index("pipe") * tiles, tiles)


def clear_mask(count_ref, tiles, rows, dates):
    lane = lax.broadcasted_iota(jnp.int32, (1, rows), 1)
    first = lax.axis_index("pipe") * tiles
    mask = jnp.zeros((1, rows), F32)
    for t in range(tiles):
        clear = (lane // (rows // tiles) == t) & (lane % dates < count_ref[first + t])
        mask = mask + clear.astype(F32)
    return mask


def temporal_fwd(before_out, tiles, pix_ref, enc_ref, count_ref, cls_ref, gain_ref, w_ref, wo_ref,
                 send_ref, nd_ref, kn_ref, rk_ref, v_ref, ad_ref, ac_ref, att_ref, cq_ref):
    d = pix_ref.shape[-1]
    dates = pix_ref.shape[2]
    classes = cls_ref.shape[0]
    gain = gain_ref[0]
    w_ref = w_ref.at[0]
    wo_ref = wo_ref.at[0]
    x = date_sequence(pix_ref[own_tiles(tiles)], enc_ref[own_tiles(tiles)])
    rows = x.shape[0]
    bps = rows // dates
    mask = clear_mask(count_ref, tiles, rows, dates)
    nd = (x * norm_scale(x) * gain).astype(BF16)
    nd_ref[...] = nd
    cls = cls_ref[...].astype(F32)
    nc = (cls * norm_scale(cls) * gain).astype(BF16)
    ones = head_ones(d)
    hmb = head_mask(d).astype(BF16)
    kv = mm(nd, w_ref[:, d:])
    qkvc = mm(nc, w_ref[...])
    kn, rk = unit(kv[:, :d], ones)
    kn_ref[...] = kn
    rk_ref[...] = rk
    v = kv[:, d:].astype(BF16)
    v_ref[...] = v
    qn, rq = unit(qkvc[:, :d], ones)
    kcn, rkc = unit(qkvc[:, d : 2 * d], ones)
    vc = qkvc[:, 2 * d :].astype(BF16)
    cq_ref[0] = qn
    cq_ref[1] = rq
    cq_ref[2] = kcn
    cq_ref[3] = rkc
    cq_ref[4] = vc.astype(F32)
    group = 128 // dates
    qe = [expand_heads(p, hmb) for p in split(qn)]
    kct = jnp.concatenate([kcn] * group, axis=0)
    ed = jnp.exp(normalizer_sharpness * scores(qe, split(kn))) * mask
    ec = jnp.exp(normalizer_sharpness * scores(qe, split(kct)))
    seg = same_block(128, 128, dates).astype(BF16)
    sum_c = mm2(ec, seg)
    vct = jnp.concatenate([vc] * group, axis=0)
    bmb = group_mask(group, dates).astype(BF16)
    atts = []
    for g in range(bps // group):
        lanes = slice(g * 128, (g + 1) * 128)
        e = ed[:, lanes]
        den = mm2(e, seg) + sum_c
        ad = e / den
        ac = ec / den
        ad_ref[:, lanes] = ad
        ac_ref[:, lanes] = ac
        a2 = jnp.concatenate([ad, ac], axis=1).astype(BF16)
        vst = jnp.concatenate([v[lanes], vct], axis=0)
        atts.append(head_sum([(by_head(expand_patches(a2, bmb)), vst)], hmb))
    att = jnp.concatenate(atts, axis=0).astype(BF16)
    att_ref[...] = att
    before_out()
    upd = jnp.concatenate([cls] * bps, axis=0) + mm(att, wo_ref[...])
    send = mm(permutation(rows, classes), upd.astype(BF16)).astype(BF16)
    part = send_ref.shape[1]
    for k in range(send_ref.shape[0]):
        send_ref[k] = send[k * part : (k + 1) * part]


def expand_patches(x, bmb):
    group, _, lanes = bmb.shape
    n = x.shape[0] // HEADS
    return (x.reshape(HEADS, 1, n, lanes) * bmb[None]).reshape(HEADS * group * n, lanes)


def group_mask(group, dates):
    g = lax.broadcasted_iota(jnp.int32, (group, 1, 256), 0)
    c = (lax.broadcasted_iota(jnp.int32, (group, 1, 256), 2) % 128) // dates
    return (g == c).astype(F32)


def temporal_bwd(arrive, tiles, back_ref, pix_ref, enc_ref, cls_ref, gain_ref, w_ref, wo_ref,
                 nd_ref, kn_ref, rk_ref, v_ref, ad_ref, ac_ref, att_ref, cq_ref,
                 dw_ref, dgain_ref, dcls_ref):
    d = pix_ref.shape[-1]
    dates = pix_ref.shape[2]
    classes = cls_ref.shape[0]
    gain = gain_ref[0]
    w_ref = w_ref.at[0]
    wo_ref = wo_ref.at[0]
    x = date_sequence(pix_ref[own_tiles(tiles)], enc_ref[own_tiles(tiles)])
    rows = x.shape[0]
    bps = rows // dates
    cls = cls_ref[...].astype(F32)
    inv_c = norm_scale(cls)
    nc = (cls * inv_c * gain).astype(BF16)
    nd = nd_ref[...]
    ones = head_ones(d)
    hmb = head_mask(d).astype(BF16)
    group = 128 // dates
    qn = cq_ref[0]
    rq = cq_ref[1]
    kcn = cq_ref[2]
    rkc = cq_ref[3]
    vct = jnp.concatenate([cq_ref[4].astype(BF16)] * group, axis=0)
    kct = jnp.concatenate([kcn] * group, axis=0)
    qe = [expand_heads(p, hmb) for p in split(qn)]
    seg = same_block(128, 128, dates).astype(BF16)
    bm = group_mask(group, dates)
    bmb = bm.astype(BF16)
    qnt = jnp.concatenate([qn] * group, axis=0)
    rqt = jnp.concatenate([rq] * group, axis=0)
    rkct = jnp.concatenate([rkc] * group, axis=0)
    w = w_ref[...]
    wq, wk, wv = w[:, :d], w[:, d : 2 * d], w[:, 2 * d :]
    nct = jnp.concatenate([nc] * group, axis=0)
    dwq = jnp.zeros((d, d), F32)
    dwk = jnp.zeros((d, d), F32)
    dwv = jnp.zeros((d, d), F32)
    dnc = jnp.zeros((classes, d), F32)
    dgain = jnp.zeros((1, d), F32)
    xhat = x * norm_scale(x)
    order = permutation(rows, rows // classes)
    arrive()
    back = jnp.concatenate([back_ref[k] for k in range(back_ref.shape[0])], axis=0)
    du = mm(order, back).astype(BF16)
    dw_ref[:, 3 * d :] = mm(att_ref[...], du, 0, 0)
    do = mm(du, wo_ref[...], 1, 1).astype(BF16)
    for g in range(bps // group):
        lanes = slice(g * 128, (g + 1) * 128)
        ad = ad_ref[:, lanes]
        ac = ac_ref[:, lanes]
        a2 = jnp.concatenate([ad, ac], axis=1)
        aexp = expand_patches(a2.astype(BF16), bmb)
        vst = jnp.concatenate([v_ref[lanes, :], vct], axis=0)
        doe = expand_heads(do[lanes], hmb)
        da = jnp.sum(mm(doe, vst, 1, 1).reshape(HEADS, group, classes, 256) * bm[None], axis=1)
        da = rounded(da.reshape(HEADS * classes, 256))
        dvst = mm(aexp, doe, 0, 0).astype(BF16)
        prod = da * a2
        dot = mm2(prod[:, :128] + prod[:, 128:], seg)
        ds = normalizer_sharpness * a2 * (da - jnp.concatenate([dot, dot], axis=1))
        kn = kn_ref[lanes, :]
        kst = jnp.concatenate([kn, kct], axis=0)
        ds = split(ds)
        dh, dl = [by_head(expand_patches(p, bmb)) for p in ds]
        kh, kl = split(kst)
        dqn = head_sum([(dh, kh), (dh, kl), (dl, kh)], hmb)
        dkst = key_back(ds, qe)
        dq = unit_back(dqn, qnt, rqt, ones)
        dk = unit_back(dkst[:128], kn, rk_ref[lanes, :], ones)
        dkc = unit_back(dkst[128:], kct, rkct, ones)
        ndg = nd[lanes]
        dwq += mm2r(nct, dq, 0, 0)
        dwk += mm2r(ndg, dk, 0, 0) + mm2r(nct, dkc, 0, 0)
        dwv += mm(ndg, dvst[:128], 0, 0) + mm(nct, dvst[128:], 0, 0)
        dn_k = rounded(mm2(jnp.concatenate([dk, dkc], axis=0), wk, 1, 1))
        dn = rounded(rounded(mm(dvst, wv, 1, 1)) + dn_k)
        dn_c = rounded(dn[128:] + rounded(mm2(dq, wq, 1, 1)))
        dgain += jnp.sum(dn[:128] * xhat[lanes], axis=0, keepdims=True)
        dnc += jnp.sum(dn_c.reshape(group, classes, d), axis=0)
    dw_ref[:, :d] = dwq
    dw_ref[:, d : 2 * d] = dwk
    dw_ref[:, 2 * d : 3 * d] = dwv
    dgain_ref[...] = dgain + jnp.sum(dnc * cls * inv_c, axis=0, keepdims=True)
    t = dnc * gain
    dcls = inv_c * (t - cls * (inv_c * inv_c * jnp.mean(t * cls, axis=-1, keepdims=True)))
    dcls_ref[...] = dcls + jnp.sum(du.astype(F32).reshape(bps, classes, d), axis=0)


def spatial_rows(recv_ref, kinds):
    sources, rows, d = recv_ref.shape
    n = rows // kinds
    blocks = [recv_ref[s].astype(F32) for s in range(sources)]
    return jnp.concatenate(
        [blocks[s][k * n : (k + 1) * n] for k in range(kinds) for s in range(sources)], axis=0
    )


def spatial_fwd(kinds, tiles, recv_ref, gain_ref, w_ref, wo_ref, head_ref,
                u_ref, n_ref, qk_ref, r_ref, v_ref, a_ref, o_ref, hid_ref, raw_ref, sum_ref):
    d = recv_ref.shape[-1]
    gain_ref = gain_ref.at[1]
    w_ref = w_ref.at[1]
    wo_ref = wo_ref.at[1]
    u = spatial_rows(recv_ref, kinds)
    u_ref[...] = u
    rows = u.shape[0]
    n = (u * norm_scale(u) * gain_ref[...]).astype(BF16)
    n_ref[...] = n
    ones = head_ones(d)
    hmb = head_mask(d).astype(BF16)
    qkv = mm(n, w_ref[...])
    qn, rq = unit(qkv[:, :d], ones)
    kn, rk = unit(qkv[:, d : 2 * d], ones)
    v = qkv[:, 2 * d :].astype(BF16)
    qk_ref[0] = qn
    qk_ref[1] = kn
    r_ref[0] = rq
    r_ref[1] = rk
    v_ref[...] = v
    per = rows // kinds
    patches = per // (recv_ref.shape[0] * tiles)
    ri = (lax.broadcasted_iota(jnp.int32, (per, per), 0) // patches) % tiles
    ci = (lax.broadcasted_iota(jnp.int32, (per, per), 1) // patches) % tiles
    tm = jnp.concatenate([(ri == ci).astype(F32)] * HEADS, axis=0)
    outs = []
    for k in range(kinds):
        rs = slice(k * per, (k + 1) * per)
        qe = [expand_heads(p, hmb) for p in split(qn[rs])]
        e = jnp.exp(normalizer_sharpness * scores(qe, split(kn[rs]))) * tm
        a = e / jnp.sum(e, axis=-1, keepdims=True)
        a_ref[k] = a
        outs.append(head_sum([(by_head(a.astype(BF16)), v[rs])], hmb))
    o = jnp.concatenate(outs, axis=0).astype(BF16)
    o_ref[...] = o
    hid = u + mm(o, wo_ref[...])
    hid_ref[...] = hid
    raw = jnp.sum(hid * head_ref[...], axis=-1, keepdims=True)
    raw = jnp.broadcast_to(raw, (rows, 128))
    raw_ref[...] = raw
    ex = jnp.exp(logit_cap * jnp.tanh(raw / logit_cap))
    total = jnp.sum(ex.reshape(kinds, per, 128), axis=0)
    total = jnp.where(diagonal(per), total, 0.0)
    sum_ref[...] = jnp.broadcast_to(jnp.sum(total, axis=0, keepdims=True), sum_ref.shape)


def diagonal(rows):
    r = lax.broadcasted_iota(jnp.int32, (rows, 128), 0)
    return r == lax.broadcasted_iota(jnp.int32, (rows, 128), 1)


def patch_columns(label_ref, slot_ref, sources, tiles, lanes):
    first = lax.axis_index("pipe") * tiles
    count = label_ref.shape[1]
    patches = count // sources
    shape = (sources * tiles * patches, count)
    row = lax.broadcasted_iota(jnp.int32, shape, 0)
    col = lax.broadcasted_iota(jnp.int32, shape, 1)
    tile = (row // patches) % tiles
    here = col == (row // (patches * tiles)) * patches + row % patches
    slot_shape = (shape[0], lanes)
    slot_tile = (lax.broadcasted_iota(jnp.int32, slot_shape, 0) // patches) % tiles
    lane = lax.broadcasted_iota(jnp.int32, slot_shape, 1)
    labels = jnp.zeros(shape, F32)
    slots = jnp.zeros(slot_shape, F32)
    for t in range(tiles):
        values = label_ref[pl.ds(first + t, 1), :].astype(F32)
        labels = labels + jnp.where(here & (tile == t), values, 0.0)
        slots = slots + ((slot_tile == t) & (lane == slot_ref[first + t])).astype(F32)
    return jnp.broadcast_to(jnp.sum(labels, axis=-1, keepdims=True), slot_shape), slots


def spatial_bwd(after_send, kinds, tiles, total_tiles, batch_norm, tot_ref, label_ref, slot_ref, gain_ref, w_ref, wo_ref, head_ref,
                u_ref, n_ref, qk_ref, r_ref, v_ref, a_ref, o_ref, hid_ref, raw_ref,
                send_ref, dw_ref, dgain_ref, dhead_ref, loss_ref):
    d = u_ref.shape[-1]
    gain_ref = gain_ref.at[1]
    w_ref = w_ref.at[1]
    wo_ref = wo_ref.at[1]
    rows = u_ref.shape[0]
    per = rows // kinds
    sources = tot_ref.shape[0]
    total = jnp.sum(tot_ref[...], axis=0)[:1]
    total = jnp.sum(jnp.where(diagonal(per), total, 0.0), axis=-1, keepdims=True)
    total = jnp.broadcast_to(total, (per, 128))
    total = jnp.concatenate([total] * kinds, axis=0)
    th = jnp.tanh(raw_ref[...] / logit_cap)
    logits = logit_cap * th
    label, slot = patch_columns(label_ref, slot_ref, sources, tiles, 128)
    kind = lax.broadcasted_iota(jnp.int32, (rows, 128), 0) // per + lax.axis_index("inner") * kinds
    ind = (jnp.concatenate([label] * kinds, axis=0) == kind.astype(F32)).astype(F32)
    slot = jnp.concatenate([slot] * kinds, axis=0)
    loss = jnp.sum(ind * (jnp.log(total) - logits) * slot, axis=0, keepdims=True) * batch_norm
    loss_ref[...] = jnp.concatenate([loss] * (d // 128), axis=1)
    draw = (jnp.exp(logits) / total - ind) / total_tiles * (1.0 - th * th)
    dr = jnp.concatenate([draw] * (d // 128), axis=1)
    head = head_ref[...]
    head_back = mm2(jnp.broadcast_to(head, (8, d)), wo_ref[...], 1, 1)[:1]
    do = (dr * head_back).astype(BF16)
    ones = head_ones(d)
    hmb = head_mask(d).astype(BF16)
    dqs, dks, dvs = [], [], []
    for k in range(kinds):
        rs = slice(k * per, (k + 1) * per)
        a = a_ref[k]
        doe = expand_heads(do[rs], hmb)
        da = rounded(mm(doe, v_ref[rs, :], 1, 1))
        dvs.append(mm(a.astype(BF16), doe, 0, 0))
        ds = normalizer_sharpness * a * (da - jnp.sum(da * a, axis=-1, keepdims=True))
        qn = qk_ref[0, rs, :]
        kn = qk_ref[1, rs, :]
        ds = split(ds)
        dh, dl = [by_head(p) for p in ds]
        kh, kl = split(kn)
        qe = [expand_heads(p, hmb) for p in split(qn)]
        dqs.append(unit_back(head_sum([(dh, kh), (dh, kl), (dl, kh)], hmb), qn, r_ref[0, rs, :], ones))
        dks.append(unit_back(key_back(ds, qe), kn, r_ref[1, rs, :], ones))
    dq = jnp.concatenate(dqs, axis=0)
    dk = jnp.concatenate(dks, axis=0)
    dv = jnp.concatenate(dvs, axis=0).astype(BF16)
    w = w_ref[...]
    dn = rounded(rounded(mm(dv, w[:, 2 * d :], 1, 1)) + rounded(mm2(dk, w[:, d : 2 * d], 1, 1)))
    dn = rounded(dn + rounded(mm2(dq, w[:, :d], 1, 1)))
    u = u_ref[...]
    inv = norm_scale(u)
    t = dn * gain_ref[...]
    du = dr * head + inv * (t - u * (inv * inv * jnp.mean(t * u, axis=-1, keepdims=True)))
    m = per // sources
    for s in range(sources):
        parts = [du[k * per + s * m : k * per + (s + 1) * m] for k in range(kinds)]
        send_ref[s] = jnp.concatenate(parts, axis=0).astype(BF16)
    after_send()
    n = n_ref[...]
    dw_ref[:, :d] = mm2r(n, dq, 0, 0)
    dw_ref[:, d : 2 * d] = mm2r(n, dk, 0, 0)
    dw_ref[:, 2 * d : 3 * d] = mm(n, dv, 0, 0)
    col = mm2r(o_ref[...], draw, 0, 0)
    dw_ref[:, 3 * d :] = jnp.concatenate([col] * (d // 128), axis=1) * head
    dgain_ref[...] = jnp.sum(dn * u * inv, axis=0, keepdims=True)
    dhead_ref[...] = jnp.sum(dr * hid_ref[...], axis=0, keepdims=True)


MESH = pl.DeviceIdType.MESH


def enter(devices):
    barrier = pltpu.get_barrier_semaphore()
    for dev in devices:
        pl.semaphore_signal(barrier, inc=1, device_id=dev, device_id_type=MESH)
    pl.semaphore_wait(barrier, len(devices))


def push(src, dst, sems, k, dev):
    copy = pltpu.make_async_remote_copy(
        src_ref=src, dst_ref=dst, send_sem=sems[0].at[k], recv_sem=sems[1].at[k],
        device_id=dev, device_id_type=MESH,
    )
    copy.start()
    return copy


def swap(src, dst, sems, first, whole):
    count = dst.shape[0]
    me = lax.axis_index("inner")
    copies = []
    for k in range(1, count):
        dev = lax.rem(me + k, count)
        block = src if whole else src.at[dev]
        copies.append(push(block, dst.at[me], sems, first + k - 1, {"inner": dev}))
    dst[me] = src[...] if whole else src[me]
    return copies


def bring_weights(wq_ref, wo_ref, g_ref, oq_ref, oo_ref, og_ref, sems, first):
    pipe = lax.axis_index("pipe")
    dp = lax.axis_index("dp")
    core = lax.rem(dp, 2)
    far = {"pipe": 1 - pipe}
    near = {"dp": dp + 1 - 2 * core}
    half = wq_ref.shape[1] // 2
    mine = pl.ds(pl.multiple_of(core * half, half), half)
    both = ((wq_ref, oq_ref), (wo_ref, oo_ref))
    started = [
        push(src.at[0, mine], dst.at[pipe, mine], sems, first + k, far) for k, (src, dst) in enumerate(both)
    ]
    gains = push(g_ref, og_ref.at[pipe], sems, first + 4, far)
    oq_ref[pipe] = wq_ref[0]
    oo_ref[pipe] = wo_ref[0]
    og_ref[pipe] = g_ref[...]

    def pass_on(k):
        started[k].wait_recv()
        there = both[k][1].at[1 - pipe, mine]
        copy = push(there, there, sems, first + 2 + k, near)
        started.append(copy)
        copy.wait_recv()

    pass_on(0)
    gains.wait_recv()
    started.append(gains)
    return started, lambda: pass_on(1)


def total_partners():
    dp = lax.axis_index("dp")
    inner = lax.axis_index("inner")
    return [
        {"dp": dp + 1 - 2 * lax.rem(dp, 2)},
        {"pipe": 1 - lax.axis_index("pipe")},
        {"dp": dp + 2 - 4 * (dp // 2)},
        {"inner": inner + 1 - 2 * lax.rem(inner, 2)},
        {"inner": inner + 2 - 4 * (inner // 2)},
    ]


def first_hop(layer, dw, b0, sems):
    core = lax.rem(lax.axis_index("dp"), 2)
    rows, width = dw.shape
    half, cols = rows // 2, width // 2
    there = pl.ds(pl.multiple_of((1 - core) * half, half), half)
    return [
        push(dw.at[there, pl.ds(c * cols, cols)], b0.at[c, layer], sems, 16 * c + layer, total_partners()[0])
        for c in range(2)
    ]


def total(early, dw0, dw1, dcls, dg0, dg1, dhead, loss, res, osmall,
          b0, a0, s1, b1, a1, s2, b2, a2, b3, a4, x0, xs, xr, sems):
    pipe = lax.axis_index("pipe")
    dp = lax.axis_index("dp")
    inner = lax.axis_index("inner")
    core = lax.rem(dp, 2)
    y = dp // 2
    rows, width = dw0.shape
    cols = width // 2
    partners = total_partners()
    started = []

    def send(k, src, dst, sem):
        started.append(push(src, dst, sems, sem, partners[k]))
        return started[-1]

    def part(bit, size):
        return pl.ds(pl.multiple_of(bit * size, size), size)

    def span(c):
        return pl.ds(c * cols, cols)

    nc = dcls.shape[0]
    x0[...] = jnp.zeros_like(x0)
    for k, gain in enumerate((dg0, dg1)):
        x0[k, :nc, :] = dcls[...]
        x0[k, nc : nc + 1, :] = gain[...]
        x0[k, nc + 1 : nc + 2, :] = dhead[...]
        x0[k, nc + 2 : nc + 3, :] = loss[...]
    half = rows // 2
    quarter = half // 2
    late = first_hop(0, dw0, b0, sems)
    started += early + late
    going = list(zip(late, early))
    small = send(0, x0, xr.at[pl.ds(0, 2)], 32)
    mine = part(core, half)
    hops = []
    for c in range(2):
        for copy in going[c]:
            copy.wait_recv()
        for k, dw in enumerate((dw0, dw1)):
            a0[c, k] = dw[mine, span(c)] + b0[c, k]
        if c == 0:
            s1[0] = a0[0, 1 - pipe].astype(s1.dtype)
            hops.append(send(1, s1.at[0], b1.at[0], 2))
        else:
            for k in range(2):
                s1[1, pl.ds(k * quarter, quarter)] = a0[1, k, part(1 - y, quarter)].astype(s1.dtype)
            hops.append(send(2, s1.at[1], b1.at[1], 19))
    small.wait_recv()
    xs[pl.ds(0, 2)] = x0[...] + xr[pl.ds(0, 2)]
    small = send(1, xs.at[1 - pipe], xr.at[2], 33)
    hops[0].wait_recv()
    a1[0] = a0[0, pipe] + b1[0].astype(F32)
    s2[0] = a1[0, part(1 - y, quarter)].astype(s2.dtype)
    hops[0] = send(2, s2.at[0], b2.at[0], 3)
    hops[1].wait_recv()
    for k in range(2):
        there = pl.ds(k * quarter, quarter)
        a1[1, there] = a0[1, k, part(y, quarter)] + b1[1, there].astype(F32)
    s2[1] = a1[1, part(1 - pipe, quarter)].astype(s2.dtype)
    hops[1] = send(1, s2.at[1], b2.at[1], 18)
    small.wait_recv()
    xs[2] = xs[pipe] + xr[2]
    small = send(2, xs.at[2], xr.at[3], 34)
    count = b3.shape[1] + 1
    size = quarter // count
    peers = [lax.rem(inner + k, count) for k in range(1, count)]
    hops_in = [[], []]
    for c, bit in enumerate((y, pipe)):
        hops[c].wait_recv()
        a2[c] = a1[c, part(bit, quarter)] + b2[c].astype(F32)
        for k, dev in enumerate(peers):
            copy = push(a2.at[c, part(dev, size)], b3.at[c, k], sems, 16 * c + 4 + k, {"inner": dev})
            hops_in[c].append(copy)
    small.wait_recv()
    xs[3] = xs[2] + xr[3]
    small = send(3, xs.at[3], xr.at[4], 35)

    def shard(y_at, inner_at):
        return pl.ds(pl.multiple_of(core * half + y_at * quarter + inner_at * size, size), size)

    ins = [[], []]
    ys = [[], []]
    for c in range(2):
        for copy in hops_in[c]:
            copy.wait_recv()
        own = a2[c, part(inner, size)]
        for k in range(count - 1):
            own = own + b3[c, k]
        a4[c] = own
        here = shard(y, inner)
        res[c, here] = own
        for k, dev in enumerate(peers):
            ins[c].append(push(a4.at[c], res.at[c, here], sems, 16 * c + 7 + k, {"inner": dev}))
        ys[c].append(send(2, a4.at[c], res.at[c, here], 16 * c + 10))
    started += hops_in[0] + hops_in[1] + ins[0] + ins[1]
    small.wait_recv()
    xs[4] = xs[3] + xr[4]
    small = send(4, xs.at[4], xr.at[5], 36)
    for k in range(1, count):
        here = shard(y, lax.rem(inner + count - k, count))
        for c in range(2):
            ins[c][k - 1].wait_recv()
            ys[c].append(send(2, res.at[c, here], res.at[c, here], 16 * c + 10 + k))
    gathers = []

    def to_core(c, y_at, sem):
        here = pl.ds(pl.multiple_of(core * half + y_at * quarter, quarter), quarter)
        gathers.append(send(0, res.at[c, here], res.at[c, here], 16 * c + sem))

    for c in range(2):
        to_core(c, y, 14)
    small.wait_recv()
    xs[5] = xs[4] + xr[5]
    for c in range(2):
        for copy in ys[c]:
            copy.wait_recv()
        to_core(c, 1 - y, 15)
    osmall[...] = xs[5]
    for copy in gathers:
        copy.wait_recv()
    for copy in started:
        copy.wait_send()


def finish(res, small, oqkv, oout, ocls, ogain, ohead, oloss):
    cols = res.shape[2]
    nc = ocls.shape[0]
    first = oqkv.shape[2] - cols
    oqkv[0, :, :cols] = res[0]
    oqkv[0, :, cols:] = res[1, :, :first]
    oout[0] = res[1, :, first:]
    ocls[...] = small[:nc, :]
    ogain[...] = small[nc : nc + 1, :]
    ohead[...] = small[nc + 1 : nc + 2, :]
    oloss[...] = small[nc + 2 : nc + 3, : oloss.shape[1]]


def small_shape(classes, width):
    return (-(-(classes + 3) // 8) * 8, width)


def total_scratch(rows, width, classes, inner_count):
    half, cols = rows // 2, width // 2
    extra = small_shape(classes, width // 4)
    return [
        pltpu.VMEM((2, 2, half, cols), F32),
        pltpu.VMEM((2, 2, half, cols), F32),
        pltpu.VMEM((2, half, cols), BF16),
        pltpu.VMEM((2, half, cols), BF16),
        pltpu.VMEM((2, half, cols), F32),
        pltpu.VMEM((2, half // 2, cols), BF16),
        pltpu.VMEM((2, half // 2, cols), BF16),
        pltpu.VMEM((2, half // 2, cols), F32),
        pltpu.VMEM((2, inner_count - 1, half // 2 // inner_count, cols), F32),
        pltpu.VMEM((2, half // 2 // inner_count, cols), F32),
        pltpu.VMEM((2,) + extra, F32),
        pltpu.VMEM((6,) + extra, F32),
        pltpu.VMEM((6,) + extra, F32),
    ]


def local(fn, outs, scalars, *args):
    specs = vmem(len(args))
    for k in scalars:
        specs[k] = pl.BlockSpec(memory_space=pltpu.SMEM)
    return pl.pallas_call(
        fn,
        out_shape=[jax.ShapeDtypeStruct(s, t) for s, t in outs],
        in_specs=specs,
        out_specs=vmem(len(outs)),
        compiler_params=params(),
    )(*args)


def date_encoding(date_days, width):
    channel = jnp.arange(width)
    frequency = jnp.exp((channel // 2 * 2).astype(F32) * (-math.log(10000.0) / width))
    phases = date_days.astype(F32)[:, :, None] * frequency
    return jnp.where(channel % 2 == 0, jnp.sin(phases), jnp.cos(phases))


def saved_shapes(rows, width):
    hq = HEADS * CLASSES
    f, b = F32, BF16
    return [((rows, width), b), ((rows, width), f), ((rows, width), f), ((rows, width), b),
            ((hq, rows), f), ((hq, rows), f), ((rows, width), b), ((5, CLASSES, width), f)]


def kept_shapes(kinds, per, width):
    srows = kinds * per
    f, b = F32, BF16
    return [((srows, width), f), ((srows, width), b), ((2, srows, width), f), ((2, srows, width), f),
            ((srows, width), b), ((kinds, HEADS * per, per), f), ((srows, width), b), ((srows, width), f),
            ((srows, 128), f)]


def grad_shapes(width):
    return [((width, 4 * width), F32), ((1, width), F32)]


def everything(tiles, kinds, total_tiles, batch_norm,
               wq_own, wo_own, g_own, pix_ref, enc_ref, count_ref, slot_ref, label_ref, cls_ref, head_ref,
               res_ref, small_ref, w_ref, wo_ref, g_ref, *refs):
    refs = list(refs)

    def take(count):
        taken, refs[:count] = refs[:count], []
        return taken

    send_ref, recv_ref, back_ref, returned_ref, sums_ref, totals_ref = take(6)
    saved = take(8)
    kept = take(9)
    dw0, dg0, dw1, dg1, dcls, dhead, loss = take(7)
    parts = take(13)
    sems = take(2)
    inner = lax.axis_index("inner")
    count = recv_ref.shape[0]
    along = total_partners()
    enter(along[:3] + [{"inner": lax.rem(inner + k, count)} for k in range(1, count)])
    started, before_out = bring_weights(wq_own, wo_own, g_own, w_ref, wo_ref, g_ref, sems, 37)
    temporal_fwd(before_out, tiles, pix_ref, enc_ref, count_ref, cls_ref, g_ref, w_ref, wo_ref, send_ref, *saved)
    copies = swap(send_ref, recv_ref, sems, 42, False)
    for copy in copies:
        copy.wait_recv()
    started += copies
    spatial_fwd(kinds, tiles, recv_ref, g_ref, w_ref, wo_ref, head_ref, *kept, sums_ref)
    copies = swap(sums_ref, totals_ref, sems, 42 + count, True)
    for copy in copies:
        copy.wait_recv()
    started += copies
    copies = []
    spatial_bwd(lambda: copies.extend(swap(back_ref, returned_ref, sems, 42 + 2 * count, False)),
                kinds, tiles, total_tiles, batch_norm, totals_ref, label_ref, slot_ref,
                g_ref, w_ref, wo_ref, head_ref, *kept, back_ref, dw1, dg1, dhead, loss)
    early = first_hop(1, dw1, parts[0], sems)
    started += copies

    def arrive():
        for copy in copies:
            copy.wait_recv()

    temporal_bwd(arrive, tiles, returned_ref, pix_ref, enc_ref, cls_ref, g_ref, w_ref, wo_ref, *saved, dw0, dg0, dcls)
    total(early, dw0, dw1, dcls, dg0, dg1, dhead, loss, res_ref, small_ref, *parts, sems)
    for copy in started:
        copy.wait_send()


def shards(pixels, date_days, clear_count, batch_slot, labels, class_tokens, section_gain,
           segment_probe_lookup_content, section_out, head_vec):
    tiles_dev, patches_dev, dates, width = pixels.shape
    inner_count = lax.axis_size("inner")
    kinds = CLASSES // inner_count
    total_tiles = tiles_dev * lax.axis_size("dp")
    tiles = tiles_dev // 2
    rows = tiles * patches_dev * dates
    batch_norm = 1.0 / (total_tiles // MICRO * PATCHES)
    enc = date_encoding(date_days, width)
    head = head_vec.reshape(1, width)
    per = inner_count * tiles * patches_dev
    exchanged = ((inner_count, rows // inner_count, width), BF16)
    shapes = [
        ((2,) + segment_probe_lookup_content.shape[1:], BF16),
        ((2,) + section_out.shape[1:], BF16),
        ((2,) + section_gain.shape, F32),
        exchanged, exchanged, exchanged, exchanged,
        ((8, 128), F32), ((inner_count, 8, 128), F32),
    ]
    shapes += saved_shapes(rows, width) + kept_shapes(kinds, per, width) + grad_shapes(width) * 2
    shapes += [((CLASSES, width), F32), ((1, width), F32), ((1, width), F32)]
    specs = vmem(10)
    specs[5] = specs[6] = pl.BlockSpec(memory_space=pltpu.SMEM)
    sems = 42 + 3 * inner_count
    grads, small = pl.pallas_call(
        functools.partial(everything, tiles, kinds, total_tiles, batch_norm),
        out_shape=[
            jax.ShapeDtypeStruct((2, width, 2 * width), F32),
            jax.ShapeDtypeStruct(small_shape(CLASSES, width), F32),
        ],
        in_specs=specs,
        out_specs=vmem(2),
        scratch_shapes=[pltpu.VMEM(s, t) for s, t in shapes]
        + total_scratch(width, 4 * width, CLASSES, inner_count)
        + [pltpu.SemaphoreType.DMA((sems,))] * 2,
        compiler_params=params(collective_id=0, has_side_effects=True),
    )(segment_probe_lookup_content, section_out, section_gain, pixels, enc, clear_count, batch_slot,
      labels, class_tokens, head)
    gqkv, gout, gcls, ggain, ghead, gloss = local(
        finish,
        [((1, width, 3 * width), F32), ((1, width, width), F32), ((CLASSES, width), F32), ((1, width), F32),
         ((1, width), F32), ((1, MICRO), F32)], (),
        grads, small,
    )
    return gloss.reshape(MICRO), gcls, ggain, gqkv, gout, ghead.reshape(width)


def solution(mesh):
    placed = (
        P("dp", "inner", None, None),
        P("dp", None),
        P("dp"),
        P("dp"),
        P("dp", None),
        P(),
        P("pipe", None),
        P("pipe", None, None),
        P("pipe", None, None),
        P(),
    )

    def body(*args):
        tiles_dev, patches_dev, dates, width = args[0].shape
        pairs = tiles_dev // 2 * patches_dev
        sizes = tuple(mesh.shape[a] for a in ("pipe", "dp", "inner"))
        fits = sizes == (2, 4, 4) and pairs % 8 == 0 and dates == CLASSES and width == 256
        fits = fits and tiles_dev // 2 * PATCHES <= 128
        return (shards if fits else shards_general)(*args)

    return jax.shard_map(
        body,
        mesh=mesh,
        in_specs=placed,
        out_specs=(P(), P(), P("pipe", None), P("pipe", None, None), P("pipe", None, None), P()),
        check_vma=False,
    )
```
